128 devices in a mesh: dev: 128 (over x, y, z, core).
Axes of the slice: x: 4, y: 4, z: 4, core: 2. Of those that a mesh axis runs over, the one named last changes fastest.
Arguments:
- bottom: bfloat16 [3, 16384, 128], P(None, 'dev'), may hold values from -6 to 6
- labels: int32 [3, 16384], P(None, 'dev'), may hold values 0 or 1
- freq_ids: int32 [3, 16384, 26, 2], P(None, 'dev'), may hold values from 0 to 16383
- req_rows: int32 [3, 128, 128, 32], P(None, 'dev'), may hold values from 0 to 4096, as said below
- req_slot: int32 [3, 128, 128, 32], P(None, 'dev'), may hold values from 0 to 3328, as said below
- freq_table: bfloat16 [16384, 128], replicated, may hold values from -3 to 3
- inf_table: bfloat16 [524288, 128], P('dev'), may hold values from -3 to 3
- cross_u: bfloat16 [3456, 512], replicated, may hold values from -0.109375 to 0.109375
- cross_v: bfloat16 [512, 3456], replicated, may hold values from -0.25 to 0.25
- cross_bias: float32 [3456], replicated, may hold values from -3 to 3
- out_w: bfloat16 [3456], replicated, may hold values from -0.109375 to 0.109375
- out_b: float32 [], replicated, may hold values from -3 to 3
Outputs:
- grad_u: float32 [3456, 512], P('dev')
- grad_v: float32 [512, 3456], P(None, 'dev')
- grad_cross_bias: float32 [3456], P('dev')
- grad_out_w: float32 [3456], P('dev')
- grad_freq: bfloat16 [16384, 128], replicated
- grad_inf: bfloat16 [524288, 128], P('dev')
The draws below stay inside these ranges and needn't reach their ends.
Inputs may be any that keep to these rules, and one draw needn't show every extreme that they name: req_rows[m, d, o, c] is request c of device d to owner o in micro-batch m: a row number within o's 4096 rows, or 4096 for an empty request. In each list [m, d, o] the live requests come first and there is at least one; in every micro-batch some owner gets 32 live requests from every device. req_slot[m, d, o, c] = s * 26 + f names sample s of device d and feature f, or is 3328 where req_rows is 4096.
All inputs are finite; a program needn't handle non-finite values. No bound on the sum of `labels` on one device may be relied on, other than what follows from the above.
Results may differ from the reference program's by a relative error of at most 0.0062.
Values may be sent and summed in bfloat16 or wider, within the bound.
No kernel may reach another device: no remote copies, remote signals or barrier semaphores. Data moves between devices by JAX's collectives and lax.ppermute only.
A program may use at most 192 MiB of HBM per device.

```python
import math
import jax
import jax.numpy as jnp
import numpy as np
from jax import lax

E = 128
F = 26
RANK = 512
FREQ = 16384
FHOT = 2
MICRO = 3
S_DEV = 128
ROWS_DEV = 4096
XW = 3456
CAP = 32
SAMPLES = 16384
IROWS = 524288
N_DEV = 128


def request_plan(key):
    base_key = jax.random.fold_in(key, 4099)
    sub_keys = jax.random.split(base_key, 5)
    full_shape = (MICRO, N_DEV, N_DEV, CAP)
    hot_owner = jax.random.randint(sub_keys[0], (MICRO,), 0, N_DEV)
    load_level = jax.random.randint(sub_keys[1], (MICRO, N_DEV), CAP // 2, 3 * CAP // 4 + 1)
    low_count = jnp.maximum(load_level * 3 // 4, 1)
    jitter_bits = jax.random.randint(sub_keys[2], (MICRO, N_DEV, N_DEV), 0, 1 << 20)
    counts = low_count[:, None, :] + jitter_bits % (load_level - low_count + 1)[:, None, :]
    owner_idx = jnp.arange(N_DEV)[None, None, :]
    counts = jnp.where(owner_idx == hot_owner[:, None, None], CAP, counts)
    filled = jnp.arange(CAP)[None, None, None, :] < counts[..., None]
    row_pick = jax.random.randint(sub_keys[3], full_shape, 0, ROWS_DEV)
    slot_pick = jax.random.randint(sub_keys[4], full_shape, 0, S_DEV * F)
    return (jnp.where(filled, row_pick, ROWS_DEV).astype(jnp.int32), jnp.where(filled, slot_pick, S_DEV * F).astype(jnp.int32))


def draw_req_rows(key, part):
    return request_plan(key)[0]


def draw_req_slot(key, part):
    return request_plan(key)[1]


def set_ends(values, key, least, largest):
    longest = values.shape.index(max(values.shape))
    spots = []
    for shift in (0, 1):
        where = [jax.random.randint(jax.random.fold_in(key, axis), (), 0, length) for axis, length in enumerate(values.shape)]
        where[longest] = (where[longest] + shift) % values.shape[longest]
        spots.append(tuple(where))
    return values.at[spots[0]].set(least).at[spots[1]].set(largest)


def shard_levels(stream_key, extent, cuts, low, largest):
    level, own = 1.0, jax.random.fold_in(stream_key, 6)
    for axis_at, shards_of in cuts:
        draws = jnp.exp(jax.random.uniform(jax.random.fold_in(own, axis_at), (shards_of,), jnp.float32, low / len(cuts), largest / len(cuts)))
        level = level * jnp.repeat(draws, extent[axis_at] // shards_of).reshape([-1 if axis == axis_at else 1 for axis in range(len(extent))])
    return level


def rank_table(amount, lean):
    weights = [(1 << 20) // math.isqrt(grade ** lean) + 1 for grade in range(1, amount + 1)]
    deviation = 1 + sum(weights) // (1 << 30)
    return np.cumsum(np.array([max(1, weight // deviation) for weight in weights]))


def ranked_ids(own_key, dims, amount, lean):
    grid = rank_table(amount, lean)
    ticket = jax.random.randint(jax.random.fold_in(own_key, 1), dims, 0, int(grid[amount - 1]))
    rank = jnp.searchsorted(jnp.asarray(grid, jnp.int32), ticket, side="right")
    return jax.random.permutation(jax.random.fold_in(own_key, 2), amount)[rank].astype(jnp.int32)


def bell_draw(key, extent, width, reach, shards=(), held_as=jnp.bfloat16):
    result = jax.random.normal(key, extent, jnp.float32) * width
    if len(shards) > 0:
        result = shard_levels(key, extent, shards, -0.22, 0.18) * result
    return jnp.clip(result, min=-reach, max=reach).astype(held_as)


def setup_inputs(seed: int = 0) -> dict:
    arg_keys = jax.random.split(jax.random.key(seed), 13)
    bottom = bell_draw(arg_keys[0], (MICRO, SAMPLES, E), 1.0, 6.0, ((1, 128),))
    labels = set_ends((jax.random.randint(arg_keys[1], (MICRO, SAMPLES), 0, 4) < 1).astype(jnp.int32), jax.random.fold_in(arg_keys[1], 1), 0, 1)
    freq_ids = set_ends(ranked_ids(arg_keys[2], (MICRO, SAMPLES, F, FHOT), FREQ, 2), jax.random.fold_in(arg_keys[2], 3), 0, FREQ - 1).astype(jnp.int32)
    req_rows = draw_req_rows(jax.random.fold_in(arg_keys[12], 71), 0)
    req_slot = draw_req_slot(jax.random.fold_in(arg_keys[12], 71), 0)
    freq_table = bell_draw(arg_keys[5], (FREQ, E), 0.5, 3.0)
    inf_table = bell_draw(arg_keys[6], (IROWS, E), 0.5, 3.0, ((0, 128),))
    cross_u = bell_draw(arg_keys[7], (XW, RANK), XW ** -0.5, 0.109375)
    cross_v = bell_draw(arg_keys[8], (RANK, XW), RANK ** -0.5, 0.25)
    cross_bias = bell_draw(arg_keys[9], (XW,), 0.5, 3.0, (), jnp.float32)
    out_w = bell_draw(arg_keys[10], (XW,), XW ** -0.5, 0.109375)
    out_b = bell_draw(arg_keys[11], (), 1.0, 3.0, (), jnp.float32)
    return dict(bottom=bottom, labels=labels, freq_ids=freq_ids, req_rows=req_rows, req_slot=req_slot, freq_table=freq_table, inf_table=inf_table, cross_u=cross_u, cross_v=cross_v, cross_bias=cross_bias, out_w=out_w, out_b=out_b)


loss_scale = 1024.0

def reference(bottom, labels, freq_ids, req_rows, req_slot, freq_table, inf_table, cross_u, cross_v, cross_bias, out_w, out_b):
    loss_mult = loss_scale / math.sqrt(MICRO * SAMPLES)
    w_float = out_w.astype(jnp.float32)
    owner_base = (jnp.arange(N_DEV, dtype=jnp.int32) * ROWS_DEV)[:, None]

    def per_device(totals, inputs):
        grad_u, grad_v, grad_b, grad_w, grad_f = totals
        bottom_rows, label_rows, freq_rows, want_rows, want_slots = inputs
        is_live = (want_rows < ROWS_DEV) & (want_slots < S_DEV * F)
        row_ids = (owner_base + jnp.minimum(want_rows, ROWS_DEV - 1)).astype(jnp.int32)
        looked_up = inf_table[row_ids].astype(jnp.float32) * is_live[:, :, None].astype(jnp.float32)
        slot_idx = jnp.where(is_live, want_slots, 0).astype(jnp.int32).reshape(-1)
        inf_part = jnp.zeros((S_DEV * F, E), jnp.float32).at[slot_idx].add(looked_up.reshape(-1, E))
        freq_part = lax.optimization_barrier(jnp.sum(freq_table[freq_rows].astype(jnp.float32), axis=2)).reshape(S_DEV * F, E)
        pooled = (freq_part + inf_part).astype(jnp.bfloat16)
        x_zero = jnp.concatenate([bottom_rows, pooled.reshape(S_DEV, F * E)], axis=1)
        hidden = jnp.dot(x_zero, cross_u, preferred_element_type=jnp.float32).astype(jnp.bfloat16)
        gate_val = jnp.dot(hidden, cross_v, preferred_element_type=jnp.float32) + cross_bias
        x_float = x_zero.astype(jnp.float32)
        crossed = x_float * gate_val + x_float
        logits = lax.optimization_barrier(jnp.sum(crossed * w_float, axis=1)) + out_b
        d_logit = (jax.nn.sigmoid(logits) - label_rows.astype(jnp.float32)) * loss_mult
        d_crossed = d_logit[:, None] * w_float
        d_gate = d_crossed * x_float
        gate_low = d_gate.astype(jnp.bfloat16)
        d_hidden = jnp.dot(gate_low, cross_v.T, preferred_element_type=jnp.float32).astype(jnp.bfloat16)
        d_input = d_crossed * (gate_val + 1.0) + jnp.dot(d_hidden, cross_u.T, preferred_element_type=jnp.float32)
        d_pooled = d_input[:, E:].reshape(S_DEV, F, E)
        spread = jnp.broadcast_to(d_pooled[:, :, None, :], (S_DEV, F, FHOT, E)).reshape(-1, E)
        grad_f = grad_f.at[freq_rows.reshape(-1).astype(jnp.int32)].add(spread)
        pooled_low = d_pooled.reshape(S_DEV * F, E).astype(jnp.bfloat16)
        returned = pooled_low[slot_idx].reshape(N_DEV, CAP, E) * is_live[:, :, None].astype(jnp.bfloat16)
        grad_u = grad_u + jnp.dot(x_zero.T, d_hidden, preferred_element_type=jnp.float32)
        grad_v = grad_v + jnp.dot(hidden.T, gate_low, preferred_element_type=jnp.float32)
        grad_b = grad_b + lax.optimization_barrier(jnp.sum(d_gate, axis=0))
        grad_w = grad_w + lax.optimization_barrier(jnp.sum(d_logit[:, None] * crossed, axis=0))
        return ((grad_u, grad_v, grad_b, grad_w, grad_f), returned)
    totals = (jnp.zeros((XW, RANK), jnp.float32), jnp.zeros((RANK, XW), jnp.float32), jnp.zeros((XW,), jnp.float32), jnp.zeros((XW,), jnp.float32), jnp.zeros((FREQ, E), jnp.float32))
    grad_inf = jnp.zeros((IROWS, E), jnp.float32)
    all_base = (jnp.arange(N_DEV, dtype=jnp.int32) * ROWS_DEV)[None, :, None]
    for batch_idx in range(MICRO):
        inputs = (bottom[batch_idx].reshape(N_DEV, S_DEV, E), labels[batch_idx].reshape(N_DEV, S_DEV), freq_ids[batch_idx].reshape(N_DEV, S_DEV, F, FHOT), req_rows[batch_idx], req_slot[batch_idx])
        totals, returned = lax.scan(per_device, totals, inputs)
        row_all = (all_base + jnp.minimum(req_rows[batch_idx], ROWS_DEV - 1)).astype(jnp.int32)
        grad_inf = grad_inf.at[row_all.reshape(-1)].add(returned.astype(jnp.float32).reshape(-1, E))
    grad_u, grad_v, grad_b, grad_w, grad_f = totals
    return (grad_u, grad_v, grad_b, grad_w, grad_f.astype(jnp.bfloat16), grad_inf.astype(jnp.bfloat16))
```

```python
import functools
import math

import jax
import jax.numpy as jnp
from jax import lax
from jax.experimental import pallas as pl
from jax.experimental.pallas import tpu as pltpu
from jax.sharding import PartitionSpec as P

loss_scale = 1024.0
f32 = jnp.float32
bf16 = jnp.bfloat16
MIB = 1024 * 1024
SMEM = pl.BlockSpec(memory_space=pltpu.SMEM)
VMEM = pl.BlockSpec(memory_space=pltpu.VMEM)
NT = (((1,), (1,)), ((), ()))
TN = (((0,), (0,)), ((), ()))


def local_call(kernel, outs, in_specs, scratch, name, limit, flops, bytes_accessed):
    return pl.pallas_call(
        kernel,
        out_shape=[jax.ShapeDtypeStruct(s, d) for s, d in outs],
        in_specs=in_specs,
        out_specs=[VMEM] * len(outs),
        scratch_shapes=scratch,
        compiler_params=pltpu.CompilerParams(vmem_limit_bytes=limit * MIB),
        cost_estimate=pl.CostEstimate(
            flops=flops, bytes_accessed=bytes_accessed, transcendentals=0
        ),
        name=name,
    )


def freq_kernel(blocks, samples, ids, table_ref, out, table):
    table[...] = table_ref[...].astype(f32)
    unroll = 32

    def group(g, carry):
        def some(k, carry):
            for u in range(unroll):
                s = k * unroll + u
                first = ids[g * 2 * samples + s]
                second = ids[g * 2 * samples + samples + s]
                out[pl.ds(g * samples + s, 1), :] = (
                    table[pl.ds(first, 1), :] + table[pl.ds(second, 1), :]
                )
            return carry

        return lax.fori_loop(0, samples // unroll, some, carry)

    lax.fori_loop(0, blocks, group, 0)


def lookup_kernel(peers, stride, start, cap, asked, table_ref, out, table, rows):
    table[...] = table_ref[...].astype(f32)

    def peer(d, carry):
        for c in range(cap):
            r = asked[d * stride + start + c]
            rows[pl.ds(d * cap + c, 1), :] = table[pl.ds(r, 1), :]
        return carry

    lax.fori_loop(0, peers, peer, 0)
    out[...] = rows[...].astype(bf16)


def micro_kernel(
    peers,
    cap,
    features,
    slot_start,
    freq_start,
    loss_mult,
    slots,
    out_b,
    fetched,
    freq_part,
    bottom,
    labels,
    cross_u,
    cross_v,
    bias,
    weight,
    returned,
    d_pooled,
    x_zero,
    hidden_out,
    d_hidden_out,
    gate_low,
    grad_bw,
    arrived,
    acc0,
    acc1,
    acc2,
    acc3,
    gate,
):
    samples, width = x_zero.shape
    emb = bottom.shape[1]
    n_slots = features * samples
    accs = (acc0, acc1, acc2, acc3)
    arrived[...] = fetched[...].astype(f32)
    acc0[pl.ds(0, n_slots), :] = freq_part[pl.ds(freq_start, n_slots), :]
    for a in accs[1:]:
        a[...] = jnp.zeros_like(a)

    def add_peer(o, carry):
        for c in range(0, cap, 4):
            at = [slots[slot_start + (c + j) * peers + o] for j in range(4)]
            new = [
                accs[j][pl.ds(at[j], 1), :] + arrived[pl.ds(o * cap + c + j, 1), :]
                for j in range(4)
            ]
            for j in range(4):
                accs[j][pl.ds(at[j], 1), :] = new[j]
        return carry

    lax.fori_loop(0, peers, add_peer, 0)

    x_zero[:, 0:emb] = bottom[...]
    for f in range(features):
        rows = pl.ds(f * samples, samples)
        total = (acc0[rows, :] + acc1[rows, :]) + (acc2[rows, :] + acc3[rows, :])
        x_zero[:, (f + 1) * emb : (f + 2) * emb] = total.astype(bf16)

    hidden = jnp.dot(x_zero[...], cross_u[...], preferred_element_type=f32).astype(bf16)
    hidden_out[...] = hidden
    chunk = 3 * emb
    chunks = width // chunk
    partial = jnp.zeros((samples, emb), f32)
    for k in range(chunks):
        cols = slice(k * chunk, (k + 1) * chunk)
        value = jnp.dot(hidden, cross_v[:, cols], preferred_element_type=f32) + bias[:, cols]
        gate[:, cols] = value
        x_float = x_zero[:, cols].astype(f32)
        scored = (x_float * value + x_float) * weight[:, cols]
        for j in range(3):
            partial = partial + scored[:, j * emb : (j + 1) * emb]
    logits = jnp.sum(partial, axis=1, keepdims=True) + out_b[0]
    d_logit = (jax.nn.sigmoid(logits) - labels[...]) * loss_mult
    for k in range(chunks):
        cols = slice(k * chunk, (k + 1) * chunk)
        x_float = x_zero[:, cols].astype(f32)
        d_gate = (d_logit * weight[:, cols]) * x_float
        gate_low[:, cols] = d_gate.astype(bf16)
        crossed = x_float * gate[:, cols] + x_float
        grad_bw[0:1, cols] = jnp.sum(d_gate, axis=0, keepdims=True)
        grad_bw[1:2, cols] = jnp.sum(d_logit * crossed, axis=0, keepdims=True)
    d_hidden = lax.dot_general(
        gate_low[...], cross_v[...], NT, preferred_element_type=f32
    ).astype(bf16)
    d_hidden_out[...] = d_hidden
    for k in range(chunks):
        cols = slice(k * chunk, (k + 1) * chunk)
        back = lax.dot_general(d_hidden, cross_u[cols, :], NT, preferred_element_type=f32)
        d_input = (d_logit * weight[:, cols]) * (gate[:, cols] + 1.0) + back
        for j in range(3):
            f = 3 * k + j - 1
            if f >= 0:
                block = d_input[:, j * emb : (j + 1) * emb]
                d_pooled[f * samples : (f + 1) * samples, :] = block
                acc0[f * samples : (f + 1) * samples, :] = block
    acc0[n_slots:, :] = jnp.zeros((acc0.shape[0] - n_slots, emb), f32)

    def take_peer(o, carry):
        for c in range(cap):
            at = slots[slot_start + c * peers + o]
            arrived[pl.ds(o * cap + c, 1), :] = acc0[pl.ds(at, 1), :]
        return carry

    lax.fori_loop(0, peers, take_peer, 0)
    returned[...] = arrived[...].astype(bf16)


def dense_grad_kernel(peers, per, core, x0, x1, x2, g0, g1, g2, h0, h1, h2, e0, e1, e2, keep, send, total):
    width = x0.shape[1]
    rank = h0.shape[1]
    chunk = 128
    h_all = jnp.concatenate([h0[...], h1[...], h2[...]], axis=0)
    e_all = jnp.concatenate([e0[...], e1[...], e2[...]], axis=0)
    for k in range(width // chunk):
        cols = slice(k * chunk, (k + 1) * chunk)
        x_all = jnp.concatenate([x0[:, cols], x1[:, cols], x2[:, cols]], axis=0)
        g_all = jnp.concatenate([g0[:, cols], g1[:, cols], g2[:, cols]], axis=0)
        total[cols, 0:rank] = lax.dot_general(x_all, e_all, TN, preferred_element_type=f32)
        total[cols, rank : 2 * rank] = lax.dot_general(
            g_all, h_all, TN, preferred_element_type=f32
        )
    total[width:, :] = jnp.zeros((total.shape[0] - width, 2 * rank), f32)
    rows = keep.shape[1]
    even = core[0] == 0

    def pairs(q, carry):
        base = q * 8 * per

        def block(i):
            skip = i * per % 8
            window = total[pl.ds(pl.multiple_of(base + (i * per - skip), 8), rows + 8), :]
            return window[skip : skip + rows]

        for i in range(4):
            first = block(2 * i)
            second = block(2 * i + 1)
            keep[q * 4 + i] = jnp.where(even, first, second).astype(bf16)
            send[q * 4 + i] = jnp.where(even, second, first).astype(bf16)
        return carry

    lax.fori_loop(0, peers // 8, pairs, 0)


def freq_grad_kernel(features, core, ids, d0, d1, d2, keep, send, acc0, acc1, acc2, acc3):
    accs = (acc0, acc1, acc2, acc3)
    samples = d0.shape[0] // features
    for a in accs:
        a[...] = jnp.zeros_like(a)
    unroll = 32
    for m, source in enumerate((d0, d1, d2)):
        start = m * features * 2 * samples

        def feature(f, carry):
            def some(k, carry):
                for u in range(0, unroll, 2):
                    s = k * unroll + u
                    at = [
                        ids[start + (2 * f + h) * samples + s + j]
                        for j in range(2)
                        for h in range(2)
                    ]
                    value = [source[pl.ds(f * samples + s + j, 1), :] for j in range(2)]
                    new = [accs[j][pl.ds(at[j], 1), :] + value[j // 2] for j in range(4)]
                    for j in range(4):
                        accs[j][pl.ds(at[j], 1), :] = new[j]
                return carry

            return lax.fori_loop(0, samples // unroll, some, carry)

        lax.fori_loop(0, features, feature, 0)
    rows = 128
    mine = core[0]

    def block(q, carry):
        for ref, parity in ((keep, mine), (send, 1 - mine)):
            at = pl.ds(pl.multiple_of((2 * q + parity) * rows, rows), rows)
            total = (acc0[at, :] + acc1[at, :]) + (acc2[at, :] + acc3[at, :])
            ref[q] = total.astype(bf16)
        return carry

    lax.fori_loop(0, keep.shape[0], block, 0)


def owner_kernel(peers, stride, cap, asked, r0, r1, r2, out, rows, acc0, acc1, acc2, acc3):
    accs = (acc0, acc1, acc2, acc3)
    for a in accs:
        a[...] = jnp.zeros_like(a)
    for m, source in enumerate((r0, r1, r2)):
        rows[...] = source[...].astype(f32)

        def peer(d, carry):
            for c in range(0, cap, 4):
                at = [asked[d * stride + m * cap + c + j] for j in range(4)]
                new = [
                    accs[j][pl.ds(at[j], 1), :] + rows[pl.ds(d * cap + c + j, 1), :]
                    for j in range(4)
                ]
                for j in range(4):
                    accs[j][pl.ds(at[j], 1), :] = new[j]
            return carry

        lax.fori_loop(0, peers, peer, 0)
    at = slice(0, out.shape[0])
    out[...] = ((acc0[at, :] + acc1[at, :]) + (acc2[at, :] + acc3[at, :])).astype(bf16)


def on_device(
    bottom,
    labels,
    freq_ids,
    req_rows,
    req_slot,
    freq_table,
    inf_table,
    cross_u,
    cross_v,
    cross_bias,
    out_w,
    out_b,
):
    devices = lax.axis_size("dev")
    micro, samples, emb = bottom.shape
    features = freq_ids.shape[2]
    hot = freq_ids.shape[3]
    owned = inf_table.shape[0]
    cap = req_rows.shape[3]
    width, rank = cross_u.shape
    freq_rows = freq_table.shape[0]
    n_slots = samples * features
    n_req = devices * cap
    per = width // devices
    loss_mult = loss_scale / math.sqrt(micro * samples * devices)
    me = lax.axis_index("dev")
    core = (me % 2).astype(jnp.int32).reshape(1)
    other_core = [(d, d ^ 1) for d in range(devices)]
    same_core = [list(range(c, devices, 2)) for c in range(2)]

    ids = jnp.transpose(freq_ids, (0, 2, 3, 1)).reshape(-1)
    rows_mc = jnp.transpose(req_rows[:, 0], (0, 2, 1))
    slot_mc = jnp.transpose(req_slot[:, 0], (0, 2, 1))
    is_live = (rows_mc < owned) & (slot_mc < n_slots)
    place = jnp.where(
        is_live, (slot_mc % features) * samples + slot_mc // features, n_slots
    ).reshape(-1)
    line = jnp.where(
        (req_rows < owned) & (req_slot < n_slots), req_rows, owned
    )[:, 0]
    line = jnp.transpose(line, (1, 0, 2)).reshape(devices, micro * cap)
    stride = -(-micro * cap // 128) * 128
    line = jnp.pad(line, ((0, 0), (0, stride - micro * cap)), constant_values=owned)
    asked = lax.all_to_all(line, "dev", split_axis=0, concat_axis=0, tiled=True).reshape(-1)
    asked_row = jnp.minimum(asked, owned - 1)

    (freq_part,) = local_call(
        functools.partial(freq_kernel, micro * features, samples),
        [((micro * n_slots, emb), f32)],
        [SMEM, VMEM],
        [pltpu.VMEM((freq_rows, emb), f32)],
        "freq_rows",
        40,
        0,
        50 * MIB,
    )(ids, freq_table)

    weight = out_w.astype(f32).reshape(1, width)
    bias = cross_bias.reshape(1, width)
    label_cols = labels.astype(f32).reshape(micro, samples, 1)
    bias_b = out_b.reshape(1)
    outs = []
    arrived = []
    for m in range(micro):
        (looked,) = local_call(
            functools.partial(lookup_kernel, devices, stride, m * cap, cap),
            [((n_req, emb), bf16)],
            [SMEM, VMEM],
            [pltpu.VMEM((owned, emb), f32), pltpu.VMEM((n_req, emb), f32)],
            f"lookup{m}",
            24,
            0,
            20 * MIB,
        )(asked_row, inf_table)
        fetched = lax.all_to_all(
            looked.reshape(devices, cap, emb), "dev", split_axis=0, concat_axis=0, tiled=True
        ).reshape(n_req, emb)
        out = local_call(
            functools.partial(
                micro_kernel,
                devices,
                cap,
                features,
                m * n_req,
                m * n_slots,
                loss_mult,
            ),
            [
                ((n_req, emb), bf16),
                ((n_slots, emb), f32),
                ((samples, width), bf16),
                ((samples, rank), bf16),
                ((samples, rank), bf16),
                ((samples, width), bf16),
                ((2, width), f32),
            ],
            [SMEM, SMEM] + [VMEM] * 8,
            [pltpu.VMEM((n_req, emb), f32)]
            + [pltpu.VMEM((n_slots + 8, emb), f32)] * 4
            + [pltpu.VMEM((samples, width), f32)],
            f"micro{m}",
            48,
            6 * samples * width * rank,
            60 * MIB,
        )(
            place,
            bias_b,
            fetched,
            freq_part,
            bottom[m],
            label_cols[m],
            cross_u,
            cross_v,
            bias,
            weight,
        )
        outs.append(out)
        arrived.append(
            lax.all_to_all(
                out[0].reshape(devices, cap, emb), "dev", split_axis=0, concat_axis=0, tiled=True
            ).reshape(n_req, emb)
        )
    d_pooled = [o[1] for o in outs]
    grad_bw = lax.psum((outs[0][6] + outs[1][6]) + outs[2][6], "dev")

    rows_pad = -(-per // 16) * 16
    keep, send = local_call(
        functools.partial(dense_grad_kernel, devices, per),
        [((devices // 2, rows_pad, 2 * rank), bf16)] * 2,
        [SMEM] + [VMEM] * 12,
        [pltpu.VMEM((width + 16, 2 * rank), f32)],
        "dense_grads",
        48,
        12 * samples * width * rank,
        40 * MIB,
    )(
        core,
        *[o[2] for o in outs],
        *[o[5] for o in outs],
        *[o[3] for o in outs],
        *[o[4] for o in outs],
    )
    got = lax.ppermute(send, "dev", other_core)
    both = (keep.astype(f32) + got.astype(f32)).astype(bf16)
    parts = lax.all_to_all(
        both, "dev", split_axis=0, concat_axis=0, axis_index_groups=same_core, tiled=True
    )
    dense = jnp.sum(parts.astype(f32), axis=0)[:per]
    grad_u = dense[:, :rank]
    grad_v = dense[:, rank:].T

    per_freq = freq_rows // devices
    keep, send = local_call(
        functools.partial(freq_grad_kernel, features),
        [((devices // 2, per_freq, emb), bf16)] * 2,
        [SMEM, SMEM] + [VMEM] * 3,
        [pltpu.VMEM((freq_rows, emb), f32)] * 4,
        "freq_grads",
        56,
        0,
        120 * MIB,
    )(core, ids, *d_pooled)
    got = lax.ppermute(send, "dev", other_core)
    both = (keep.astype(f32) + got.astype(f32)).astype(bf16)
    parts = lax.all_to_all(
        both, "dev", split_axis=0, concat_axis=0, axis_index_groups=same_core, tiled=True
    )
    mine = jnp.sum(parts.astype(f32), axis=0).astype(bf16)
    grad_freq = lax.all_gather(mine, "dev", tiled=True)

    (grad_inf,) = local_call(
        functools.partial(owner_kernel, devices, stride, cap),
        [((owned, emb), bf16)],
        [SMEM] + [VMEM] * 3,
        [pltpu.VMEM((n_req, emb), f32)] + [pltpu.VMEM((owned + 8, emb), f32)] * 4,
        "owner_grads",
        32,
        0,
        60 * MIB,
    )(asked, *arrived)

    grad_b = lax.dynamic_slice_in_dim(grad_bw[0], me * per, per)
    grad_w = lax.dynamic_slice_in_dim(grad_bw[1], me * per, per)
    return (grad_u, grad_v, grad_b, grad_w, grad_freq, grad_inf)


def solution(mesh):
    in_specs = (
        P(None, "dev", None),
        P(None, "dev"),
        P(None, "dev", None, None),
        P(None, "dev", None, None),
        P(None, "dev", None, None),
        P(),
        P("dev", None),
        P(),
        P(),
        P(),
        P(),
        P(),
    )
    out_specs = (P("dev", None), P(None, "dev"), P("dev"), P("dev"), P(), P("dev", None))
    return jax.shard_map(
        on_device, mesh=mesh, in_specs=in_specs, out_specs=out_specs, check_vma=False
    )
```

```python
import functools
import math

import jax
import jax.numpy as jnp
from jax import lax
from jax.experimental import pallas as pl
from jax.experimental.pallas import tpu as pltpu
from jax.sharding import PartitionSpec as P

loss_scale = 1024.0
f32 = jnp.float32
bf16 = jnp.bfloat16
MIB = 1024 * 1024
SMEM = pl.BlockSpec(memory_space=pltpu.SMEM)
VMEM = pl.BlockSpec(memory_space=pltpu.VMEM)
HBM = pl.BlockSpec(memory_space=pltpu.HBM)
NT = (((1,), (1,)), ((), ()))
TN = (((0,), (0,)), ((), ()))


def local_call(
    kernel, outs, in_specs, scratch, name, limit, flops, bytes_accessed, out_specs=None, aliases={}
):
    return pl.pallas_call(
        kernel,
        out_shape=[jax.ShapeDtypeStruct(s, d) for s, d in outs],
        in_specs=in_specs,
        out_specs=out_specs or [VMEM] * len(outs),
        scratch_shapes=scratch,
        compiler_params=pltpu.CompilerParams(vmem_limit_bytes=limit * MIB),
        cost_estimate=pl.CostEstimate(
            flops=flops, bytes_accessed=bytes_accessed, transcendentals=0
        ),
        input_output_aliases=aliases,
        name=name,
    )


def freq_kernel(blocks, samples, ids, table_ref, *refs):
    *outs, table = refs
    table[...] = table_ref[...].astype(f32)
    unroll = 32
    for m, out in enumerate(outs):
        start = m * blocks * 2 * samples

        def group(g, carry):
            def some(k, carry):
                for u in range(unroll):
                    s = k * unroll + u
                    first = ids[start + g * 2 * samples + s]
                    second = ids[start + g * 2 * samples + samples + s]
                    out[pl.ds(g * samples + s, 1), :] = (
                        table[pl.ds(first, 1), :] + table[pl.ds(second, 1), :]
                    )
                return carry

            return lax.fori_loop(0, samples // unroll, some, carry)

        lax.fori_loop(0, blocks, group, 0)


def lookup_kernel(peers, stride, start, cap, asked, table_ref, out, table, rows):
    table[...] = table_ref[...].astype(f32)

    def peer(d, carry):
        for c in range(cap):
            r = asked[d * stride + start + c]
            rows[pl.ds(d * cap + c, 1), :] = table[pl.ds(r, 1), :]
        return carry

    lax.fori_loop(0, peers, peer, 0)
    out[...] = rows[...].astype(bf16)


def micro_kernel(
    peers,
    cap,
    features,
    slot_start,
    ret_start,
    loss_mult,
    slots,
    out_b,
    fetched,
    freq_part,
    bottom,
    labels,
    cross_u,
    cross_v,
    bias,
    weight,
    *refs,
):
    (
        returned_hbm,
        d_pooled_hbm,
        x_zero_hbm,
        hidden_hbm,
        d_hidden_hbm,
        gate_low_hbm,
        grad_bw,
        arrived,
        acc0,
        acc1,
        acc2,
        acc3,
        gate,
        returned,
        x_zero,
        hidden_out,
        d_hidden_out,
        gate_low,
        sems,
    ) = refs[-19:]
    samples, width = x_zero.shape
    emb = bottom.shape[1]
    n_slots = features * samples
    accs = (acc0, acc1, acc2, acc3)
    arrived[...] = fetched[...].astype(f32)
    acc0[pl.ds(0, n_slots), :] = freq_part[...]
    for a in accs[1:]:
        a[...] = jnp.zeros_like(a)

    def add_peer(o, carry):
        for c in range(0, cap, 4):
            at = [slots[slot_start + (c + j) * peers + o] for j in range(4)]
            new = [
                accs[j][pl.ds(at[j], 1), :] + arrived[pl.ds(o * cap + c + j, 1), :]
                for j in range(4)
            ]
            for j in range(4):
                accs[j][pl.ds(at[j], 1), :] = new[j]
        return carry

    lax.fori_loop(0, peers, add_peer, 0)

    x_zero[:, 0:emb] = bottom[...]
    for f in range(features):
        rows = pl.ds(f * samples, samples)
        total = (acc0[rows, :] + acc1[rows, :]) + (acc2[rows, :] + acc3[rows, :])
        x_zero[:, (f + 1) * emb : (f + 2) * emb] = total.astype(bf16)

    hidden = jnp.dot(x_zero[...], cross_u[...], preferred_element_type=f32).astype(bf16)
    hidden_out[...] = hidden
    copies = [
        pltpu.make_async_copy(x_zero, x_zero_hbm, sems.at[0]),
        pltpu.make_async_copy(hidden_out, hidden_hbm, sems.at[1]),
    ]
    for copy in copies:
        copy.start()
    chunk = 3 * emb
    chunks = width // chunk
    partial = jnp.zeros((samples, emb), f32)
    for k in range(chunks):
        cols = slice(k * chunk, (k + 1) * chunk)
        value = jnp.dot(hidden, cross_v[:, cols], preferred_element_type=f32) + bias[:, cols]
        gate[:, cols] = value
        x_float = x_zero[:, cols].astype(f32)
        scored = (x_float * value + x_float) * weight[:, cols]
        for j in range(3):
            partial = partial + scored[:, j * emb : (j + 1) * emb]
    logits = jnp.sum(partial, axis=1, keepdims=True) + out_b[0]
    d_logit = (jax.nn.sigmoid(logits) - labels[...]) * loss_mult
    for k in range(chunks):
        cols = slice(k * chunk, (k + 1) * chunk)
        x_float = x_zero[:, cols].astype(f32)
        d_gate = (d_logit * weight[:, cols]) * x_float
        gate_low[:, cols] = d_gate.astype(bf16)
        crossed = x_float * gate[:, cols] + x_float
        grad_bw[0:1, cols] = jnp.sum(d_gate, axis=0, keepdims=True)
        grad_bw[1:2, cols] = jnp.sum(d_logit * crossed, axis=0, keepdims=True)
    d_hidden = lax.dot_general(
        gate_low[...], cross_v[...], NT, preferred_element_type=f32
    ).astype(bf16)
    d_hidden_out[...] = d_hidden
    later = [
        pltpu.make_async_copy(gate_low, gate_low_hbm, sems.at[2]),
        pltpu.make_async_copy(d_hidden_out, d_hidden_hbm, sems.at[3]),
    ]
    for copy in later:
        copy.start()
    for k in range(chunks):
        cols = slice(k * chunk, (k + 1) * chunk)
        back = lax.dot_general(d_hidden, cross_u[cols, :], NT, preferred_element_type=f32)
        d_input = (d_logit * weight[:, cols]) * (gate[:, cols] + 1.0) + back
        for j in range(3):
            f = 3 * k + j - 1
            if f >= 0:
                acc0[f * samples : (f + 1) * samples, :] = d_input[:, j * emb : (j + 1) * emb]
    acc0[n_slots:, :] = jnp.zeros((acc0.shape[0] - n_slots, emb), f32)
    pooled_copy = pltpu.make_async_copy(acc0.at[pl.ds(0, n_slots), :], d_pooled_hbm, sems.at[4])
    pooled_copy.start()

    def take_peer(o, carry):
        for c in range(cap):
            at = slots[slot_start + c * peers + o]
            arrived[pl.ds(o * cap + c, 1), :] = acc0[pl.ds(at, 1), :]
        return carry

    lax.fori_loop(0, peers, take_peer, 0)
    returned[...] = arrived[...].astype(bf16).reshape(peers, cap, emb)
    returned_copy = pltpu.make_async_copy(
        returned, returned_hbm.at[:, pl.ds(ret_start, cap), :], sems.at[5]
    )
    returned_copy.start()
    for copy in copies + later:
        copy.wait()
    pooled_copy.wait()
    returned_copy.wait()


def dense_grad_kernel(
    peers, per, core, columns, x0, x1, x2, g0, g1, g2, h0, h1, h2, e0, e1, e2, keep, send, total
):
    width = x0.shape[1]
    rank = h0.shape[1]
    chunk = 128
    h_all = jnp.concatenate([h0[...], h1[...], h2[...]], axis=0)
    e_all = jnp.concatenate([e0[...], e1[...], e2[...]], axis=0)
    for k in range(width // chunk):
        cols = slice(k * chunk, (k + 1) * chunk)
        x_all = jnp.concatenate([x0[:, cols], x1[:, cols], x2[:, cols]], axis=0)
        g_all = jnp.concatenate([g0[:, cols], g1[:, cols], g2[:, cols]], axis=0)
        total[cols, 0:rank] = lax.dot_general(x_all, e_all, TN, preferred_element_type=f32)
        total[cols, rank : 2 * rank] = lax.dot_general(
            g_all, h_all, TN, preferred_element_type=f32
        )
    total[width:, :] = jnp.zeros((total.shape[0] - width, 2 * rank), f32)
    rows = keep.shape[1]
    even = core[0] == 0

    def pairs(q, carry):
        base = q * 8 * per

        def block(i):
            skip = i * per % 8
            window = total[pl.ds(pl.multiple_of(base + (i * per - skip), 8), rows + 8), :]
            return window[skip : skip + rows]

        spare = lax.broadcasted_iota(jnp.int32, (16, 128), 0) >= per - 16
        for i in range(4):
            first = block(2 * i)
            second = block(2 * i + 1)
            at = q * 4 + i
            for ref, value, row in (
                (keep, jnp.where(even, first, second), 2 * at + core[0]),
                (send, jnp.where(even, second, first), 2 * at + 1 - core[0]),
            ):
                ref[at, 0:16, :] = value[0:16].astype(bf16)
                ref[at, 16:32, 128:] = value[16:32, 128:].astype(bf16)
                ref[at, 16:32, 0:128] = jnp.where(
                    spare, columns[row], value[16:32, 0:128]
                ).astype(bf16)
        return carry

    lax.fori_loop(0, peers // 8, pairs, 0)


def freq_grad_kernel(features, core, ids, d0, d1, d2, keep, send, acc0, acc1, acc2, acc3):
    accs = (acc0, acc1, acc2, acc3)
    samples = d0.shape[0] // features
    for a in accs:
        a[...] = jnp.zeros_like(a)
    unroll = 32
    for m, source in enumerate((d0, d1, d2)):
        start = m * features * 2 * samples

        def feature(f, carry):
            def some(k, carry):
                for u in range(0, unroll, 2):
                    s = k * unroll + u
                    at = [
                        ids[start + (2 * f + h) * samples + s + j]
                        for j in range(2)
                        for h in range(2)
                    ]
                    value = [source[pl.ds(f * samples + s + j, 1), :] for j in range(2)]
                    new = [accs[j][pl.ds(at[j], 1), :] + value[j // 2] for j in range(4)]
                    for j in range(4):
                        accs[j][pl.ds(at[j], 1), :] = new[j]
                return carry

            return lax.fori_loop(0, samples // unroll, some, carry)

        lax.fori_loop(0, features, feature, 0)
    rows = 128
    mine = core[0]

    def block(q, carry):
        for ref, parity in ((keep, mine), (send, 1 - mine)):
            at = pl.ds(pl.multiple_of((2 * q + parity) * rows, rows), rows)
            total = (acc0[at, :] + acc1[at, :]) + (acc2[at, :] + acc3[at, :])
            ref[q] = total.astype(bf16)
        return carry

    lax.fori_loop(0, keep.shape[0], block, 0)


def owner_kernel(peers, stride, cap, asked, alone, pair, out, rows, acc0, acc1, acc2, acc3):
    accs = (acc0, acc1, acc2, acc3)
    for a in accs:
        a[...] = jnp.zeros_like(a)
    emb = out.shape[1]
    for m in range(3):
        if m == 0:
            rows[...] = alone[...].astype(f32)
        else:
            part = pair[:, (m - 1) * cap : m * cap, :]
            rows[...] = part.astype(f32).reshape(peers * cap, emb)

        def peer(d, carry):
            for c in range(0, cap, 4):
                at = [asked[d * stride + m * cap + c + j] for j in range(4)]
                new = [
                    accs[j][pl.ds(at[j], 1), :] + rows[pl.ds(d * cap + c + j, 1), :]
                    for j in range(4)
                ]
                for j in range(4):
                    accs[j][pl.ds(at[j], 1), :] = new[j]
            return carry

        lax.fori_loop(0, peers, peer, 0)
    at = slice(0, out.shape[0])
    out[...] = ((acc0[at, :] + acc1[at, :]) + (acc2[at, :] + acc3[at, :])).astype(bf16)


def on_device(
    bottom,
    labels,
    freq_ids,
    req_rows,
    req_slot,
    freq_table,
    inf_table,
    cross_u,
    cross_v,
    cross_bias,
    out_w,
    out_b,
):
    devices = lax.axis_size("dev")
    micro, samples, emb = bottom.shape
    features = freq_ids.shape[2]
    hot = freq_ids.shape[3]
    owned = inf_table.shape[0]
    cap = req_rows.shape[3]
    width, rank = cross_u.shape
    freq_rows = freq_table.shape[0]
    n_slots = samples * features
    n_req = devices * cap
    per = width // devices
    loss_mult = loss_scale / math.sqrt(micro * samples * devices)
    me = lax.axis_index("dev")
    core = (me % 2).astype(jnp.int32).reshape(1)
    other_core = [(d, d ^ 1) for d in range(devices)]
    same_core = [list(range(c, devices, 2)) for c in range(2)]

    ids = jnp.transpose(freq_ids, (0, 2, 3, 1)).reshape(-1)
    rows_mc = jnp.transpose(req_rows[:, 0], (0, 2, 1))
    slot_mc = jnp.transpose(req_slot[:, 0], (0, 2, 1))
    is_live = (rows_mc < owned) & (slot_mc < n_slots)
    place = jnp.where(
        is_live, (slot_mc % features) * samples + slot_mc // features, n_slots
    ).reshape(-1)
    line = jnp.where(
        (req_rows < owned) & (req_slot < n_slots), req_rows, owned
    )[:, 0]
    line = jnp.transpose(line, (1, 0, 2)).reshape(devices, micro * cap)
    stride = -(-micro * cap // 128) * 128
    line = jnp.pad(line, ((0, 0), (0, stride - micro * cap)), constant_values=owned)
    asked = lax.all_to_all(line, "dev", split_axis=0, concat_axis=0, tiled=True).reshape(-1)

    freq_part = local_call(
        functools.partial(freq_kernel, features, samples),
        [((n_slots, emb), f32)] * micro,
        [SMEM, VMEM],
        [pltpu.VMEM((freq_rows, emb), f32)],
        "freq_rows",
        62,
        0,
        50 * MIB,
    )(ids, freq_table)

    asked, freq_part = lax.optimization_barrier((asked, freq_part))
    asked_row = jnp.minimum(asked, owned - 1)
    weight = out_w.astype(f32).reshape(1, width)
    bias = cross_bias.reshape(1, width)
    label_cols = labels.astype(f32).reshape(micro, samples, 1)
    bias_b = out_b.reshape(1)

    def exchange(rows, count):
        return lax.all_to_all(
            rows.reshape(devices, count, emb), "dev", split_axis=0, concat_axis=0, tiled=True
        ).reshape(n_req * count // cap, emb)

    outs = []
    arrived = []
    looked_all = []
    for m in range(micro):
        (looked,) = local_call(
            functools.partial(lookup_kernel, devices, stride, m * cap, cap),
            [((n_req, emb), bf16)],
            [SMEM, VMEM],
            [pltpu.VMEM((owned, emb), f32), pltpu.VMEM((n_req, emb), f32)],
            f"lookup{m}",
            24,
            0,
            20 * MIB,
        )(asked_row, inf_table)
        asked_row, looked = lax.optimization_barrier((asked_row, looked))
        looked_all.append(looked)
    looked_all[1], looked_all[2] = lax.optimization_barrier((looked_all[1], looked_all[2]))
    fetched = exchange(looked_all[0], cap)
    later = exchange(looked_all[1], cap)
    pair = None
    for m in range(micro):
        if m > 0:
            fetched = later
        if m == 1:
            looked_all[2], outs[0][6] = lax.optimization_barrier((looked_all[2], outs[0][6]))
            later = exchange(looked_all[2], cap)
            fetched, outs[0][6] = lax.optimization_barrier((fetched, outs[0][6]))
        if m == 2:
            fetched, outs[1][6] = lax.optimization_barrier((fetched, outs[1][6]))
            back, outs[1][6] = lax.optimization_barrier((outs[0][0], outs[1][6]))
            arrived.append(exchange(back, cap))
        out = local_call(
            functools.partial(
                micro_kernel,
                devices,
                cap,
                features,
                m * n_req,
                cap if m == 2 else 0,
                loss_mult,
            ),
            [
                ((devices, cap if m == 0 else 2 * cap, emb), bf16),
                ((n_slots, emb), f32),
                ((samples, width), bf16),
                ((samples, rank), bf16),
                ((samples, rank), bf16),
                ((samples, width), bf16),
                ((2, width), f32),
            ],
            [SMEM, SMEM] + [VMEM] * 8 + ([HBM] if m == 2 else []),
            [pltpu.VMEM((n_req, emb), f32)]
            + [pltpu.VMEM((n_slots + 8, emb), f32)] * 4
            + [pltpu.VMEM((samples, width), f32)]
            + [pltpu.VMEM((devices, cap, emb), bf16), pltpu.VMEM((samples, width), bf16)]
            + [pltpu.VMEM((samples, rank), bf16)] * 2
            + [pltpu.VMEM((samples, width), bf16), pltpu.SemaphoreType.DMA((6,))],
            f"micro{m}",
            62,
            6 * samples * width * rank,
            60 * MIB,
            [HBM] * 6 + [VMEM],
            {10: 0} if m == 2 else {},
        )(
            place,
            bias_b,
            fetched,
            freq_part[m],
            bottom[m],
            label_cols[m],
            cross_u,
            cross_v,
            bias,
            weight,
            *([outs[1][0]] if m == 2 else []),
        )
        outs.append(list(out))
    arrived.append(exchange(outs[2][0], 2 * cap))
    d_pooled = [o[1] for o in outs]
    grad_bw = ((outs[0][6] + outs[1][6]) + outs[2][6]).reshape(2, devices, per)
    columns = jnp.pad(
        jnp.transpose(grad_bw, (1, 0, 2)), ((0, 0), (per - 16, 30 - per), (0, 128 - per))
    )

    rows_pad = -(-per // 16) * 16
    per_freq = freq_rows // devices
    d_pooled, arrived[0] = lax.optimization_barrier((d_pooled, arrived[0]))
    keep_f, send_f = local_call(
        functools.partial(freq_grad_kernel, features),
        [((devices // 2, per_freq, emb), bf16)] * 2,
        [SMEM, SMEM] + [VMEM] * 3,
        [pltpu.VMEM((freq_rows, emb), f32)] * 4,
        "freq_grads",
        62,
        0,
        120 * MIB,
    )(core, ids, *d_pooled)
    send_f, arrived[1] = lax.optimization_barrier((send_f, arrived[1]))
    got = lax.ppermute(send_f, "dev", other_core)
    both_f = (keep_f.astype(f32) + got.astype(f32)).astype(bf16)
    core_d, columns, both_f = lax.optimization_barrier((core, columns, both_f))
    parts_f = lax.all_to_all(
        both_f, "dev", split_axis=0, concat_axis=0, axis_index_groups=same_core, tiled=True
    )
    keep, send = local_call(
        functools.partial(dense_grad_kernel, devices, per),
        [((devices // 2, rows_pad, 2 * rank), bf16)] * 2,
        [SMEM] + [VMEM] * 13,
        [pltpu.VMEM((width + 16, 2 * rank), f32)],
        "dense_grads",
        62,
        12 * samples * width * rank,
        40 * MIB,
    )(
        core_d,
        columns,
        *[o[2] for o in outs],
        *[o[5] for o in outs],
        *[o[3] for o in outs],
        *[o[4] for o in outs],
    )
    got = lax.ppermute(send, "dev", other_core)
    both = (keep.astype(f32) + got.astype(f32)).astype(bf16)
    both, parts_f = lax.optimization_barrier((both, parts_f))
    parts = lax.all_to_all(
        both, "dev", split_axis=0, concat_axis=0, axis_index_groups=same_core, tiled=True
    )
    dense = jnp.sum(parts.astype(f32), axis=0)
    grad_u = dense[:per, :rank]
    grad_v = dense[:per, rank:].T
    grad_b = dense[per, :per]
    grad_w = dense[per + 1, :per]

    mine = jnp.sum(parts_f.astype(f32), axis=0).astype(bf16)
    grad_freq = lax.all_gather(mine, "dev", tiled=True)

    (grad_inf,) = local_call(
        functools.partial(owner_kernel, devices, stride, cap),
        [((owned, emb), bf16)],
        [SMEM] + [VMEM] * 2,
        [pltpu.VMEM((n_req, emb), f32)] + [pltpu.VMEM((owned + 8, emb), f32)] * 4,
        "owner_grads",
        32,
        0,
        60 * MIB,
    )(asked, arrived[0], arrived[1].reshape(devices, 2 * cap, emb))

    return (grad_u, grad_v, grad_b, grad_w, grad_freq, grad_inf)


def solution(mesh):
    in_specs = (
        P(None, "dev", None),
        P(None, "dev"),
        P(None, "dev", None, None),
        P(None, "dev", None, None),
        P(None, "dev", None, None),
        P(),
        P("dev", None),
        P(),
        P(),
        P(),
        P(),
        P(),
    )
    out_specs = (P("dev", None), P(None, "dev"), P("dev"), P("dev"), P(), P("dev", None))
    return jax.shard_map(
        on_device, mesh=mesh, in_specs=in_specs, out_specs=out_specs, check_vma=False
    )
```

```python
import functools
import math

import jax
import jax.numpy as jnp
from jax import lax
from jax.experimental import pallas as pl
from jax.experimental.pallas import tpu as pltpu
from jax.sharding import PartitionSpec as P

loss_scale = 1024.0
f32 = jnp.float32
bf16 = jnp.bfloat16
MIB = 1024 * 1024
SMEM = pl.BlockSpec(memory_space=pltpu.SMEM)
VMEM = pl.BlockSpec(memory_space=pltpu.VMEM)
HBM = pl.BlockSpec(memory_space=pltpu.HBM)
NT = (((1,), (1,)), ((), ()))
TN = (((0,), (0,)), ((), ()))


def local_call(
    kernel, outs, in_specs, scratch, name, limit, flops, bytes_accessed, out_specs=None, aliases={}
):
    return pl.pallas_call(
        kernel,
        out_shape=[jax.ShapeDtypeStruct(s, d) for s, d in outs],
        in_specs=in_specs,
        out_specs=out_specs or [VMEM] * len(outs),
        scratch_shapes=scratch,
        compiler_params=pltpu.CompilerParams(vmem_limit_bytes=limit * MIB),
        cost_estimate=pl.CostEstimate(
            flops=flops, bytes_accessed=bytes_accessed, transcendentals=0
        ),
        input_output_aliases=aliases,
        name=name,
    )


def freq_kernel(blocks, samples, first_micro, ids, table_ref, *refs):
    *outs, table = refs
    table[...] = table_ref[...].astype(f32)
    unroll = 32
    for m, out in enumerate(outs):
        start = (first_micro + m) * blocks * 2 * samples

        def group(g, carry):
            def some(k, carry):
                for u in range(unroll):
                    s = k * unroll + u
                    first = ids[start + g * 2 * samples + s]
                    second = ids[start + g * 2 * samples + samples + s]
                    out[pl.ds(g * samples + s, 1), :] = (
                        table[pl.ds(first, 1), :] + table[pl.ds(second, 1), :]
                    )
                return carry

            return lax.fori_loop(0, samples // unroll, some, carry)

        lax.fori_loop(0, blocks, group, 0)


def lookup_kernel(peers, stride, start, cap, asked, table_ref, out, table, rows):
    table[...] = table_ref[...].astype(f32)

    def peer(d, carry):
        for c in range(cap):
            r = asked[d * stride + start + c]
            rows[pl.ds(d * cap + c, 1), :] = table[pl.ds(r, 1), :]
        return carry

    lax.fori_loop(0, peers, peer, 0)
    out[...] = rows[...].astype(bf16)


def micro_kernel(
    peers,
    cap,
    features,
    slot_start,
    fetch_start,
    ret_start,
    loss_mult,
    slots,
    out_b,
    fetched_hbm,
    freq_part_hbm,
    bottom,
    labels,
    cross_u_hbm,
    cross_v_hbm,
    bias,
    weight,
    *refs,
):
    (
        returned_hbm,
        d_pooled_hbm,
        x_zero_hbm,
        hidden_hbm,
        d_hidden_hbm,
        gate_low_hbm,
        grad_bw,
        arrived,
        acc0,
        acc1,
        acc2,
        acc3,
        gate,
        returned,
        x_zero,
        hidden_out,
        d_hidden_out,
        gate_low,
        cross_u,
        cross_v,
        sems,
    ) = refs[-21:]
    samples, width = x_zero.shape
    emb = bottom.shape[1]
    n_slots = features * samples
    accs = (acc0, acc1, acc2, acc3)
    loads = [
        pltpu.make_async_copy(
            fetched_hbm.at[:, pl.ds(fetch_start, cap), :], returned, sems.at[6]
        ),
        pltpu.make_async_copy(freq_part_hbm, acc0.at[pl.ds(0, n_slots), :], sems.at[7]),
        pltpu.make_async_copy(cross_u_hbm, cross_u, sems.at[8]),
        pltpu.make_async_copy(cross_v_hbm, cross_v, sems.at[9]),
    ]
    for load in loads:
        load.start()
    for a in accs[1:]:
        a[...] = jnp.zeros_like(a)
    acc0[n_slots:, :] = jnp.zeros((acc0.shape[0] - n_slots, emb), f32)
    loads[0].wait()
    arrived[...] = returned[...].astype(f32).reshape(peers * cap, emb)
    loads[1].wait()

    def add_peer(o, carry):
        for c in range(0, cap, 4):
            at = [slots[slot_start + (c + j) * peers + o] for j in range(4)]
            new = [
                accs[j][pl.ds(at[j], 1), :] + arrived[pl.ds(o * cap + c + j, 1), :]
                for j in range(4)
            ]
            for j in range(4):
                accs[j][pl.ds(at[j], 1), :] = new[j]
        return carry

    lax.fori_loop(0, peers, add_peer, 0)

    x_zero[:, 0:emb] = bottom[...]
    for f in range(features):
        rows = pl.ds(f * samples, samples)
        total = (acc0[rows, :] + acc1[rows, :]) + (acc2[rows, :] + acc3[rows, :])
        x_zero[:, (f + 1) * emb : (f + 2) * emb] = total.astype(bf16)

    loads[2].wait()
    loads[3].wait()
    hidden = jnp.dot(x_zero[...], cross_u[...], preferred_element_type=f32).astype(bf16)
    hidden_out[...] = hidden
    copies = [
        pltpu.make_async_copy(x_zero, x_zero_hbm, sems.at[0]),
        pltpu.make_async_copy(hidden_out, hidden_hbm, sems.at[1]),
    ]
    for copy in copies:
        copy.start()
    chunk = 3 * emb
    chunks = width // chunk
    partial = jnp.zeros((samples, emb), f32)
    for k in range(chunks):
        cols = slice(k * chunk, (k + 1) * chunk)
        value = jnp.dot(hidden, cross_v[:, cols], preferred_element_type=f32) + bias[:, cols]
        gate[:, cols] = value
        x_float = x_zero[:, cols].astype(f32)
        scored = (x_float * value + x_float) * weight[:, cols]
        for j in range(3):
            partial = partial + scored[:, j * emb : (j + 1) * emb]
    logits = jnp.sum(partial, axis=1, keepdims=True) + out_b[0]
    d_logit = (jax.nn.sigmoid(logits) - labels[...]) * loss_mult
    for k in range(chunks):
        cols = slice(k * chunk, (k + 1) * chunk)
        x_float = x_zero[:, cols].astype(f32)
        d_gate = (d_logit * weight[:, cols]) * x_float
        gate_low[:, cols] = d_gate.astype(bf16)
        crossed = x_float * gate[:, cols] + x_float
        grad_bw[0:1, cols] = jnp.sum(d_gate, axis=0, keepdims=True)
        grad_bw[1:2, cols] = jnp.sum(d_logit * crossed, axis=0, keepdims=True)
    d_hidden = lax.dot_general(
        gate_low[...], cross_v[...], NT, preferred_element_type=f32
    ).astype(bf16)
    d_hidden_out[...] = d_hidden
    later = [
        pltpu.make_async_copy(gate_low, gate_low_hbm, sems.at[2]),
        pltpu.make_async_copy(d_hidden_out, d_hidden_hbm, sems.at[3]),
    ]
    for copy in later:
        copy.start()
    for k in range(chunks):
        cols = slice(k * chunk, (k + 1) * chunk)
        back = lax.dot_general(d_hidden, cross_u[cols, :], NT, preferred_element_type=f32)
        d_input = (d_logit * weight[:, cols]) * (gate[:, cols] + 1.0) + back
        for j in range(3):
            f = 3 * k + j - 1
            if f >= 0:
                acc0[f * samples : (f + 1) * samples, :] = d_input[:, j * emb : (j + 1) * emb]
    acc0[n_slots:, :] = jnp.zeros((acc0.shape[0] - n_slots, emb), f32)
    pooled_copy = pltpu.make_async_copy(acc0.at[pl.ds(0, n_slots), :], d_pooled_hbm, sems.at[4])
    pooled_copy.start()

    def take_peer(o, carry):
        for c in range(cap):
            at = slots[slot_start + c * peers + o]
            arrived[pl.ds(o * cap + c, 1), :] = acc0[pl.ds(at, 1), :]
        return carry

    lax.fori_loop(0, peers, take_peer, 0)
    returned[...] = arrived[...].astype(bf16).reshape(peers, cap, emb)
    returned_copy = pltpu.make_async_copy(
        returned, returned_hbm.at[:, pl.ds(ret_start, cap), :], sems.at[5]
    )
    returned_copy.start()
    for copy in copies + later:
        copy.wait()
    pooled_copy.wait()
    returned_copy.wait()


def dense_grad_kernel(
    peers, per, columns, x0, x1, x2, g0, g1, g2, h0, h1, h2, e0, e1, e2, parts, total
):
    width = x0.shape[1]
    rank = h0.shape[1]
    chunk = 128
    h_all = jnp.concatenate([h0[...], h1[...], h2[...]], axis=0)
    e_all = jnp.concatenate([e0[...], e1[...], e2[...]], axis=0)
    for k in range(width // chunk):
        cols = slice(k * chunk, (k + 1) * chunk)
        x_all = jnp.concatenate([x0[:, cols], x1[:, cols], x2[:, cols]], axis=0)
        g_all = jnp.concatenate([g0[:, cols], g1[:, cols], g2[:, cols]], axis=0)
        total[cols, 0:rank] = lax.dot_general(x_all, e_all, TN, preferred_element_type=f32)
        total[cols, rank : 2 * rank] = lax.dot_general(
            g_all, h_all, TN, preferred_element_type=f32
        )
    total[width:, :] = jnp.zeros((total.shape[0] - width, 2 * rank), f32)
    rows = parts.shape[1]
    spare = lax.broadcasted_iota(jnp.int32, (16, 128), 0) >= per - 16

    def blocks(q, carry):
        base = q * 8 * per
        for i in range(8):
            skip = i * per % 8
            window = total[pl.ds(pl.multiple_of(base + (i * per - skip), 8), rows + 8), :]
            value = window[skip : skip + rows]
            at = (i * 4 + q % 4) * 4 + q // 4
            parts[at, 0:16, :] = value[0:16].astype(bf16)
            parts[at, 16:32, 128:] = value[16:32, 128:].astype(bf16)
            parts[at, 16:32, 0:128] = jnp.where(
                spare, columns[q * 8 + i], value[16:32, 0:128]
            ).astype(bf16)
        return carry

    lax.fori_loop(0, peers // 8, blocks, 0)


def freq_grad_kernel(features, core, ids, d0, d1, d2, keep, send, acc0, acc1, acc2, acc3):
    accs = (acc0, acc1, acc2, acc3)
    samples = d0.shape[0] // features
    for a in accs:
        a[...] = jnp.zeros_like(a)
    unroll = 32
    for m, source in enumerate((d0, d1, d2)):
        start = m * features * 2 * samples

        def feature(f, carry):
            def some(k, carry):
                for u in range(0, unroll, 2):
                    s = k * unroll + u
                    at = [
                        ids[start + (2 * f + h) * samples + s + j]
                        for j in range(2)
                        for h in range(2)
                    ]
                    value = [source[pl.ds(f * samples + s + j, 1), :] for j in range(2)]
                    new = [accs[j][pl.ds(at[j], 1), :] + value[j // 2] for j in range(4)]
                    for j in range(4):
                        accs[j][pl.ds(at[j], 1), :] = new[j]
                return carry

            return lax.fori_loop(0, samples // unroll, some, carry)

        lax.fori_loop(0, features, feature, 0)
    rows = 128
    mine = core[0]

    def block(q, carry):
        for ref, parity in ((keep, mine), (send, 1 - mine)):
            at = pl.ds(pl.multiple_of((2 * q + parity) * rows, rows), rows)
            total = (acc0[at, :] + acc1[at, :]) + (acc2[at, :] + acc3[at, :])
            ref[q] = total.astype(bf16)
        return carry

    lax.fori_loop(0, keep.shape[0], block, 0)


def owner_kernel(peers, stride, cap, asked, arrived, out, rows, acc0, acc1, acc2, acc3):
    accs = (acc0, acc1, acc2, acc3)
    for a in accs:
        a[...] = jnp.zeros_like(a)
    emb = out.shape[1]
    for m in range(3):
        part = arrived[:, m * cap : (m + 1) * cap, :]
        rows[...] = part.astype(f32).reshape(peers * cap, emb)

        def peer(d, carry):
            for c in range(0, cap, 4):
                at = [asked[d * stride + m * cap + c + j] for j in range(4)]
                new = [
                    accs[j][pl.ds(at[j], 1), :] + rows[pl.ds(d * cap + c + j, 1), :]
                    for j in range(4)
                ]
                for j in range(4):
                    accs[j][pl.ds(at[j], 1), :] = new[j]
            return carry

        lax.fori_loop(0, peers, peer, 0)
    at = slice(0, out.shape[0])
    out[...] = ((acc0[at, :] + acc1[at, :]) + (acc2[at, :] + acc3[at, :])).astype(bf16)


def on_device(
    bottom,
    labels,
    freq_ids,
    req_rows,
    req_slot,
    freq_table,
    inf_table,
    cross_u,
    cross_v,
    cross_bias,
    out_w,
    out_b,
):
    devices = lax.axis_size("dev")
    micro, samples, emb = bottom.shape
    features = freq_ids.shape[2]
    hot = freq_ids.shape[3]
    owned = inf_table.shape[0]
    cap = req_rows.shape[3]
    width, rank = cross_u.shape
    freq_rows = freq_table.shape[0]
    n_slots = samples * features
    n_req = devices * cap
    per = width // devices
    loss_mult = loss_scale / math.sqrt(micro * samples * devices)
    me = lax.axis_index("dev")
    core = (me % 2).astype(jnp.int32).reshape(1)
    other_core = [(d, d ^ 1) for d in range(devices)]
    same_core = [list(range(c, devices, 2)) for c in range(2)]

    ids = jnp.transpose(freq_ids, (0, 2, 3, 1)).reshape(-1)
    rows_mc = jnp.transpose(req_rows[:, 0], (0, 2, 1))
    slot_mc = jnp.transpose(req_slot[:, 0], (0, 2, 1))
    is_live = (rows_mc < owned) & (slot_mc < n_slots)
    place = jnp.where(
        is_live, (slot_mc % features) * samples + slot_mc // features, n_slots
    ).reshape(-1)
    line = jnp.where(
        (req_rows < owned) & (req_slot < n_slots), req_rows, owned
    )[:, 0]
    line = jnp.transpose(line, (1, 0, 2)).reshape(devices, micro * cap)
    stride = -(-micro * cap // 128) * 128
    line = jnp.pad(line, ((0, 0), (0, stride - micro * cap)), constant_values=owned)
    asked = lax.all_to_all(line, "dev", split_axis=0, concat_axis=0, tiled=True).reshape(-1)

    def freq_rows_of(first_micro, count):
        return local_call(
            functools.partial(freq_kernel, features, samples, first_micro),
            [((n_slots, emb), f32)] * count,
            [SMEM, VMEM],
            [pltpu.VMEM((freq_rows, emb), f32)],
            f"freq_rows{first_micro}",
            62,
            0,
            (12 + 14 * count) * MIB,
        )(ids, freq_table)

    freq_part = list(freq_rows_of(0, 1))
    asked, freq_part[0] = lax.optimization_barrier((asked, freq_part[0]))
    asked_row = jnp.minimum(asked, owned - 1)
    weight = out_w.astype(f32).reshape(1, width)
    bias = cross_bias.reshape(1, width)
    label_cols = labels.astype(f32).reshape(micro, samples, 1)
    bias_b = out_b.reshape(1)

    def exchange(rows, count):
        return lax.all_to_all(
            rows.reshape(devices, count, emb), "dev", split_axis=0, concat_axis=0, tiled=True
        ).reshape(n_req * count // cap, emb)

    outs = []

    def lookup(start, count):
        return local_call(
            functools.partial(lookup_kernel, devices, stride, start, count),
            [((devices * count, emb), bf16)],
            [SMEM, VMEM],
            [pltpu.VMEM((owned, emb), f32), pltpu.VMEM((devices * count, emb), f32)],
            f"lookup{start}",
            62,
            0,
            count * MIB * 5 // 8,
        )(asked_row, inf_table)[0]

    looked = lookup(0, cap)
    asked_row, looked = lax.optimization_barrier((asked_row, looked))
    looked_rest = lookup(cap, (micro - 1) * cap)
    fetched = exchange(looked, cap)
    looked_rest, fetched = lax.optimization_barrier((looked_rest, fetched))
    fetched_rest = exchange(looked_rest, (micro - 1) * cap)
    ids, looked_rest = lax.optimization_barrier((ids, looked_rest))
    freq_part += freq_rows_of(1, micro - 1)
    fetched, freq_part[1] = lax.optimization_barrier((fetched, freq_part[1]))
    for m in range(micro):
        if m == 1:
            fetched_rest, outs[0][6] = lax.optimization_barrier((fetched_rest, outs[0][6]))
        out = local_call(
            functools.partial(
                micro_kernel,
                devices,
                cap,
                features,
                m * n_req,
                max(m - 1, 0) * cap,
                m * cap,
                loss_mult,
            ),
            [
                ((devices, micro * cap, emb), bf16),
                ((n_slots, emb), f32),
                ((samples, width), bf16),
                ((samples, rank), bf16),
                ((samples, rank), bf16),
                ((samples, width), bf16),
                ((2, width), f32),
            ],
            [SMEM, SMEM, HBM, HBM, VMEM, VMEM, HBM, HBM, VMEM, VMEM] + ([HBM] if m else []),
            [pltpu.VMEM((n_req, emb), f32)]
            + [pltpu.VMEM((n_slots + 8, emb), f32)] * 4
            + [pltpu.VMEM((samples, width), f32)]
            + [pltpu.VMEM((devices, cap, emb), bf16), pltpu.VMEM((samples, width), bf16)]
            + [pltpu.VMEM((samples, rank), bf16)] * 2
            + [pltpu.VMEM((samples, width), bf16)]
            + [pltpu.VMEM((width, rank), bf16), pltpu.VMEM((rank, width), bf16)]
            + [pltpu.SemaphoreType.DMA((10,))],
            f"micro{m}",
            62,
            6 * samples * width * rank,
            60 * MIB,
            [HBM] * 6 + [VMEM],
            {10: 0} if m else {},
        )(
            place,
            bias_b,
            (fetched_rest if m else fetched).reshape(devices, -1, emb),
            freq_part[m],
            bottom[m],
            label_cols[m],
            cross_u,
            cross_v,
            bias,
            weight,
            *([outs[m - 1][0]] if m else []),
        )
        outs.append(list(out))
        if m == 1:
            place, outs[1][6] = lax.optimization_barrier((place, outs[1][6]))
    arrived = exchange(outs[2][0], micro * cap)
    d_pooled = [o[1] for o in outs]
    grad_bw = ((outs[0][6] + outs[1][6]) + outs[2][6]).reshape(2, devices, per)
    columns = jnp.pad(
        jnp.transpose(grad_bw, (1, 0, 2)), ((0, 0), (per - 16, 30 - per), (0, 128 - per))
    )

    rows_pad = -(-per // 16) * 16
    per_freq = freq_rows // devices
    (dense,) = local_call(
        functools.partial(dense_grad_kernel, devices, per),
        [((devices, rows_pad, 2 * rank), bf16)],
        [VMEM] * 13,
        [pltpu.VMEM((width + 16, 2 * rank), f32)],
        "dense_grads",
        62,
        12 * samples * width * rank,
        40 * MIB,
    )(
        columns,
        *[o[2] for o in outs],
        *[o[5] for o in outs],
        *[o[3] for o in outs],
        *[o[4] for o in outs],
    )
    core, dense = lax.optimization_barrier((core, dense))
    for step, size in ((1, 8), (8, 4), (32, 4)):
        groups = [
            [d + k * step for k in range(size)]
            for d in range(devices)
            if d // step % size == 0
        ]
        dense = lax.psum_scatter(dense, "dev", axis_index_groups=groups, tiled=True)
    dense = dense.reshape(rows_pad, 2 * rank).astype(f32)
    grad_u = dense[:per, :rank]
    grad_v = dense[:per, rank:].T
    grad_b = dense[per, :per]
    grad_w = dense[per + 1, :per]

    keep_f, send_f = local_call(
        functools.partial(freq_grad_kernel, features),
        [((devices // 2, per_freq, emb), bf16)] * 2,
        [SMEM, SMEM] + [VMEM] * 3,
        [pltpu.VMEM((freq_rows, emb), f32)] * 4,
        "freq_grads",
        62,
        0,
        120 * MIB,
    )(core, ids, *d_pooled)
    send_f, arrived = lax.optimization_barrier((send_f, arrived))
    got = lax.ppermute(send_f, "dev", other_core)
    both = (keep_f.astype(f32) + got.astype(f32)).astype(bf16)
    parts = lax.all_to_all(
        both, "dev", split_axis=0, concat_axis=0, axis_index_groups=same_core, tiled=True
    )
    mine = jnp.sum(parts.astype(f32), axis=0).astype(bf16)
    half = lax.all_to_all(
        jnp.broadcast_to(mine[None], parts.shape),
        "dev",
        split_axis=0,
        concat_axis=0,
        axis_index_groups=same_core,
        tiled=True,
    )
    rest = lax.ppermute(half, "dev", other_core)
    grad_freq = jnp.where(
        core[0] == 0, jnp.stack([half, rest], axis=1), jnp.stack([rest, half], axis=1)
    ).reshape(freq_rows, emb)

    (grad_inf,) = local_call(
        functools.partial(owner_kernel, devices, stride, cap),
        [((owned, emb), bf16)],
        [SMEM, VMEM],
        [pltpu.VMEM((n_req, emb), f32)] + [pltpu.VMEM((owned + 8, emb), f32)] * 4,
        "owner_grads",
        32,
        0,
        60 * MIB,
    )(asked, arrived.reshape(devices, micro * cap, emb))

    return (grad_u, grad_v, grad_b, grad_w, grad_freq, grad_inf)


def solution(mesh):
    in_specs = (
        P(None, "dev", None),
        P(None, "dev"),
        P(None, "dev", None, None),
        P(None, "dev", None, None),
        P(None, "dev", None, None),
        P(),
        P("dev", None),
        P(),
        P(),
        P(),
        P(),
        P(),
    )
    out_specs = (P("dev", None), P(None, "dev"), P("dev"), P("dev"), P(), P("dev", None))
    return jax.shard_map(
        on_device, mesh=mesh, in_specs=in_specs, out_specs=out_specs, check_vma=False
    )
```

```python
import functools
import math

import jax
import jax.numpy as jnp
from jax import lax
from jax.experimental import pallas as pl
from jax.experimental.pallas import tpu as pltpu
from jax.sharding import PartitionSpec as P

loss_scale = 1024.0
f32 = jnp.float32
bf16 = jnp.bfloat16
MIB = 1024 * 1024
SMEM = pl.BlockSpec(memory_space=pltpu.SMEM)
VMEM = pl.BlockSpec(memory_space=pltpu.VMEM)
HBM = pl.BlockSpec(memory_space=pltpu.HBM)
NT = (((1,), (1,)), ((), ()))
TN = (((0,), (0,)), ((), ()))


def local_call(
    kernel, outs, in_specs, scratch, name, limit, flops, bytes_accessed, out_specs=None, aliases={}
):
    return pl.pallas_call(
        kernel,
        out_shape=[jax.ShapeDtypeStruct(s, d) for s, d in outs],
        in_specs=in_specs,
        out_specs=out_specs or [VMEM] * len(outs),
        scratch_shapes=scratch,
        compiler_params=pltpu.CompilerParams(vmem_limit_bytes=limit * MIB),
        cost_estimate=pl.CostEstimate(
            flops=flops, bytes_accessed=bytes_accessed, transcendentals=0
        ),
        input_output_aliases=aliases,
        name=name,
    )


def freq_kernel(blocks, samples, first_micro, ids, table_ref, *refs):
    *outs, table = refs
    table[...] = table_ref[...].astype(f32)
    unroll = 32
    for m, out in enumerate(outs):
        start = (first_micro + m) * blocks * 2 * samples

        def group(g, carry):
            def some(k, carry):
                for u in range(unroll):
                    s = k * unroll + u
                    first = ids[start + g * 2 * samples + s]
                    second = ids[start + g * 2 * samples + samples + s]
                    out[pl.ds(g * samples + s, 1), :] = (
                        table[pl.ds(first, 1), :] + table[pl.ds(second, 1), :]
                    )
                return carry

            return lax.fori_loop(0, samples // unroll, some, carry)

        lax.fori_loop(0, blocks, group, 0)


def lookup_kernel(peers, stride, start, cap, asked, table_ref, out, table, rows):
    table[...] = table_ref[...].astype(f32)

    def peer(d, carry):
        for c in range(cap):
            r = asked[d * stride + start + c]
            rows[pl.ds(d * cap + c, 1), :] = table[pl.ds(r, 1), :]
        return carry

    lax.fori_loop(0, peers, peer, 0)
    out[...] = rows[...].astype(bf16)


def micro_kernel(
    peers,
    cap,
    features,
    m,
    slot_start,
    fetch_start,
    ret_start,
    loss_mult,
    slots,
    out_b,
    fetched_hbm,
    freq_part_hbm,
    bottom,
    labels,
    cross_u_hbm,
    cross_v_hbm,
    bias,
    weight,
    *refs,
):
    (
        returned_hbm,
        d_pooled_hbm,
        x_zero_hbm,
        hidden_hbm,
        d_hidden_hbm,
        gate_low_hbm,
        grad_bw,
        arrived,
        acc0,
        acc1,
        acc2,
        acc3,
        gate,
        returned,
        x_zero,
        hidden_out,
        d_hidden_out,
        gate_low,
        cross_u,
        cross_v,
        sems,
    ) = refs[-21:]
    samples, width = x_zero.shape
    emb = bottom.shape[2]
    n_slots = features * samples
    accs = (acc0, acc1, acc2, acc3)
    loads = [
        pltpu.make_async_copy(
            fetched_hbm.at[:, pl.ds(fetch_start, cap), :], returned, sems.at[6]
        ),
        pltpu.make_async_copy(freq_part_hbm, acc0.at[pl.ds(0, n_slots), :], sems.at[7]),
        pltpu.make_async_copy(cross_u_hbm, cross_u, sems.at[8]),
        pltpu.make_async_copy(cross_v_hbm, cross_v, sems.at[9]),
    ]
    for load in loads:
        load.start()
    for a in accs[1:]:
        a[...] = jnp.zeros_like(a)
    acc0[n_slots:, :] = jnp.zeros((acc0.shape[0] - n_slots, emb), f32)
    loads[0].wait()
    arrived[...] = returned[...].astype(f32).reshape(peers * cap, emb)
    loads[1].wait()

    def add_peer(o, carry):
        for c in range(0, cap, 4):
            at = [slots[slot_start + (c + j) * peers + o] for j in range(4)]
            new = [
                accs[j][pl.ds(at[j], 1), :] + arrived[pl.ds(o * cap + c + j, 1), :]
                for j in range(4)
            ]
            for j in range(4):
                accs[j][pl.ds(at[j], 1), :] = new[j]
        return carry

    lax.fori_loop(0, peers, add_peer, 0)

    x_zero[:, 0:emb] = bottom[m]
    for f in range(features):
        rows = pl.ds(f * samples, samples)
        total = (acc0[rows, :] + acc1[rows, :]) + (acc2[rows, :] + acc3[rows, :])
        x_zero[:, (f + 1) * emb : (f + 2) * emb] = total.astype(bf16)

    loads[2].wait()
    loads[3].wait()
    hidden = jnp.dot(x_zero[...], cross_u[...], preferred_element_type=f32).astype(bf16)
    hidden_out[...] = hidden
    copies = [
        pltpu.make_async_copy(x_zero, x_zero_hbm, sems.at[0]),
        pltpu.make_async_copy(hidden_out, hidden_hbm, sems.at[1]),
    ]
    for copy in copies:
        copy.start()
    chunk = 3 * emb
    chunks = width // chunk
    partial = jnp.zeros((samples, emb), f32)
    for k in range(chunks):
        cols = slice(k * chunk, (k + 1) * chunk)
        value = jnp.dot(hidden, cross_v[:, cols], preferred_element_type=f32) + bias[:, cols]
        gate[:, cols] = value
        x_float = x_zero[:, cols].astype(f32)
        scored = (x_float * value + x_float) * weight[:, cols]
        for j in range(3):
            partial = partial + scored[:, j * emb : (j + 1) * emb]
    logits = jnp.sum(partial, axis=1, keepdims=True) + out_b[0]
    square = (samples, samples)
    diagonal = lax.broadcasted_iota(jnp.int32, square, 0) == lax.broadcasted_iota(
        jnp.int32, square, 1
    )
    label = jnp.sum(jnp.where(diagonal, labels[m : m + 1, :], 0.0), axis=1, keepdims=True)
    d_logit = (jax.nn.sigmoid(logits) - label) * loss_mult
    for k in range(chunks):
        cols = slice(k * chunk, (k + 1) * chunk)
        x_float = x_zero[:, cols].astype(f32)
        d_gate = (d_logit * weight[:, cols]) * x_float
        gate_low[:, cols] = d_gate.astype(bf16)
        crossed = x_float * gate[:, cols] + x_float
        grad_bw[0:1, cols] = jnp.sum(d_gate, axis=0, keepdims=True)
        grad_bw[1:2, cols] = jnp.sum(d_logit * crossed, axis=0, keepdims=True)
    d_hidden = lax.dot_general(
        gate_low[...], cross_v[...], NT, preferred_element_type=f32
    ).astype(bf16)
    d_hidden_out[...] = d_hidden
    later = [
        pltpu.make_async_copy(gate_low, gate_low_hbm, sems.at[2]),
        pltpu.make_async_copy(d_hidden_out, d_hidden_hbm, sems.at[3]),
    ]
    for copy in later:
        copy.start()
    for k in range(chunks):
        cols = slice(k * chunk, (k + 1) * chunk)
        back = lax.dot_general(d_hidden, cross_u[cols, :], NT, preferred_element_type=f32)
        d_input = (d_logit * weight[:, cols]) * (gate[:, cols] + 1.0) + back
        for j in range(3):
            f = 3 * k + j - 1
            if f >= 0:
                acc0[f * samples : (f + 1) * samples, :] = d_input[:, j * emb : (j + 1) * emb]
    acc0[n_slots:, :] = jnp.zeros((acc0.shape[0] - n_slots, emb), f32)
    pooled_copy = pltpu.make_async_copy(acc0.at[pl.ds(0, n_slots), :], d_pooled_hbm, sems.at[4])
    pooled_copy.start()

    def take_peer(o, carry):
        for c in range(cap):
            at = slots[slot_start + c * peers + o]
            arrived[pl.ds(o * cap + c, 1), :] = acc0[pl.ds(at, 1), :]
        return carry

    lax.fori_loop(0, peers, take_peer, 0)
    returned[...] = arrived[...].astype(bf16).reshape(peers, cap, emb)
    returned_copy = pltpu.make_async_copy(
        returned, returned_hbm.at[:, pl.ds(ret_start, cap), :], sems.at[5]
    )
    returned_copy.start()
    for copy in copies + later:
        copy.wait()
    pooled_copy.wait()
    returned_copy.wait()


def dense_grad_kernel(
    peers, per, columns, x0, x1, x2, g0, g1, g2, h0, h1, h2, e0, e1, e2, parts_hbm, total, parts, sem
):
    width = x0.shape[1]
    rank = h0.shape[1]
    chunk = 128
    h_all = jnp.concatenate([h0[...], h1[...], h2[...]], axis=0)
    e_all = jnp.concatenate([e0[...], e1[...], e2[...]], axis=0)
    for k in range(width // chunk):
        cols = slice(k * chunk, (k + 1) * chunk)
        x_all = jnp.concatenate([x0[:, cols], x1[:, cols], x2[:, cols]], axis=0)
        g_all = jnp.concatenate([g0[:, cols], g1[:, cols], g2[:, cols]], axis=0)
        total[cols, 0:rank] = lax.dot_general(x_all, e_all, TN, preferred_element_type=f32)
        total[cols, rank : 2 * rank] = lax.dot_general(
            g_all, h_all, TN, preferred_element_type=f32
        )
    total[width:, :] = jnp.zeros((total.shape[0] - width, 2 * rank), f32)
    rows = parts.shape[2]
    spare = lax.broadcasted_iota(jnp.int32, (16, 128), 0) >= per - 16

    def blocks(q, carry):
        base = q * 8 * per
        for i in range(8):
            skip = i * per % 8
            window = total[pl.ds(pl.multiple_of(base + (i * per - skip), 8), rows + 8), :]
            value = window[skip : skip + rows]
            parts[q, i, 0:16, :] = value[0:16].astype(bf16)
            parts[q, i, 16:32, 128:] = value[16:32, 128:].astype(bf16)
            parts[q, i, 16:32, 0:128] = jnp.where(
                spare, columns[q * 8 + i], value[16:32, 0:128]
            ).astype(bf16)
        pltpu.make_async_copy(
            parts.at[q], parts_hbm.at[:, q % 4 * 4 + q // 4], sem.at[q]
        ).start()
        return carry

    lax.fori_loop(0, peers // 8, blocks, 0)

    def ends(q, carry):
        pltpu.make_async_copy(
            parts.at[q], parts_hbm.at[:, q % 4 * 4 + q // 4], sem.at[q]
        ).wait()
        return carry

    lax.fori_loop(0, peers // 8, ends, 0)


def freq_grad_kernel(
    features, core, ids, d0, d1, d2, keep, send, acc0, acc1, acc2, acc3, buf0, buf1, buf2, sems
):
    accs = (acc0, acc1, acc2, acc3)
    samples = d0.shape[0] // features
    loads = [
        pltpu.make_async_copy(d, buf, sems.at[k])
        for k, (d, buf) in enumerate(((d0, buf0), (d1, buf1), (d2, buf2)))
    ]
    for load in loads:
        load.start()
    for a in accs:
        a[...] = jnp.zeros_like(a)
    unroll = 64
    for m, source in enumerate((buf0, buf1, buf2)):
        loads[m].wait()
        start = m * features * 2 * samples

        def feature(f, carry):
            def some(k, carry):
                for u in range(0, unroll, 2):
                    s = k * unroll + u
                    at = [
                        ids[start + (2 * f + h) * samples + s + j]
                        for j in range(2)
                        for h in range(2)
                    ]
                    value = [source[pl.ds(f * samples + s + j, 1), :] for j in range(2)]
                    new = [accs[j][pl.ds(at[j], 1), :] + value[j // 2] for j in range(4)]
                    for j in range(4):
                        accs[j][pl.ds(at[j], 1), :] = new[j]
                return carry

            return lax.fori_loop(0, samples // unroll, some, carry)

        lax.fori_loop(0, features, feature, 0)
    rows = 128
    mine = core[0]

    def block(q, carry):
        for ref, parity in ((keep, mine), (send, 1 - mine)):
            at = pl.ds(pl.multiple_of((2 * q + parity) * rows, rows), rows)
            total = (acc0[at, :] + acc1[at, :]) + (acc2[at, :] + acc3[at, :])
            ref[q] = total.astype(bf16)
        return carry

    lax.fori_loop(0, keep.shape[0], block, 0)


def owner_kernel(peers, stride, cap, asked, first, last, out, rows, acc0, acc1, acc2, acc3):
    accs = (acc0, acc1, acc2, acc3)
    for a in accs:
        a[...] = jnp.zeros_like(a)
    emb = out.shape[1]
    for m in range(3):
        part = last[...] if m == 2 else first[:, m * cap : (m + 1) * cap, :]
        rows[...] = part.astype(f32).reshape(peers * cap, emb)

        def peer(d, carry):
            for c in range(0, cap, 4):
                at = [asked[d * stride + m * cap + c + j] for j in range(4)]
                new = [
                    accs[j][pl.ds(at[j], 1), :] + rows[pl.ds(d * cap + c + j, 1), :]
                    for j in range(4)
                ]
                for j in range(4):
                    accs[j][pl.ds(at[j], 1), :] = new[j]
            return carry

        lax.fori_loop(0, peers, peer, 0)
    at = slice(0, out.shape[0])
    out[...] = ((acc0[at, :] + acc1[at, :]) + (acc2[at, :] + acc3[at, :])).astype(bf16)


def on_device(
    bottom,
    labels,
    freq_ids,
    req_rows,
    req_slot,
    freq_table,
    inf_table,
    cross_u,
    cross_v,
    cross_bias,
    out_w,
    out_b,
):
    devices = lax.axis_size("dev")
    micro, samples, emb = bottom.shape
    features = freq_ids.shape[2]
    hot = freq_ids.shape[3]
    owned = inf_table.shape[0]
    cap = req_rows.shape[3]
    width, rank = cross_u.shape
    freq_rows = freq_table.shape[0]
    n_slots = samples * features
    n_req = devices * cap
    per = width // devices
    loss_mult = loss_scale / math.sqrt(micro * samples * devices)
    me = lax.axis_index("dev")
    core = (me % 2).astype(jnp.int32).reshape(1)
    other_core = [(d, d ^ 1) for d in range(devices)]
    same_core = [list(range(c, devices, 2)) for c in range(2)]

    ids = jnp.transpose(freq_ids, (0, 2, 3, 1)).reshape(-1)
    rows_mc = jnp.transpose(req_rows[:, 0], (0, 2, 1))
    slot_mc = jnp.transpose(req_slot[:, 0], (0, 2, 1))
    is_live = (rows_mc < owned) & (slot_mc < n_slots)
    place = jnp.where(
        is_live, (slot_mc % features) * samples + slot_mc // features, n_slots
    ).reshape(-1)
    line = jnp.where(
        (req_rows < owned) & (req_slot < n_slots), req_rows, owned
    )[:, 0]
    line = jnp.transpose(line, (1, 0, 2)).reshape(devices, micro * cap)
    stride = -(-micro * cap // 128) * 128
    line = jnp.pad(line, ((0, 0), (0, stride - micro * cap)), constant_values=owned)
    asked = lax.all_to_all(line, "dev", split_axis=0, concat_axis=0, tiled=True).reshape(-1)

    def freq_rows_of(first_micro, count):
        return local_call(
            functools.partial(freq_kernel, features, samples, first_micro),
            [((n_slots, emb), f32)] * count,
            [SMEM, VMEM],
            [pltpu.VMEM((freq_rows, emb), f32)],
            f"freq_rows{first_micro}",
            62,
            0,
            (12 + 14 * count) * MIB,
        )(ids, freq_table)

    freq_part = list(freq_rows_of(0, 1))
    asked, freq_part[0] = lax.optimization_barrier((asked, freq_part[0]))
    asked_row = jnp.minimum(asked, owned - 1)
    weight = out_w.astype(f32).reshape(1, width)
    bias = cross_bias.reshape(1, width)
    label_rows = labels.astype(f32)
    bias_b = out_b.reshape(1)

    def exchange(rows, count):
        return lax.all_to_all(
            rows.reshape(devices, count, emb), "dev", split_axis=0, concat_axis=0, tiled=True
        ).reshape(n_req * count // cap, emb)

    outs = []

    def lookup(start, count):
        return local_call(
            functools.partial(lookup_kernel, devices, stride, start, count),
            [((devices * count, emb), bf16)],
            [SMEM, VMEM],
            [pltpu.VMEM((owned, emb), f32), pltpu.VMEM((devices * count, emb), f32)],
            f"lookup{start}",
            62,
            0,
            count * MIB * 5 // 8,
        )(asked_row, inf_table)[0]

    looked = lookup(0, cap)
    asked_row, looked = lax.optimization_barrier((asked_row, looked))
    looked_rest = lookup(cap, (micro - 1) * cap)
    fetched = exchange(looked, cap)
    ids, looked_rest = lax.optimization_barrier((ids, looked_rest))
    freq_part += freq_rows_of(1, 1)
    small = (place, weight, bias, label_rows, bias_b)
    looked_rest, fetched, freq_part[1], small = lax.optimization_barrier(
        (looked_rest, fetched, freq_part[1], small)
    )
    place, weight, bias, label_rows, bias_b = small
    fetched_rest = exchange(looked_rest, (micro - 1) * cap)
    ids, freq_part[1] = lax.optimization_barrier((ids, freq_part[1]))
    freq_part += freq_rows_of(2, 1)
    for m in range(micro):
        if m == 1:
            fetched_rest, outs[0][6], freq_part[2] = lax.optimization_barrier(
                (fetched_rest, outs[0][6], freq_part[2])
            )
        out = local_call(
            functools.partial(
                micro_kernel,
                devices,
                cap,
                features,
                m,
                m * n_req,
                max(m - 1, 0) * cap,
                cap if m == 1 else 0,
                loss_mult,
            ),
            [
                ((devices, cap if m == 2 else 2 * cap, emb), bf16),
                ((n_slots, emb), f32),
                ((samples, width), bf16),
                ((samples, rank), bf16),
                ((samples, rank), bf16),
                ((samples, width), bf16),
                ((2, width), f32),
            ],
            [SMEM, SMEM, HBM, HBM, VMEM, VMEM, HBM, HBM, VMEM, VMEM] + ([HBM] if m == 1 else []),
            [pltpu.VMEM((n_req, emb), f32)]
            + [pltpu.VMEM((n_slots + 8, emb), f32)] * 4
            + [pltpu.VMEM((samples, width), f32)]
            + [pltpu.VMEM((devices, cap, emb), bf16), pltpu.VMEM((samples, width), bf16)]
            + [pltpu.VMEM((samples, rank), bf16)] * 2
            + [pltpu.VMEM((samples, width), bf16)]
            + [pltpu.VMEM((width, rank), bf16), pltpu.VMEM((rank, width), bf16)]
            + [pltpu.SemaphoreType.DMA((10,))],
            f"micro{m}",
            62,
            6 * samples * width * rank,
            60 * MIB,
            [HBM] * 6 + [VMEM],
            {10: 0} if m == 1 else {},
        )(
            place,
            bias_b,
            (fetched_rest if m else fetched).reshape(devices, -1, emb),
            freq_part[m],
            bottom,
            label_rows,
            cross_u,
            cross_v,
            bias,
            weight,
            *([outs[0][0]] if m == 1 else []),
        )
        outs.append(list(out))
        if m == 1:
            place, outs[1][6] = lax.optimization_barrier((place, outs[1][6]))
    arrived_first = exchange(outs[1][0], 2 * cap)
    outs[2][0], arrived_first = lax.optimization_barrier((outs[2][0], arrived_first))
    arrived_last = exchange(outs[2][0], cap)
    d_pooled = [o[1] for o in outs]
    grad_bw = ((outs[0][6] + outs[1][6]) + outs[2][6]).reshape(2, devices, per)
    columns = jnp.pad(
        jnp.transpose(grad_bw, (1, 0, 2)), ((0, 0), (per - 16, 30 - per), (0, 128 - per))
    )

    rows_pad = -(-per // 16) * 16
    per_freq = freq_rows // devices
    (dense,) = local_call(
        functools.partial(dense_grad_kernel, devices, per),
        [((8, devices // 8, rows_pad, 2 * rank), bf16)],
        [VMEM] * 13,
        [
            pltpu.VMEM((width + 16, 2 * rank), f32),
            pltpu.VMEM((devices // 8, 8, rows_pad, 2 * rank), bf16),
            pltpu.SemaphoreType.DMA((devices // 8,)),
        ],
        "dense_grads",
        62,
        12 * samples * width * rank,
        40 * MIB,
        [HBM],
    )(
        columns,
        *[o[2] for o in outs],
        *[o[5] for o in outs],
        *[o[3] for o in outs],
        *[o[4] for o in outs],
    )
    core, dense, arrived_first = lax.optimization_barrier((core, dense, arrived_first))
    dense = dense.reshape(devices, rows_pad, 2 * rank)
    for step, size in ((1, 8), (8, 4), (32, 4)):
        groups = [
            [d + k * step for k in range(size)]
            for d in range(devices)
            if d // step % size == 0
        ]
        dense = lax.psum_scatter(dense, "dev", axis_index_groups=groups, tiled=True)
    dense = dense.reshape(rows_pad, 2 * rank).astype(f32)
    grad_u = dense[:per, :rank]
    grad_v = dense[:per, rank:].T
    grad_b = dense[per, :per]
    grad_w = dense[per + 1, :per]

    keep_f, send_f = local_call(
        functools.partial(freq_grad_kernel, features),
        [((devices // 2, per_freq, emb), bf16)] * 2,
        [SMEM, SMEM] + [HBM] * 3,
        [pltpu.VMEM((freq_rows, emb), f32)] * 4
        + [pltpu.VMEM((n_slots, emb), f32)] * 3
        + [pltpu.SemaphoreType.DMA((3,))],
        "freq_grads",
        62,
        0,
        120 * MIB,
    )(core, ids, *d_pooled)
    send_f, arrived_last = lax.optimization_barrier((send_f, arrived_last))
    got = lax.ppermute(send_f, "dev", other_core)
    both = (keep_f.astype(f32) + got.astype(f32)).astype(bf16)
    parts = lax.all_to_all(
        both, "dev", split_axis=0, concat_axis=0, axis_index_groups=same_core, tiled=True
    )
    (grad_inf,) = local_call(
        functools.partial(owner_kernel, devices, stride, cap),
        [((owned, emb), bf16)],
        [SMEM, VMEM, VMEM],
        [pltpu.VMEM((n_req, emb), f32)] + [pltpu.VMEM((owned + 8, emb), f32)] * 4,
        "owner_grads",
        32,
        0,
        60 * MIB,
    )(
        asked,
        arrived_first.reshape(devices, 2 * cap, emb),
        arrived_last.reshape(devices, cap, emb),
    )

    parts, grad_inf = lax.optimization_barrier((parts, grad_inf))
    mine = jnp.sum(parts.astype(f32), axis=0).astype(bf16)
    half = lax.all_to_all(
        jnp.broadcast_to(mine[None], parts.shape),
        "dev",
        split_axis=0,
        concat_axis=0,
        axis_index_groups=same_core,
        tiled=True,
    )
    rest = lax.ppermute(half, "dev", other_core)
    grad_freq = jnp.where(
        core[0] == 0, jnp.stack([half, rest], axis=1), jnp.stack([rest, half], axis=1)
    ).reshape(freq_rows, emb)

    return (grad_u, grad_v, grad_b, grad_w, grad_freq, grad_inf)


def solution(mesh):
    in_specs = (
        P(None, "dev", None),
        P(None, "dev"),
        P(None, "dev", None, None),
        P(None, "dev", None, None),
        P(None, "dev", None, None),
        P(),
        P("dev", None),
        P(),
        P(),
        P(),
        P(),
        P(),
    )
    out_specs = (P("dev", None), P(None, "dev"), P("dev"), P("dev"), P(), P("dev", None))
    return jax.shard_map(
        on_device, mesh=mesh, in_specs=in_specs, out_specs=out_specs, check_vma=False
    )
```

```python
import functools
import math

import jax
import jax.numpy as jnp
from jax import lax
from jax.experimental import pallas as pl
from jax.experimental.pallas import tpu as pltpu
from jax.sharding import PartitionSpec as P

loss_scale = 1024.0
f32 = jnp.float32
bf16 = jnp.bfloat16
MIB = 1024 * 1024
SMEM = pl.BlockSpec(memory_space=pltpu.SMEM)
VMEM = pl.BlockSpec(memory_space=pltpu.VMEM)
HBM = pl.BlockSpec(memory_space=pltpu.HBM)
NT = (((1,), (1,)), ((), ()))
TN = (((0,), (0,)), ((), ()))


def tree_sum(terms):
    while len(terms) > 1:
        terms = [sum(terms[k : k + 2][1:], terms[k]) for k in range(0, len(terms), 2)]
    return terms[0]


def local_call(
    kernel, outs, in_specs, scratch, name, limit, flops, bytes_accessed, out_specs=None, aliases={}
):
    return pl.pallas_call(
        kernel,
        out_shape=[jax.ShapeDtypeStruct(s, d) for s, d in outs],
        in_specs=in_specs,
        out_specs=out_specs or [VMEM] * len(outs),
        scratch_shapes=scratch,
        compiler_params=pltpu.CompilerParams(vmem_limit_bytes=limit * MIB),
        cost_estimate=pl.CostEstimate(
            flops=flops, bytes_accessed=bytes_accessed, transcendentals=0
        ),
        input_output_aliases=aliases,
        name=name,
    )


def freq_kernel(blocks, samples, first_micro, ids, table_ref, *refs):
    *outs, table = refs
    table[...] = table_ref[...].astype(f32)
    unroll = 32
    for m, out in enumerate(outs):
        start = (first_micro + m) * blocks * 2 * samples

        def group(g, carry):
            def some(k, carry):
                for u in range(unroll):
                    s = k * unroll + u
                    first = ids[start + g * 2 * samples + s]
                    second = ids[start + g * 2 * samples + samples + s]
                    out[pl.ds(g * samples + s, 1), :] = (
                        table[pl.ds(first, 1), :] + table[pl.ds(second, 1), :]
                    )
                return carry

            return lax.fori_loop(0, samples // unroll, some, carry)

        lax.fori_loop(0, blocks, group, 0)


def lookup_kernel(peers, stride, start, cap, asked, table_ref, out, table, rows):
    table[...] = table_ref[...].astype(f32)

    def peer(d, carry):
        for c in range(cap):
            r = asked[d * stride + start + c]
            rows[pl.ds(d * cap + c, 1), :] = table[pl.ds(r, 1), :]
        return carry

    lax.fori_loop(0, peers, peer, 0)
    out[...] = rows[...].astype(bf16)


def micro_kernel(
    peers,
    cap,
    features,
    m,
    slot_start,
    fetch_start,
    ret_start,
    loss_mult,
    slots,
    out_b,
    fetched_hbm,
    freq_part_hbm,
    bottom,
    labels,
    cross_u_hbm,
    cross_v_hbm,
    bias,
    weight,
    *refs,
):
    (
        returned_hbm,
        d_pooled_hbm,
        x_zero_hbm,
        hidden_hbm,
        d_hidden_hbm,
        gate_low_hbm,
        grad_bw,
        arrived,
        *accs,
        gate,
        returned,
        x_zero,
        hidden_out,
        d_hidden_out,
        gate_low,
        cross_u,
        cross_v,
        sems,
    ) = refs[-25:]
    acc0 = accs[0]
    samples, width = x_zero.shape
    emb = bottom.shape[2]
    n_slots = features * samples
    ways = len(accs)
    loads = [
        pltpu.make_async_copy(
            fetched_hbm.at[:, pl.ds(fetch_start, cap), :], returned, sems.at[6]
        ),
        pltpu.make_async_copy(freq_part_hbm, acc0.at[pl.ds(0, n_slots), :], sems.at[7]),
        pltpu.make_async_copy(cross_u_hbm, cross_u, sems.at[8]),
        pltpu.make_async_copy(cross_v_hbm, cross_v, sems.at[9]),
    ]
    for load in loads:
        load.start()
    for a in accs[1:]:
        a[...] = jnp.zeros_like(a)
    acc0[n_slots:, :] = jnp.zeros((acc0.shape[0] - n_slots, emb), f32)
    loads[0].wait()
    arrived[...] = returned[...].astype(f32).reshape(peers * cap, emb)
    loads[1].wait()

    def add_peer(o, carry):
        for c in range(0, cap, ways):
            at = [slots[slot_start + (c + j) * peers + o] for j in range(ways)]
            new = [
                accs[j][pl.ds(at[j], 1), :] + arrived[pl.ds(o * cap + c + j, 1), :]
                for j in range(ways)
            ]
            for j in range(ways):
                accs[j][pl.ds(at[j], 1), :] = new[j]
        return carry

    lax.fori_loop(0, peers, add_peer, 0)

    x_zero[:, 0:emb] = bottom[m]
    for f in range(features):
        rows = pl.ds(f * samples, samples)
        total = tree_sum([a[rows, :] for a in accs])
        x_zero[:, (f + 1) * emb : (f + 2) * emb] = total.astype(bf16)

    loads[2].wait()
    loads[3].wait()
    hidden = jnp.dot(x_zero[...], cross_u[...], preferred_element_type=f32).astype(bf16)
    hidden_out[...] = hidden
    copies = [
        pltpu.make_async_copy(x_zero, x_zero_hbm, sems.at[0]),
        pltpu.make_async_copy(hidden_out, hidden_hbm, sems.at[1]),
    ]
    for copy in copies:
        copy.start()
    chunk = 3 * emb
    chunks = width // chunk
    partial = jnp.zeros((samples, emb), f32)
    for k in range(chunks):
        cols = slice(k * chunk, (k + 1) * chunk)
        value = jnp.dot(hidden, cross_v[:, cols], preferred_element_type=f32) + bias[:, cols]
        gate[:, cols] = value
        x_float = x_zero[:, cols].astype(f32)
        scored = (x_float * value + x_float) * weight[:, cols]
        for j in range(3):
            partial = partial + scored[:, j * emb : (j + 1) * emb]
    logits = jnp.sum(partial, axis=1, keepdims=True) + out_b[0]
    square = (samples, samples)
    diagonal = lax.broadcasted_iota(jnp.int32, square, 0) == lax.broadcasted_iota(
        jnp.int32, square, 1
    )
    label = jnp.sum(jnp.where(diagonal, labels[m : m + 1, :], 0.0), axis=1, keepdims=True)
    d_logit = (jax.nn.sigmoid(logits) - label) * loss_mult
    for k in range(chunks):
        cols = slice(k * chunk, (k + 1) * chunk)
        x_float = x_zero[:, cols].astype(f32)
        d_gate = (d_logit * weight[:, cols]) * x_float
        gate_low[:, cols] = d_gate.astype(bf16)
        crossed = x_float * gate[:, cols] + x_float
        grad_bw[0:1, cols] = jnp.sum(d_gate, axis=0, keepdims=True)
        grad_bw[1:2, cols] = jnp.sum(d_logit * crossed, axis=0, keepdims=True)
    d_hidden = lax.dot_general(
        gate_low[...], cross_v[...], NT, preferred_element_type=f32
    ).astype(bf16)
    d_hidden_out[...] = d_hidden
    later = [
        pltpu.make_async_copy(gate_low, gate_low_hbm, sems.at[2]),
        pltpu.make_async_copy(d_hidden_out, d_hidden_hbm, sems.at[3]),
    ]
    for copy in later:
        copy.start()
    for k in range(chunks):
        cols = slice(k * chunk, (k + 1) * chunk)
        back = lax.dot_general(d_hidden, cross_u[cols, :], NT, preferred_element_type=f32)
        d_input = (d_logit * weight[:, cols]) * (gate[:, cols] + 1.0) + back
        for j in range(3):
            f = 3 * k + j - 1
            if f >= 0:
                acc0[f * samples : (f + 1) * samples, :] = d_input[:, j * emb : (j + 1) * emb]
    acc0[n_slots:, :] = jnp.zeros((acc0.shape[0] - n_slots, emb), f32)
    pooled_copy = pltpu.make_async_copy(acc0.at[pl.ds(0, n_slots), :], d_pooled_hbm, sems.at[4])
    pooled_copy.start()

    def take_peer(o, carry):
        for c in range(cap):
            at = slots[slot_start + c * peers + o]
            arrived[pl.ds(o * cap + c, 1), :] = acc0[pl.ds(at, 1), :]
        return carry

    lax.fori_loop(0, peers, take_peer, 0)
    returned[...] = arrived[...].astype(bf16).reshape(peers, cap, emb)
    returned_copy = pltpu.make_async_copy(
        returned, returned_hbm.at[:, pl.ds(ret_start, cap), :], sems.at[5]
    )
    returned_copy.start()
    for copy in copies + later:
        copy.wait()
    pooled_copy.wait()
    returned_copy.wait()


def dense_grad_kernel(
    peers, per, columns, x0, x1, x2, g0, g1, g2, h0, h1, h2, e0, e1, e2, parts_hbm, total, parts, sem
):
    width = x0.shape[1]
    rank = h0.shape[1]
    chunk = 128
    h_all = jnp.concatenate([h0[...], h1[...], h2[...]], axis=0)
    e_all = jnp.concatenate([e0[...], e1[...], e2[...]], axis=0)
    for k in range(width // chunk):
        cols = slice(k * chunk, (k + 1) * chunk)
        x_all = jnp.concatenate([x0[:, cols], x1[:, cols], x2[:, cols]], axis=0)
        g_all = jnp.concatenate([g0[:, cols], g1[:, cols], g2[:, cols]], axis=0)
        total[cols, 0:rank] = lax.dot_general(x_all, e_all, TN, preferred_element_type=f32)
        total[cols, rank : 2 * rank] = lax.dot_general(
            g_all, h_all, TN, preferred_element_type=f32
        )
    total[width:, :] = jnp.zeros((total.shape[0] - width, 2 * rank), f32)
    rows = parts.shape[2]
    spare = lax.broadcasted_iota(jnp.int32, (16, 128), 0) >= per - 16

    def blocks(q, carry):
        base = q * 8 * per
        for i in range(8):
            skip = i * per % 8
            window = total[pl.ds(pl.multiple_of(base + (i * per - skip), 8), rows + 8), :]
            value = window[skip : skip + rows]
            parts[q, i, 0:16, :] = value[0:16].astype(bf16)
            parts[q, i, 16:32, 128:] = value[16:32, 128:].astype(bf16)
            parts[q, i, 16:32, 0:128] = jnp.where(
                spare, columns[q * 8 + i], value[16:32, 0:128]
            ).astype(bf16)
        pltpu.make_async_copy(
            parts.at[q], parts_hbm.at[:, q % 4 * 4 + q // 4], sem.at[q]
        ).start()
        return carry

    lax.fori_loop(0, peers // 8, blocks, 0)

    def ends(q, carry):
        pltpu.make_async_copy(
            parts.at[q], parts_hbm.at[:, q % 4 * 4 + q // 4], sem.at[q]
        ).wait()
        return carry

    lax.fori_loop(0, peers // 8, ends, 0)


def freq_grad_kernel(
    features, core, ids, d0, d1, d2, keep, send, *scratch
):
    *accs, buf0, buf1, buf2, sems = scratch
    pairs = len(accs) // 2
    samples = d0.shape[0] // features
    loads = [
        pltpu.make_async_copy(d, buf, sems.at[k])
        for k, (d, buf) in enumerate(((d0, buf0), (d1, buf1), (d2, buf2)))
    ]
    for load in loads:
        load.start()
    for a in accs:
        a[...] = jnp.zeros_like(a)
    for m, source in enumerate((buf0, buf1, buf2)):
        loads[m].wait()
        start = m * features * 2 * samples

        def feature(f, carry):
            base = f * samples
            first = start + f * 2 * samples
            for s in range(0, samples, pairs):
                count = min(pairs, samples - s)
                at = [
                    ids[first + h * samples + s + j] for j in range(count) for h in range(2)
                ]
                value = [source[pl.ds(base + s + j, 1), :] for j in range(count)]
                new = [accs[j][pl.ds(at[j], 1), :] + value[j // 2] for j in range(2 * count)]
                for j in range(2 * count):
                    accs[j][pl.ds(at[j], 1), :] = new[j]
            return carry

        lax.fori_loop(0, features, feature, 0)
    rows = 128
    mine = core[0]

    def block(q, carry):
        for ref, parity in ((keep, mine), (send, 1 - mine)):
            at = pl.ds(pl.multiple_of((2 * q + parity) * rows, rows), rows)
            ref[q] = tree_sum([a[at, :] for a in accs]).astype(bf16)
        return carry

    lax.fori_loop(0, keep.shape[0], block, 0)


def spread_kernel(parts, out):
    total = parts[0].astype(f32)
    for k in range(1, parts.shape[0]):
        total = total + parts[k].astype(f32)
    total = total.astype(bf16)
    for k in range(parts.shape[0]):
        out[k] = total


def place_kernel(other, core, half, *refs):
    out, sem = refs[-2:]
    at = core[0] if other == 0 else 1 - core[0]
    copy = pltpu.make_async_copy(half, out.at[:, at], sem)
    copy.start()
    copy.wait()


def owner_kernel(peers, stride, cap, asked, first, last, out, rows, *accs):
    ways = len(accs)
    for a in accs:
        a[...] = jnp.zeros_like(a)
    emb = out.shape[1]
    for m in range(3):
        part = last[...] if m == 2 else first[:, m * cap : (m + 1) * cap, :]
        rows[...] = part.astype(f32).reshape(peers * cap, emb)

        def peer(d, carry):
            for c in range(0, cap, ways):
                at = [asked[d * stride + m * cap + c + j] for j in range(ways)]
                new = [
                    accs[j][pl.ds(at[j], 1), :] + rows[pl.ds(d * cap + c + j, 1), :]
                    for j in range(ways)
                ]
                for j in range(ways):
                    accs[j][pl.ds(at[j], 1), :] = new[j]
            return carry

        lax.fori_loop(0, peers, peer, 0)
    at = slice(0, out.shape[0])
    out[...] = tree_sum([a[at, :] for a in accs]).astype(bf16)


def on_device(
    bottom,
    labels,
    freq_ids,
    req_rows,
    req_slot,
    freq_table,
    inf_table,
    cross_u,
    cross_v,
    cross_bias,
    out_w,
    out_b,
):
    devices = lax.axis_size("dev")
    micro, samples, emb = bottom.shape
    features = freq_ids.shape[2]
    hot = freq_ids.shape[3]
    owned = inf_table.shape[0]
    cap = req_rows.shape[3]
    width, rank = cross_u.shape
    freq_rows = freq_table.shape[0]
    n_slots = samples * features
    n_req = devices * cap
    per = width // devices
    loss_mult = loss_scale / math.sqrt(micro * samples * devices)
    me = lax.axis_index("dev")
    core = (me % 2).astype(jnp.int32).reshape(1)
    other_core = [(d, d ^ 1) for d in range(devices)]
    same_core = [list(range(c, devices, 2)) for c in range(2)]

    ids = jnp.transpose(freq_ids, (0, 2, 3, 1)).reshape(-1)
    rows_mc = jnp.transpose(req_rows[:, 0], (0, 2, 1))
    slot_mc = jnp.transpose(req_slot[:, 0], (0, 2, 1))
    is_live = (rows_mc < owned) & (slot_mc < n_slots)
    place = jnp.where(
        is_live, (slot_mc % features) * samples + slot_mc // features, n_slots
    ).reshape(-1)
    line = jnp.where(
        (req_rows < owned) & (req_slot < n_slots), req_rows, owned
    )[:, 0]
    line = jnp.transpose(line, (1, 0, 2)).reshape(devices, micro * cap)
    stride = -(-micro * cap // 128) * 128
    line = jnp.pad(line, ((0, 0), (0, stride - micro * cap)), constant_values=owned)
    asked = lax.all_to_all(line, "dev", split_axis=0, concat_axis=0, tiled=True).reshape(-1)

    def freq_rows_of(first_micro, count):
        return local_call(
            functools.partial(freq_kernel, features, samples, first_micro),
            [((n_slots, emb), f32)] * count,
            [SMEM, VMEM],
            [pltpu.VMEM((freq_rows, emb), f32)],
            f"freq_rows{first_micro}",
            62,
            0,
            (12 + 14 * count) * MIB,
        )(ids, freq_table)

    freq_part = list(freq_rows_of(0, 1))
    asked, freq_part[0] = lax.optimization_barrier((asked, freq_part[0]))
    asked_row = jnp.minimum(asked, owned - 1)
    weight = out_w.astype(f32).reshape(1, width)
    bias = cross_bias.reshape(1, width)
    label_rows = labels.astype(f32)
    bias_b = out_b.reshape(1)

    def axis_sum(blocks, step):
        at = me // step % 4
        total = lax.dynamic_index_in_dim(blocks, at, 0, keepdims=False).astype(f32)
        for k in range(1, 4):
            block = lax.dynamic_index_in_dim(blocks, (at + k) % 4, 0, keepdims=False)
            to = [(d, d + ((d // step % 4 + k) % 4 - d // step % 4) * step) for d in range(devices)]
            total = total + lax.ppermute(block, "dev", to).astype(f32)
        return total

    def exchange(rows, count):
        return lax.all_to_all(
            rows.reshape(devices, count, emb), "dev", split_axis=0, concat_axis=0, tiled=True
        ).reshape(n_req * count // cap, emb)

    outs = []

    def lookup(start, count):
        return local_call(
            functools.partial(lookup_kernel, devices, stride, start, count),
            [((devices * count, emb), bf16)],
            [SMEM, VMEM],
            [pltpu.VMEM((owned, emb), f32), pltpu.VMEM((devices * count, emb), f32)],
            f"lookup{start}",
            62,
            0,
            count * MIB * 5 // 8,
        )(asked_row, inf_table)[0]

    looked = lookup(0, cap)
    asked_row, looked = lax.optimization_barrier((asked_row, looked))
    looked_rest = lookup(cap, (micro - 1) * cap)
    fetched = exchange(looked, cap)
    ids, looked_rest = lax.optimization_barrier((ids, looked_rest))
    freq_part += freq_rows_of(1, 1)
    small = (place, weight, bias, label_rows, bias_b)
    looked_rest, fetched, freq_part[1], small = lax.optimization_barrier(
        (looked_rest, fetched, freq_part[1], small)
    )
    place, weight, bias, label_rows, bias_b = small
    fetched_rest = exchange(looked_rest, (micro - 1) * cap)
    ids, freq_part[1] = lax.optimization_barrier((ids, freq_part[1]))
    freq_part += freq_rows_of(2, 1)
    for m in range(micro):
        if m == 1:
            fetched_rest, outs[0][6], freq_part[2] = lax.optimization_barrier(
                (fetched_rest, outs[0][6], freq_part[2])
            )
        out = local_call(
            functools.partial(
                micro_kernel,
                devices,
                cap,
                features,
                m,
                m * n_req,
                max(m - 1, 0) * cap,
                cap if m == 1 else 0,
                loss_mult,
            ),
            [
                ((devices, cap if m == 2 else 2 * cap, emb), bf16),
                ((n_slots, emb), f32),
                ((samples, width), bf16),
                ((samples, rank), bf16),
                ((samples, rank), bf16),
                ((samples, width), bf16),
                ((2, width), f32),
            ],
            [SMEM, SMEM, HBM, HBM, VMEM, VMEM, HBM, HBM, VMEM, VMEM] + ([HBM] if m == 1 else []),
            [pltpu.VMEM((n_req, emb), f32)]
            + [pltpu.VMEM((n_slots + 8, emb), f32)] * 8
            + [pltpu.VMEM((samples, width), f32)]
            + [pltpu.VMEM((devices, cap, emb), bf16), pltpu.VMEM((samples, width), bf16)]
            + [pltpu.VMEM((samples, rank), bf16)] * 2
            + [pltpu.VMEM((samples, width), bf16)]
            + [pltpu.VMEM((width, rank), bf16), pltpu.VMEM((rank, width), bf16)]
            + [pltpu.SemaphoreType.DMA((10,))],
            f"micro{m}",
            62,
            6 * samples * width * rank,
            60 * MIB,
            [HBM] * 6 + [VMEM],
            {10: 0} if m == 1 else {},
        )(
            place,
            bias_b,
            (fetched_rest if m else fetched).reshape(devices, -1, emb),
            freq_part[m],
            bottom,
            label_rows,
            cross_u,
            cross_v,
            bias,
            weight,
            *([outs[0][0]] if m == 1 else []),
        )
        outs.append(list(out))
        if m == 1:
            place, outs[1][6] = lax.optimization_barrier((place, outs[1][6]))
    arrived_first = exchange(outs[1][0], 2 * cap)
    outs[2][0], arrived_first = lax.optimization_barrier((outs[2][0], arrived_first))
    arrived_last = exchange(outs[2][0], cap)
    d_pooled = [o[1] for o in outs]
    grad_bw = ((outs[0][6] + outs[1][6]) + outs[2][6]).reshape(2, devices, per)
    columns = jnp.pad(
        jnp.transpose(grad_bw, (1, 0, 2)), ((0, 0), (per - 16, 30 - per), (0, 128 - per))
    )

    rows_pad = -(-per // 16) * 16
    per_freq = freq_rows // devices
    (dense,) = local_call(
        functools.partial(dense_grad_kernel, devices, per),
        [((8, devices // 8, rows_pad, 2 * rank), bf16)],
        [VMEM] * 13,
        [
            pltpu.VMEM((width + 16, 2 * rank), f32),
            pltpu.VMEM((devices // 8, 8, rows_pad, 2 * rank), bf16),
            pltpu.SemaphoreType.DMA((devices // 8,)),
        ],
        "dense_grads",
        62,
        12 * samples * width * rank,
        40 * MIB,
        [HBM],
    )(
        columns,
        *[o[2] for o in outs],
        *[o[5] for o in outs],
        *[o[3] for o in outs],
        *[o[4] for o in outs],
    )
    core, dense, arrived_first = lax.optimization_barrier((core, dense, arrived_first))
    dense = dense.reshape(devices, rows_pad, 2 * rank)
    near = [list(range(d, d + 8)) for d in range(0, devices, 8)]
    dense = lax.psum_scatter(dense, "dev", axis_index_groups=near, tiled=True)
    dense = axis_sum(dense.reshape(4, 4, rows_pad, 2 * rank), 8).astype(bf16)
    dense = axis_sum(dense, 32)
    keep_f, send_f = local_call(
        functools.partial(freq_grad_kernel, features),
        [((devices // 2, per_freq, emb), bf16)] * 2,
        [SMEM, SMEM] + [HBM] * 3,
        [pltpu.VMEM((freq_rows, emb), f32)] * 6
        + [pltpu.VMEM((n_slots, emb), f32)] * 3
        + [pltpu.SemaphoreType.DMA((3,))],
        "freq_grads",
        62,
        0,
        120 * MIB,
    )(core, ids, *d_pooled)
    send_f, arrived_last = lax.optimization_barrier((send_f, arrived_last))
    got = lax.ppermute(send_f, "dev", other_core)
    both = (keep_f.astype(f32) + got.astype(f32)).astype(bf16)
    parts = lax.all_to_all(
        both, "dev", split_axis=0, concat_axis=0, axis_index_groups=same_core, tiled=True
    )
    (grad_inf,) = local_call(
        functools.partial(owner_kernel, devices, stride, cap),
        [((owned, emb), bf16)],
        [SMEM, VMEM, VMEM],
        [pltpu.VMEM((n_req, emb), f32)] + [pltpu.VMEM((owned + 8, emb), f32)] * 8,
        "owner_grads",
        62,
        0,
        60 * MIB,
    )(
        asked,
        arrived_first.reshape(devices, 2 * cap, emb),
        arrived_last.reshape(devices, cap, emb),
    )

    parts, grad_inf = lax.optimization_barrier((parts, grad_inf))
    (spread,) = local_call(
        spread_kernel,
        [(parts.shape, bf16)],
        [VMEM],
        [],
        "spread",
        62,
        0,
        4 * MIB,
    )(parts)
    half = lax.all_to_all(
        spread, "dev", split_axis=0, concat_axis=0, axis_index_groups=same_core, tiled=True
    )
    half, dense = lax.optimization_barrier((half, dense))
    rest = lax.ppermute(half, "dev", other_core)
    full = (devices // 2, 2, per_freq, emb)
    (placed,) = local_call(
        functools.partial(place_kernel, 0),
        [(full, bf16)],
        [SMEM, HBM],
        [pltpu.SemaphoreType.DMA],
        "place_own",
        62,
        0,
        4 * MIB,
        [HBM],
    )(core, half)
    (placed,) = local_call(
        functools.partial(place_kernel, 1),
        [(full, bf16)],
        [SMEM, HBM, HBM],
        [pltpu.SemaphoreType.DMA],
        "place_other",
        62,
        0,
        4 * MIB,
        [HBM],
        {2: 0},
    )(core, rest, placed)
    grad_freq = placed.reshape(freq_rows, emb)

    grad_u = dense[:per, :rank]
    grad_v = dense[:per, rank:].T
    grad_b = dense[per, :per]
    grad_w = dense[per + 1, :per]
    return (grad_u, grad_v, grad_b, grad_w, grad_freq, grad_inf)


def solution(mesh):
    in_specs = (
        P(None, "dev", None),
        P(None, "dev"),
        P(None, "dev", None, None),
        P(None, "dev", None, None),
        P(None, "dev", None, None),
        P(),
        P("dev", None),
        P(),
        P(),
        P(),
        P(),
        P(),
    )
    out_specs = (P("dev", None), P(None, "dev"), P("dev"), P("dev"), P(), P("dev", None))
    return jax.shard_map(
        on_device, mesh=mesh, in_specs=in_specs, out_specs=out_specs, check_vma=False
    )
```

```python
import functools
import math

import jax
import jax.numpy as jnp
from jax import lax
from jax.experimental import pallas as pl
from jax.experimental.pallas import tpu as pltpu
from jax.sharding import PartitionSpec as P

loss_scale = 1024.0
f32 = jnp.float32
bf16 = jnp.bfloat16
MIB = 1024 * 1024
SMEM = pl.BlockSpec(memory_space=pltpu.SMEM)
VMEM = pl.BlockSpec(memory_space=pltpu.VMEM)
HBM = pl.BlockSpec(memory_space=pltpu.HBM)
NT = (((1,), (1,)), ((), ()))
TN = (((0,), (0,)), ((), ()))


def tree_sum(terms):
    while len(terms) > 1:
        terms = [sum(terms[k : k + 2][1:], terms[k]) for k in range(0, len(terms), 2)]
    return terms[0]


def local_call(
    kernel, outs, in_specs, scratch, name, limit, flops, bytes_accessed, out_specs=None, aliases={}
):
    return pl.pallas_call(
        kernel,
        out_shape=[jax.ShapeDtypeStruct(s, d) for s, d in outs],
        in_specs=in_specs,
        out_specs=out_specs or [VMEM] * len(outs),
        scratch_shapes=scratch,
        compiler_params=pltpu.CompilerParams(vmem_limit_bytes=limit * MIB),
        cost_estimate=pl.CostEstimate(
            flops=flops, bytes_accessed=bytes_accessed, transcendentals=0
        ),
        input_output_aliases=aliases,
        name=name,
    )


def freq_kernel(blocks, samples, first_micro, ids, table_ref, *refs):
    *outs, table, low, sems = refs
    pieces = sems.shape[0]
    size = table.shape[0] // pieces
    loads = []
    for k in range(pieces):
        at = pl.ds(k * size, size)
        loads.append(pltpu.make_async_copy(table_ref.at[at, :], low.at[at, :], sems.at[k]))
        loads[k].start()
    for k in range(pieces):
        at = slice(k * size, (k + 1) * size)
        loads[k].wait()
        table[at, :] = low[at, :].astype(f32)
    unroll = 64
    for m, out in enumerate(outs):
        start = (first_micro + m) * blocks * 2 * samples

        def group(g, carry):
            def some(k, carry):
                for u in range(unroll):
                    s = k * unroll + u
                    first = ids[start + g * 2 * samples + s]
                    second = ids[start + g * 2 * samples + samples + s]
                    out[pl.ds(g * samples + s, 1), :] = (
                        table[pl.ds(first, 1), :] + table[pl.ds(second, 1), :]
                    )
                return carry

            return lax.fori_loop(0, samples // unroll, some, carry)

        lax.fori_loop(0, blocks, group, 0)


def lookup_kernel(peers, stride, start, cap, asked, table_ref, out, table, rows):
    table[...] = table_ref[...].astype(f32)

    def peer(d, carry):
        for c in range(cap):
            r = asked[d * stride + start + c]
            rows[pl.ds(d * cap + c, 1), :] = table[pl.ds(r, 1), :]
        return carry

    lax.fori_loop(0, peers, peer, 0)
    out[...] = rows[...].astype(bf16)


def micro_kernel(
    peers,
    cap,
    features,
    m,
    slot_start,
    fetch_start,
    ret_start,
    loss_mult,
    slots,
    out_b,
    fetched_hbm,
    freq_part_hbm,
    bottom,
    labels,
    cross_u_hbm,
    cross_v_hbm,
    bias,
    weight,
    *refs,
):
    (
        returned_hbm,
        d_pooled_hbm,
        x_zero_hbm,
        hidden_hbm,
        d_hidden_hbm,
        gate_low_hbm,
        grad_bw,
        arrived,
        *accs,
        gate,
        returned,
        x_zero,
        hidden_out,
        d_hidden_out,
        gate_low,
        cross_u,
        cross_v,
        sems,
    ) = refs[-25:]
    acc0 = accs[0]
    samples, width = x_zero.shape
    emb = bottom.shape[2]
    n_slots = features * samples
    ways = len(accs)
    loads = [
        pltpu.make_async_copy(
            fetched_hbm.at[:, pl.ds(fetch_start, cap), :], returned, sems.at[6]
        ),
        pltpu.make_async_copy(freq_part_hbm, acc0.at[pl.ds(0, n_slots), :], sems.at[7]),
        pltpu.make_async_copy(cross_u_hbm, cross_u, sems.at[8]),
        pltpu.make_async_copy(cross_v_hbm, cross_v, sems.at[9]),
    ]
    for load in loads:
        load.start()
    for a in accs[1:]:
        a[...] = jnp.zeros_like(a)
    acc0[n_slots:, :] = jnp.zeros((acc0.shape[0] - n_slots, emb), f32)
    loads[0].wait()
    arrived[...] = returned[...].astype(f32).reshape(peers * cap, emb)
    loads[1].wait()

    def add_peer(o, carry):
        for c in range(0, cap, ways):
            at = [slots[slot_start + (c + j) * peers + o] for j in range(ways)]
            new = [
                accs[j][pl.ds(at[j], 1), :] + arrived[pl.ds(o * cap + c + j, 1), :]
                for j in range(ways)
            ]
            for j in range(ways):
                accs[j][pl.ds(at[j], 1), :] = new[j]
        return carry

    lax.fori_loop(0, peers, add_peer, 0)

    x_zero[:, 0:emb] = bottom[m]
    for f in range(features):
        rows = pl.ds(f * samples, samples)
        total = tree_sum([a[rows, :] for a in accs])
        x_zero[:, (f + 1) * emb : (f + 2) * emb] = total.astype(bf16)

    loads[2].wait()
    loads[3].wait()
    hidden = jnp.dot(x_zero[...], cross_u[...], preferred_element_type=f32).astype(bf16)
    hidden_out[...] = hidden
    copies = [
        pltpu.make_async_copy(x_zero, x_zero_hbm, sems.at[0]),
        pltpu.make_async_copy(hidden_out, hidden_hbm, sems.at[1]),
    ]
    for copy in copies:
        copy.start()
    chunk = 3 * emb
    chunks = width // chunk
    partial = jnp.zeros((samples, emb), f32)
    for k in range(chunks):
        cols = slice(k * chunk, (k + 1) * chunk)
        value = jnp.dot(hidden, cross_v[:, cols], preferred_element_type=f32) + bias[:, cols]
        gate[:, cols] = value
        x_float = x_zero[:, cols].astype(f32)
        scored = (x_float * value + x_float) * weight[:, cols]
        for j in range(3):
            partial = partial + scored[:, j * emb : (j + 1) * emb]
    logits = jnp.sum(partial, axis=1, keepdims=True) + out_b[0]
    square = (samples, samples)
    diagonal = lax.broadcasted_iota(jnp.int32, square, 0) == lax.broadcasted_iota(
        jnp.int32, square, 1
    )
    label = jnp.sum(jnp.where(diagonal, labels[m : m + 1, :], 0.0), axis=1, keepdims=True)
    d_logit = (jax.nn.sigmoid(logits) - label) * loss_mult
    for k in range(chunks):
        cols = slice(k * chunk, (k + 1) * chunk)
        x_float = x_zero[:, cols].astype(f32)
        d_gate = (d_logit * weight[:, cols]) * x_float
        gate_low[:, cols] = d_gate.astype(bf16)
        crossed = x_float * gate[:, cols] + x_float
        grad_bw[0:1, cols] = jnp.sum(d_gate, axis=0, keepdims=True)
        grad_bw[1:2, cols] = jnp.sum(d_logit * crossed, axis=0, keepdims=True)
    d_hidden = lax.dot_general(
        gate_low[...], cross_v[...], NT, preferred_element_type=f32
    ).astype(bf16)
    d_hidden_out[...] = d_hidden
    later = [
        pltpu.make_async_copy(gate_low, gate_low_hbm, sems.at[2]),
        pltpu.make_async_copy(d_hidden_out, d_hidden_hbm, sems.at[3]),
    ]
    for copy in later:
        copy.start()
    for k in range(chunks):
        cols = slice(k * chunk, (k + 1) * chunk)
        back = lax.dot_general(d_hidden, cross_u[cols, :], NT, preferred_element_type=f32)
        d_input = (d_logit * weight[:, cols]) * (gate[:, cols] + 1.0) + back
        for j in range(3):
            f = 3 * k + j - 1
            if f >= 0:
                acc0[f * samples : (f + 1) * samples, :] = d_input[:, j * emb : (j + 1) * emb]
    acc0[n_slots:, :] = jnp.zeros((acc0.shape[0] - n_slots, emb), f32)
    pooled_copy = pltpu.make_async_copy(acc0.at[pl.ds(0, n_slots), :], d_pooled_hbm, sems.at[4])
    pooled_copy.start()

    def take_peer(o, carry):
        for c in range(cap):
            at = slots[slot_start + c * peers + o]
            arrived[pl.ds(o * cap + c, 1), :] = acc0[pl.ds(at, 1), :]
        return carry

    lax.fori_loop(0, peers, take_peer, 0)
    returned[...] = arrived[...].astype(bf16).reshape(peers, cap, emb)
    returned_copy = pltpu.make_async_copy(
        returned, returned_hbm.at[:, pl.ds(ret_start, cap), :], sems.at[5]
    )
    returned_copy.start()
    for copy in copies + later:
        copy.wait()
    pooled_copy.wait()
    returned_copy.wait()


def dense_grad_kernel(
    peers, per, columns, x0, x1, x2, g0, g1, g2, h0, h1, h2, e0, e1, e2, parts_hbm, total, parts, sem
):
    width = x0.shape[1]
    rank = h0.shape[1]
    chunk = 128
    h_all = jnp.concatenate([h0[...], h1[...], h2[...]], axis=0)
    e_all = jnp.concatenate([e0[...], e1[...], e2[...]], axis=0)
    for k in range(width // chunk):
        cols = slice(k * chunk, (k + 1) * chunk)
        x_all = jnp.concatenate([x0[:, cols], x1[:, cols], x2[:, cols]], axis=0)
        g_all = jnp.concatenate([g0[:, cols], g1[:, cols], g2[:, cols]], axis=0)
        total[cols, 0:rank] = lax.dot_general(x_all, e_all, TN, preferred_element_type=f32)
        total[cols, rank : 2 * rank] = lax.dot_general(
            g_all, h_all, TN, preferred_element_type=f32
        )
    total[width:, :] = jnp.zeros((total.shape[0] - width, 2 * rank), f32)
    rows = parts.shape[2]
    spare = lax.broadcasted_iota(jnp.int32, (16, 128), 0) >= per - 16

    def blocks(q, carry):
        base = q * 8 * per
        for i in range(8):
            skip = i * per % 8
            window = total[pl.ds(pl.multiple_of(base + (i * per - skip), 8), rows + 8), :]
            value = window[skip : skip + rows]
            parts[q, i, 0:16, :] = value[0:16].astype(bf16)
            parts[q, i, 16:32, 128:] = value[16:32, 128:].astype(bf16)
            parts[q, i, 16:32, 0:128] = jnp.where(
                spare, columns[q * 8 + i], value[16:32, 0:128]
            ).astype(bf16)
        pltpu.make_async_copy(
            parts.at[q], parts_hbm.at[:, q % 4 * 4 + q // 4], sem.at[q]
        ).start()
        return carry

    lax.fori_loop(0, peers // 8, blocks, 0)

    def ends(q, carry):
        pltpu.make_async_copy(
            parts.at[q], parts_hbm.at[:, q % 4 * 4 + q // 4], sem.at[q]
        ).wait()
        return carry

    lax.fori_loop(0, peers // 8, ends, 0)


def freq_grad_kernel(
    features, core, ids, d0, d1, d2, keep, send, *scratch
):
    *accs, buf0, buf1, buf2, sems = scratch
    pairs = len(accs) // 2
    samples = d0.shape[0] // features
    loads = [
        pltpu.make_async_copy(d, buf, sems.at[k])
        for k, (d, buf) in enumerate(((d0, buf0), (d1, buf1), (d2, buf2)))
    ]
    for load in loads:
        load.start()
    for a in accs:
        a[...] = jnp.zeros_like(a)
    for m, source in enumerate((buf0, buf1, buf2)):
        loads[m].wait()
        start = m * features * 2 * samples

        def feature(f, carry):
            base = f * samples
            first = start + f * 2 * samples
            for s in range(0, samples, pairs):
                count = min(pairs, samples - s)
                at = [
                    ids[first + h * samples + s + j] for j in range(count) for h in range(2)
                ]
                value = [source[pl.ds(base + s + j, 1), :] for j in range(count)]
                new = [accs[j][pl.ds(at[j], 1), :] + value[j // 2] for j in range(2 * count)]
                for j in range(2 * count):
                    accs[j][pl.ds(at[j], 1), :] = new[j]
            return carry

        lax.fori_loop(0, features, feature, 0)
    rows = 128
    mine = core[0]

    def block(q, carry):
        for ref, parity in ((keep, mine), (send, 1 - mine)):
            at = pl.ds(pl.multiple_of((2 * q + parity) * rows, rows), rows)
            ref[q] = tree_sum([a[at, :] for a in accs]).astype(bf16)
        return carry

    lax.fori_loop(0, keep.shape[0], block, 0)


def spread_kernel(parts, out):
    total = parts[0].astype(f32)
    for k in range(1, parts.shape[0]):
        total = total + parts[k].astype(f32)
    total = total.astype(bf16)
    for k in range(parts.shape[0]):
        out[k] = total


def place_kernel(other, core, half, *refs):
    out, sem = refs[-2:]
    at = core[0] if other == 0 else 1 - core[0]
    copy = pltpu.make_async_copy(half, out.at[:, at], sem)
    copy.start()
    copy.wait()


def owner_kernel(peers, stride, cap, asked, first, last, out, rows, *accs):
    ways = len(accs)
    for a in accs:
        a[...] = jnp.zeros_like(a)
    emb = out.shape[1]
    for m in range(3):
        part = last[...] if m == 2 else first[:, m * cap : (m + 1) * cap, :]
        rows[...] = part.astype(f32).reshape(peers * cap, emb)

        def peer(d, carry):
            for c in range(0, cap, ways):
                at = [asked[d * stride + m * cap + c + j] for j in range(ways)]
                new = [
                    accs[j][pl.ds(at[j], 1), :] + rows[pl.ds(d * cap + c + j, 1), :]
                    for j in range(ways)
                ]
                for j in range(ways):
                    accs[j][pl.ds(at[j], 1), :] = new[j]
            return carry

        lax.fori_loop(0, peers, peer, 0)
    at = slice(0, out.shape[0])
    out[...] = tree_sum([a[at, :] for a in accs]).astype(bf16)


def on_device(
    bottom,
    labels,
    freq_ids,
    req_rows,
    req_slot,
    freq_table,
    inf_table,
    cross_u,
    cross_v,
    cross_bias,
    out_w,
    out_b,
):
    devices = lax.axis_size("dev")
    micro, samples, emb = bottom.shape
    features = freq_ids.shape[2]
    hot = freq_ids.shape[3]
    owned = inf_table.shape[0]
    cap = req_rows.shape[3]
    width, rank = cross_u.shape
    freq_rows = freq_table.shape[0]
    n_slots = samples * features
    n_req = devices * cap
    per = width // devices
    loss_mult = loss_scale / math.sqrt(micro * samples * devices)
    me = lax.axis_index("dev")
    core = (me % 2).astype(jnp.int32).reshape(1)
    other_core = [(d, d ^ 1) for d in range(devices)]
    same_core = [list(range(c, devices, 2)) for c in range(2)]

    ids = jnp.transpose(freq_ids, (0, 2, 3, 1)).reshape(-1)
    rows_mc = jnp.transpose(req_rows[:, 0], (0, 2, 1))
    slot_mc = jnp.transpose(req_slot[:, 0], (0, 2, 1))
    is_live = (rows_mc < owned) & (slot_mc < n_slots)
    place = jnp.where(
        is_live, (slot_mc % features) * samples + slot_mc // features, n_slots
    ).reshape(-1)
    line = jnp.where(
        (req_rows < owned) & (req_slot < n_slots), req_rows, owned
    )[:, 0]
    line = jnp.transpose(line, (1, 0, 2)).reshape(devices, micro * cap)
    stride = -(-micro * cap // 128) * 128
    line = jnp.pad(line, ((0, 0), (0, stride - micro * cap)), constant_values=owned)
    asked = lax.all_to_all(line, "dev", split_axis=0, concat_axis=0, tiled=True).reshape(-1)

    def freq_rows_of(first_micro, count):
        return local_call(
            functools.partial(freq_kernel, features, samples, first_micro),
            [((n_slots, emb), f32)] * count,
            [SMEM, HBM],
            [
                pltpu.VMEM((freq_rows, emb), f32),
                pltpu.VMEM((freq_rows, emb), bf16),
                pltpu.SemaphoreType.DMA((8,)),
            ],
            f"freq_rows{first_micro}",
            62,
            0,
            (12 + 14 * count) * MIB,
        )(ids, freq_table)

    freq_part = list(freq_rows_of(0, 1))
    asked, freq_part[0] = lax.optimization_barrier((asked, freq_part[0]))
    asked_row = jnp.minimum(asked, owned - 1)
    weight = out_w.astype(f32).reshape(1, width)
    bias = cross_bias.reshape(1, width)
    label_rows = labels.astype(f32)
    bias_b = out_b.reshape(1)

    def axis_sum(blocks, step):
        at = me // step % 4
        total = lax.dynamic_index_in_dim(blocks, at, 0, keepdims=False).astype(f32)
        for k in range(1, 4):
            block = lax.dynamic_index_in_dim(blocks, (at + k) % 4, 0, keepdims=False)
            to = [(d, d + ((d // step % 4 + k) % 4 - d // step % 4) * step) for d in range(devices)]
            total = total + lax.ppermute(block, "dev", to).astype(f32)
        return total

    def exchange(rows, count):
        return lax.all_to_all(
            rows.reshape(devices, count, emb), "dev", split_axis=0, concat_axis=0, tiled=True
        ).reshape(n_req * count // cap, emb)

    outs = []

    def lookup(start, count):
        return local_call(
            functools.partial(lookup_kernel, devices, stride, start, count),
            [((devices * count, emb), bf16)],
            [SMEM, VMEM],
            [pltpu.VMEM((owned, emb), f32), pltpu.VMEM((devices * count, emb), f32)],
            f"lookup{start}",
            62,
            0,
            count * MIB * 5 // 8,
        )(asked_row, inf_table)[0]

    looked = lookup(0, cap)
    asked_row, looked = lax.optimization_barrier((asked_row, looked))
    looked_rest = lookup(cap, (micro - 1) * cap)
    fetched = exchange(looked, cap)
    ids, looked_rest = lax.optimization_barrier((ids, looked_rest))
    freq_part += freq_rows_of(1, 1)
    small = (place, weight, bias, label_rows, bias_b)
    looked_rest, fetched, freq_part[1], small = lax.optimization_barrier(
        (looked_rest, fetched, freq_part[1], small)
    )
    place, weight, bias, label_rows, bias_b = small
    fetched_rest = exchange(looked_rest, (micro - 1) * cap)
    ids, freq_part[1] = lax.optimization_barrier((ids, freq_part[1]))
    freq_part += freq_rows_of(2, 1)
    for m in range(micro):
        if m == 1:
            fetched_rest, outs[0][6], freq_part[2] = lax.optimization_barrier(
                (fetched_rest, outs[0][6], freq_part[2])
            )
        out = local_call(
            functools.partial(
                micro_kernel,
                devices,
                cap,
                features,
                m,
                m * n_req,
                max(m - 1, 0) * cap,
                cap if m == 1 else 0,
                loss_mult,
            ),
            [
                ((devices, cap if m == 2 else 2 * cap, emb), bf16),
                ((n_slots, emb), f32),
                ((samples, width), bf16),
                ((samples, rank), bf16),
                ((samples, rank), bf16),
                ((samples, width), bf16),
                ((2, width), f32),
            ],
            [SMEM, SMEM, HBM, HBM, VMEM, VMEM, HBM, HBM, VMEM, VMEM] + ([HBM] if m == 1 else []),
            [pltpu.VMEM((n_req, emb), f32)]
            + [pltpu.VMEM((n_slots + 8, emb), f32)] * 8
            + [pltpu.VMEM((samples, width), f32)]
            + [pltpu.VMEM((devices, cap, emb), bf16), pltpu.VMEM((samples, width), bf16)]
            + [pltpu.VMEM((samples, rank), bf16)] * 2
            + [pltpu.VMEM((samples, width), bf16)]
            + [pltpu.VMEM((width, rank), bf16), pltpu.VMEM((rank, width), bf16)]
            + [pltpu.SemaphoreType.DMA((10,))],
            f"micro{m}",
            62,
            6 * samples * width * rank,
            60 * MIB,
            [HBM] * 6 + [VMEM],
            {10: 0} if m == 1 else {},
        )(
            place,
            bias_b,
            (fetched_rest if m else fetched).reshape(devices, -1, emb),
            freq_part[m],
            bottom,
            label_rows,
            cross_u,
            cross_v,
            bias,
            weight,
            *([outs[0][0]] if m == 1 else []),
        )
        outs.append(list(out))
        if m == 1:
            place, outs[1][6] = lax.optimization_barrier((place, outs[1][6]))
    arrived_first = exchange(outs[1][0], 2 * cap)
    outs[2][0], arrived_first = lax.optimization_barrier((outs[2][0], arrived_first))
    arrived_last = exchange(outs[2][0], cap)
    d_pooled = [o[1] for o in outs]
    grad_bw = ((outs[0][6] + outs[1][6]) + outs[2][6]).reshape(2, devices, per)
    columns = jnp.pad(
        jnp.transpose(grad_bw, (1, 0, 2)), ((0, 0), (per - 16, 30 - per), (0, 128 - per))
    )

    rows_pad = -(-per // 16) * 16
    per_freq = freq_rows // devices
    (dense,) = local_call(
        functools.partial(dense_grad_kernel, devices, per),
        [((8, devices // 8, rows_pad, 2 * rank), bf16)],
        [VMEM] * 13,
        [
            pltpu.VMEM((width + 16, 2 * rank), f32),
            pltpu.VMEM((devices // 8, 8, rows_pad, 2 * rank), bf16),
            pltpu.SemaphoreType.DMA((devices // 8,)),
        ],
        "dense_grads",
        62,
        12 * samples * width * rank,
        40 * MIB,
        [HBM],
    )(
        columns,
        *[o[2] for o in outs],
        *[o[5] for o in outs],
        *[o[3] for o in outs],
        *[o[4] for o in outs],
    )
    core, dense, arrived_first = lax.optimization_barrier((core, dense, arrived_first))
    dense = dense.reshape(devices, rows_pad, 2 * rank)
    near = [list(range(d, d + 8)) for d in range(0, devices, 8)]
    dense = lax.psum_scatter(dense, "dev", axis_index_groups=near, tiled=True)
    dense = axis_sum(dense.reshape(4, 4, rows_pad, 2 * rank), 8).astype(bf16)
    dense = axis_sum(dense, 32)
    keep_f, send_f = local_call(
        functools.partial(freq_grad_kernel, features),
        [((devices // 2, per_freq, emb), bf16)] * 2,
        [SMEM, SMEM] + [HBM] * 3,
        [pltpu.VMEM((freq_rows, emb), f32)] * 6
        + [pltpu.VMEM((n_slots, emb), f32)] * 3
        + [pltpu.SemaphoreType.DMA((3,))],
        "freq_grads",
        62,
        0,
        120 * MIB,
    )(core, ids, *d_pooled)
    send_f, arrived_last = lax.optimization_barrier((send_f, arrived_last))
    got = lax.ppermute(send_f, "dev", other_core)
    both = (keep_f.astype(f32) + got.astype(f32)).astype(bf16)
    parts = lax.all_to_all(
        both, "dev", split_axis=0, concat_axis=0, axis_index_groups=same_core, tiled=True
    )
    (grad_inf,) = local_call(
        functools.partial(owner_kernel, devices, stride, cap),
        [((owned, emb), bf16)],
        [SMEM, VMEM, VMEM],
        [pltpu.VMEM((n_req, emb), f32)] + [pltpu.VMEM((owned + 8, emb), f32)] * 8,
        "owner_grads",
        62,
        0,
        60 * MIB,
    )(
        asked,
        arrived_first.reshape(devices, 2 * cap, emb),
        arrived_last.reshape(devices, cap, emb),
    )

    parts, grad_inf = lax.optimization_barrier((parts, grad_inf))
    (spread,) = local_call(
        spread_kernel,
        [(parts.shape, bf16)],
        [VMEM],
        [],
        "spread",
        62,
        0,
        4 * MIB,
    )(parts)
    half = lax.all_to_all(
        spread, "dev", split_axis=0, concat_axis=0, axis_index_groups=same_core, tiled=True
    )
    half, dense = lax.optimization_barrier((half, dense))
    rest = lax.ppermute(half, "dev", other_core)
    full = (devices // 2, 2, per_freq, emb)
    (placed,) = local_call(
        functools.partial(place_kernel, 0),
        [(full, bf16)],
        [SMEM, VMEM],
        [pltpu.SemaphoreType.DMA],
        "place_own",
        40,
        0,
        4 * MIB,
        [HBM],
    )(core, half)
    (placed,) = local_call(
        functools.partial(place_kernel, 1),
        [(full, bf16)],
        [SMEM, VMEM, HBM],
        [pltpu.SemaphoreType.DMA],
        "place_other",
        40,
        0,
        4 * MIB,
        [HBM],
        {2: 0},
    )(core, rest, placed)
    grad_freq = placed.reshape(freq_rows, emb)

    grad_u = dense[:per, :rank]
    grad_v = dense[:per, rank:].T
    grad_b = dense[per, :per]
    grad_w = dense[per + 1, :per]
    return (grad_u, grad_v, grad_b, grad_w, grad_freq, grad_inf)


def solution(mesh):
    in_specs = (
        P(None, "dev", None),
        P(None, "dev"),
        P(None, "dev", None, None),
        P(None, "dev", None, None),
        P(None, "dev", None, None),
        P(),
        P("dev", None),
        P(),
        P(),
        P(),
        P(),
        P(),
    )
    out_specs = (P("dev", None), P(None, "dev"), P("dev"), P("dev"), P(), P("dev", None))
    return jax.shard_map(
        on_device, mesh=mesh, in_specs=in_specs, out_specs=out_specs, check_vma=False
    )
```

```python
import functools
import math

import jax
import jax.numpy as jnp
from jax import lax
from jax.experimental import pallas as pl
from jax.experimental.pallas import tpu as pltpu
from jax.sharding import PartitionSpec as P

loss_scale = 1024.0
f32 = jnp.float32
bf16 = jnp.bfloat16
MIB = 1024 * 1024
SMEM = pl.BlockSpec(memory_space=pltpu.SMEM)
VMEM = pl.BlockSpec(memory_space=pltpu.VMEM)
HBM = pl.BlockSpec(memory_space=pltpu.HBM)
NT = (((1,), (1,)), ((), ()))
TN = (((0,), (0,)), ((), ()))


def tree_sum(terms):
    while len(terms) > 1:
        terms = [sum(terms[k : k + 2][1:], terms[k]) for k in range(0, len(terms), 2)]
    return terms[0]


def local_call(
    kernel, outs, in_specs, scratch, name, limit, flops, bytes_accessed, out_specs=None, aliases={}
):
    return pl.pallas_call(
        kernel,
        out_shape=[jax.ShapeDtypeStruct(s, d) for s, d in outs],
        in_specs=in_specs,
        out_specs=out_specs or [VMEM] * len(outs),
        scratch_shapes=scratch,
        compiler_params=pltpu.CompilerParams(vmem_limit_bytes=limit * MIB),
        cost_estimate=pl.CostEstimate(
            flops=flops, bytes_accessed=bytes_accessed, transcendentals=0
        ),
        input_output_aliases=aliases,
        name=name,
    )


def freq_kernel(blocks, samples, first_micro, ids, table_ref, *refs):
    *outs, table = refs
    table[...] = table_ref[...].astype(f32)
    unroll = 32
    for m, out in enumerate(outs):
        start = (first_micro + m) * blocks * 2 * samples

        def group(g, carry):
            def some(k, carry):
                for u in range(unroll):
                    s = k * unroll + u
                    first = ids[start + g * 2 * samples + s]
                    second = ids[start + g * 2 * samples + samples + s]
                    out[pl.ds(g * samples + s, 1), :] = (
                        table[pl.ds(first, 1), :] + table[pl.ds(second, 1), :]
                    )
                return carry

            return lax.fori_loop(0, samples // unroll, some, carry)

        lax.fori_loop(0, blocks, group, 0)


def lookup_kernel(peers, stride, start, cap, asked, table_ref, out, table, rows):
    table[...] = table_ref[...].astype(f32)

    def peer(d, carry):
        for c in range(cap):
            r = asked[d * stride + start + c]
            rows[pl.ds(d * cap + c, 1), :] = table[pl.ds(r, 1), :]
        return carry

    lax.fori_loop(0, peers, peer, 0)
    out[...] = rows[...].astype(bf16)


def micro_kernel(
    peers,
    cap,
    features,
    m,
    slot_start,
    fetch_start,
    ret_start,
    loss_mult,
    slots,
    out_b,
    fetched_hbm,
    freq_part_hbm,
    bottom,
    labels,
    cross_u_hbm,
    cross_v_hbm,
    bias,
    weight,
    *refs,
):
    (
        returned_hbm,
        d_pooled_hbm,
        x_zero_hbm,
        hidden_hbm,
        d_hidden_hbm,
        gate_low_hbm,
        grad_bw,
        arrived,
        *accs,
        gate,
        returned,
        x_zero,
        hidden_out,
        d_hidden_out,
        gate_low,
        cross_u,
        cross_v,
        sems,
    ) = refs[-25:]
    acc0 = accs[0]
    samples, width = x_zero.shape
    emb = bottom.shape[2]
    n_slots = features * samples
    ways = len(accs)
    loads = [
        pltpu.make_async_copy(
            fetched_hbm.at[:, pl.ds(fetch_start, cap), :], returned, sems.at[6]
        ),
        pltpu.make_async_copy(freq_part_hbm, acc0.at[pl.ds(0, n_slots), :], sems.at[7]),
        pltpu.make_async_copy(cross_u_hbm, cross_u, sems.at[8]),
        pltpu.make_async_copy(cross_v_hbm, cross_v, sems.at[9]),
    ]
    for load in loads:
        load.start()
    for a in accs[1:]:
        a[...] = jnp.zeros_like(a)
    acc0[n_slots:, :] = jnp.zeros((acc0.shape[0] - n_slots, emb), f32)
    loads[0].wait()
    arrived[...] = returned[...].astype(f32).reshape(peers * cap, emb)
    loads[1].wait()

    def add_peer(o, carry):
        for c in range(0, cap, ways):
            at = [slots[slot_start + (c + j) * peers + o] for j in range(ways)]
            new = [
                accs[j][pl.ds(at[j], 1), :] + arrived[pl.ds(o * cap + c + j, 1), :]
                for j in range(ways)
            ]
            for j in range(ways):
                accs[j][pl.ds(at[j], 1), :] = new[j]
        return carry

    lax.fori_loop(0, peers, add_peer, 0)

    x_zero[:, 0:emb] = bottom[m]
    for f in range(features):
        rows = pl.ds(f * samples, samples)
        total = tree_sum([a[rows, :] for a in accs])
        x_zero[:, (f + 1) * emb : (f + 2) * emb] = total.astype(bf16)

    loads[2].wait()
    loads[3].wait()
    hidden = jnp.dot(x_zero[...], cross_u[...], preferred_element_type=f32).astype(bf16)
    hidden_out[...] = hidden
    copies = [
        pltpu.make_async_copy(x_zero, x_zero_hbm, sems.at[0]),
        pltpu.make_async_copy(hidden_out, hidden_hbm, sems.at[1]),
    ]
    for copy in copies:
        copy.start()
    chunk = 3 * emb
    chunks = width // chunk
    partial = jnp.zeros((samples, emb), f32)
    for k in range(chunks):
        cols = slice(k * chunk, (k + 1) * chunk)
        value = jnp.dot(hidden, cross_v[:, cols], preferred_element_type=f32) + bias[:, cols]
        gate[:, cols] = value
        x_float = x_zero[:, cols].astype(f32)
        scored = (x_float * value + x_float) * weight[:, cols]
        for j in range(3):
            partial = partial + scored[:, j * emb : (j + 1) * emb]
    logits = jnp.sum(partial, axis=1, keepdims=True) + out_b[0]
    square = (samples, samples)
    diagonal = lax.broadcasted_iota(jnp.int32, square, 0) == lax.broadcasted_iota(
        jnp.int32, square, 1
    )
    label = jnp.sum(jnp.where(diagonal, labels[m : m + 1, :], 0.0), axis=1, keepdims=True)
    d_logit = (jax.nn.sigmoid(logits) - label) * loss_mult
    for k in range(chunks):
        cols = slice(k * chunk, (k + 1) * chunk)
        x_float = x_zero[:, cols].astype(f32)
        d_gate = (d_logit * weight[:, cols]) * x_float
        gate_low[:, cols] = d_gate.astype(bf16)
        crossed = x_float * gate[:, cols] + x_float
        grad_bw[0:1, cols] = jnp.sum(d_gate, axis=0, keepdims=True)
        grad_bw[1:2, cols] = jnp.sum(d_logit * crossed, axis=0, keepdims=True)
    d_hidden = lax.dot_general(
        gate_low[...], cross_v[...], NT, preferred_element_type=f32
    ).astype(bf16)
    d_hidden_out[...] = d_hidden
    later = [
        pltpu.make_async_copy(gate_low, gate_low_hbm, sems.at[2]),
        pltpu.make_async_copy(d_hidden_out, d_hidden_hbm, sems.at[3]),
    ]
    for copy in later:
        copy.start()
    for k in range(chunks):
        cols = slice(k * chunk, (k + 1) * chunk)
        back = lax.dot_general(d_hidden, cross_u[cols, :], NT, preferred_element_type=f32)
        d_input = (d_logit * weight[:, cols]) * (gate[:, cols] + 1.0) + back
        for j in range(3):
            f = 3 * k + j - 1
            if f >= 0:
                acc0[f * samples : (f + 1) * samples, :] = d_input[:, j * emb : (j + 1) * emb]
    acc0[n_slots:, :] = jnp.zeros((acc0.shape[0] - n_slots, emb), f32)
    pooled_copy = pltpu.make_async_copy(acc0.at[pl.ds(0, n_slots), :], d_pooled_hbm, sems.at[4])
    pooled_copy.start()

    def take_peer(o, carry):
        for c in range(cap):
            at = slots[slot_start + c * peers + o]
            arrived[pl.ds(o * cap + c, 1), :] = acc0[pl.ds(at, 1), :]
        return carry

    lax.fori_loop(0, peers, take_peer, 0)
    returned[...] = arrived[...].astype(bf16).reshape(peers, cap, emb)
    returned_copy = pltpu.make_async_copy(
        returned, returned_hbm.at[:, pl.ds(ret_start, cap), :], sems.at[5]
    )
    returned_copy.start()
    for copy in copies + later:
        copy.wait()
    pooled_copy.wait()
    returned_copy.wait()


def dense_grad_kernel(
    peers, per, columns, x0, x1, x2, g0, g1, g2, h0, h1, h2, e0, e1, e2, parts_hbm, total, parts, sem
):
    width = x0.shape[1]
    rank = h0.shape[1]
    chunk = 128
    h_all = jnp.concatenate([h0[...], h1[...], h2[...]], axis=0)
    e_all = jnp.concatenate([e0[...], e1[...], e2[...]], axis=0)
    for k in range(width // chunk):
        cols = slice(k * chunk, (k + 1) * chunk)
        x_all = jnp.concatenate([x0[:, cols], x1[:, cols], x2[:, cols]], axis=0)
        g_all = jnp.concatenate([g0[:, cols], g1[:, cols], g2[:, cols]], axis=0)
        total[cols, 0:rank] = lax.dot_general(x_all, e_all, TN, preferred_element_type=f32)
        total[cols, rank : 2 * rank] = lax.dot_general(
            g_all, h_all, TN, preferred_element_type=f32
        )
    total[width:, :] = jnp.zeros((total.shape[0] - width, 2 * rank), f32)
    rows = parts.shape[2]
    spare = lax.broadcasted_iota(jnp.int32, (16, 128), 0) >= per - 16

    def blocks(q, carry):
        base = q * 8 * per
        for i in range(8):
            skip = i * per % 8
            window = total[pl.ds(pl.multiple_of(base + (i * per - skip), 8), rows + 8), :]
            value = window[skip : skip + rows]
            parts[q, i, 0:16, :] = value[0:16].astype(bf16)
            parts[q, i, 16:32, 128:] = value[16:32, 128:].astype(bf16)
            parts[q, i, 16:32, 0:128] = jnp.where(
                spare, columns[q * 8 + i], value[16:32, 0:128]
            ).astype(bf16)
        pltpu.make_async_copy(
            parts.at[q], parts_hbm.at[:, q % 4 * 4 + q // 4], sem.at[q]
        ).start()
        return carry

    lax.fori_loop(0, peers // 8, blocks, 0)

    def ends(q, carry):
        pltpu.make_async_copy(
            parts.at[q], parts_hbm.at[:, q % 4 * 4 + q // 4], sem.at[q]
        ).wait()
        return carry

    lax.fori_loop(0, peers // 8, ends, 0)


def freq_grad_kernel(
    features, core, ids, d0, d1, d2, keep, send, *scratch
):
    *accs, buf0, buf1, buf2, sems = scratch
    pairs = len(accs) // 2
    samples = d0.shape[0] // features
    loads = [
        pltpu.make_async_copy(d, buf, sems.at[k])
        for k, (d, buf) in enumerate(((d0, buf0), (d1, buf1), (d2, buf2)))
    ]
    for load in loads:
        load.start()
    for a in accs:
        a[...] = jnp.zeros_like(a)
    for m, source in enumerate((buf0, buf1, buf2)):
        loads[m].wait()
        start = m * features * 2 * samples

        def feature(f, carry):
            base = f * samples
            first = start + f * 2 * samples
            for s in range(0, samples, pairs):
                count = min(pairs, samples - s)
                at = [
                    ids[first + h * samples + s + j] for j in range(count) for h in range(2)
                ]
                value = [source[pl.ds(base + s + j, 1), :] for j in range(count)]
                new = [accs[j][pl.ds(at[j], 1), :] + value[j // 2] for j in range(2 * count)]
                for j in range(2 * count):
                    accs[j][pl.ds(at[j], 1), :] = new[j]
            return carry

        lax.fori_loop(0, features, feature, 0)
    rows = 128
    mine = core[0]

    def block(q, carry):
        for ref, parity in ((keep, mine), (send, 1 - mine)):
            at = pl.ds(pl.multiple_of(((q % 4 * 2 + parity) * 16 + q // 4) * rows, rows), rows)
            ref[q] = tree_sum([a[at, :] for a in accs]).astype(bf16)
        return carry

    lax.fori_loop(0, keep.shape[0], block, 0)


def spread_kernel(parts, out):
    total = parts[0].astype(f32)
    for k in range(1, parts.shape[0]):
        total = total + parts[k].astype(f32)
    total = total.astype(bf16)
    for k in range(out.shape[0]):
        out[k] = total


def owner_kernel(peers, stride, cap, asked, first, last, out, rows, *accs):
    ways = len(accs)
    for a in accs:
        a[...] = jnp.zeros_like(a)
    emb = out.shape[1]
    for m in range(3):
        part = last[...] if m == 2 else first[:, m * cap : (m + 1) * cap, :]
        rows[...] = part.astype(f32).reshape(peers * cap, emb)

        def peer(d, carry):
            for c in range(0, cap, ways):
                at = [asked[d * stride + m * cap + c + j] for j in range(ways)]
                new = [
                    accs[j][pl.ds(at[j], 1), :] + rows[pl.ds(d * cap + c + j, 1), :]
                    for j in range(ways)
                ]
                for j in range(ways):
                    accs[j][pl.ds(at[j], 1), :] = new[j]
            return carry

        lax.fori_loop(0, peers, peer, 0)
    at = slice(0, out.shape[0])
    out[...] = tree_sum([a[at, :] for a in accs]).astype(bf16)


def on_device(
    bottom,
    labels,
    freq_ids,
    req_rows,
    req_slot,
    freq_table,
    inf_table,
    cross_u,
    cross_v,
    cross_bias,
    out_w,
    out_b,
):
    devices = lax.axis_size("dev")
    micro, samples, emb = bottom.shape
    features = freq_ids.shape[2]
    hot = freq_ids.shape[3]
    owned = inf_table.shape[0]
    cap = req_rows.shape[3]
    width, rank = cross_u.shape
    freq_rows = freq_table.shape[0]
    n_slots = samples * features
    n_req = devices * cap
    per = width // devices
    loss_mult = loss_scale / math.sqrt(micro * samples * devices)
    me = lax.axis_index("dev")
    core = (me % 2).astype(jnp.int32).reshape(1)
    other_core = [(d, d ^ 1) for d in range(devices)]
    same_core = [list(range(c, devices, 2)) for c in range(2)]

    ids = jnp.transpose(freq_ids, (0, 2, 3, 1)).reshape(-1)
    rows_mc = jnp.transpose(req_rows[:, 0], (0, 2, 1))
    slot_mc = jnp.transpose(req_slot[:, 0], (0, 2, 1))
    is_live = (rows_mc < owned) & (slot_mc < n_slots)
    place = jnp.where(
        is_live, (slot_mc % features) * samples + slot_mc // features, n_slots
    ).reshape(-1)
    line = jnp.where(
        (req_rows < owned) & (req_slot < n_slots), req_rows, owned
    )[:, 0]
    line = jnp.transpose(line, (1, 0, 2)).reshape(devices, micro * cap)
    stride = -(-micro * cap // 128) * 128
    line = jnp.pad(line, ((0, 0), (0, stride - micro * cap)), constant_values=owned)
    asked = lax.all_to_all(line, "dev", split_axis=0, concat_axis=0, tiled=True).reshape(-1)

    def freq_rows_of(first_micro, count):
        return local_call(
            functools.partial(freq_kernel, features, samples, first_micro),
            [((n_slots, emb), f32)] * count,
            [SMEM, VMEM],
            [pltpu.VMEM((freq_rows, emb), f32)],
            f"freq_rows{first_micro}",
            62,
            0,
            (12 + 14 * count) * MIB,
        )(ids, freq_table)

    freq_part = list(freq_rows_of(0, 1))
    asked, freq_part[0] = lax.optimization_barrier((asked, freq_part[0]))
    asked_row = jnp.minimum(asked, owned - 1)
    weight = out_w.astype(f32).reshape(1, width)
    bias = cross_bias.reshape(1, width)
    label_rows = labels.astype(f32)
    bias_b = out_b.reshape(1)

    def axis_sum(blocks, step):
        at = me // step % 4
        total = lax.dynamic_index_in_dim(blocks, at, 0, keepdims=False).astype(f32)
        for k in range(1, 4):
            block = lax.dynamic_index_in_dim(blocks, (at + k) % 4, 0, keepdims=False)
            to = [(d, d + ((d // step % 4 + k) % 4 - d // step % 4) * step) for d in range(devices)]
            total = total + lax.ppermute(block, "dev", to).astype(f32)
        return total

    def exchange(rows, count):
        return lax.all_to_all(
            rows.reshape(devices, count, emb), "dev", split_axis=0, concat_axis=0, tiled=True
        ).reshape(n_req * count // cap, emb)

    outs = []

    def lookup(start, count):
        return local_call(
            functools.partial(lookup_kernel, devices, stride, start, count),
            [((devices * count, emb), bf16)],
            [SMEM, VMEM],
            [pltpu.VMEM((owned, emb), f32), pltpu.VMEM((devices * count, emb), f32)],
            f"lookup{start}",
            62,
            0,
            count * MIB * 5 // 8,
        )(asked_row, inf_table)[0]

    looked = lookup(0, cap)
    asked_row, looked = lax.optimization_barrier((asked_row, looked))
    looked_rest = lookup(cap, (micro - 1) * cap)
    fetched = exchange(looked, cap)
    ids, looked_rest = lax.optimization_barrier((ids, looked_rest))
    freq_part += freq_rows_of(1, 1)
    small = (place, weight, bias, label_rows, bias_b)
    looked_rest, fetched, freq_part[1], small = lax.optimization_barrier(
        (looked_rest, fetched, freq_part[1], small)
    )
    place, weight, bias, label_rows, bias_b = small
    fetched_rest = exchange(looked_rest, (micro - 1) * cap)
    ids, freq_part[1] = lax.optimization_barrier((ids, freq_part[1]))
    freq_part += freq_rows_of(2, 1)
    for m in range(micro):
        if m == 1:
            fetched_rest, outs[0][6], freq_part[2] = lax.optimization_barrier(
                (fetched_rest, outs[0][6], freq_part[2])
            )
        out = local_call(
            functools.partial(
                micro_kernel,
                devices,
                cap,
                features,
                m,
                m * n_req,
                max(m - 1, 0) * cap,
                cap if m == 1 else 0,
                loss_mult,
            ),
            [
                ((devices, cap if m == 2 else 2 * cap, emb), bf16),
                ((n_slots, emb), f32),
                ((samples, width), bf16),
                ((samples, rank), bf16),
                ((samples, rank), bf16),
                ((samples, width), bf16),
                ((2, width), f32),
            ],
            [SMEM, SMEM, HBM, HBM, VMEM, VMEM, HBM, HBM, VMEM, VMEM] + ([HBM] if m == 1 else []),
            [pltpu.VMEM((n_req, emb), f32)]
            + [pltpu.VMEM((n_slots + 8, emb), f32)] * 8
            + [pltpu.VMEM((samples, width), f32)]
            + [pltpu.VMEM((devices, cap, emb), bf16), pltpu.VMEM((samples, width), bf16)]
            + [pltpu.VMEM((samples, rank), bf16)] * 2
            + [pltpu.VMEM((samples, width), bf16)]
            + [pltpu.VMEM((width, rank), bf16), pltpu.VMEM((rank, width), bf16)]
            + [pltpu.SemaphoreType.DMA((10,))],
            f"micro{m}",
            62,
            6 * samples * width * rank,
            60 * MIB,
            [HBM] * 6 + [VMEM],
            {10: 0} if m == 1 else {},
        )(
            place,
            bias_b,
            (fetched_rest if m else fetched).reshape(devices, -1, emb),
            freq_part[m],
            bottom,
            label_rows,
            cross_u,
            cross_v,
            bias,
            weight,
            *([outs[0][0]] if m == 1 else []),
        )
        outs.append(list(out))
        if m == 1:
            place, outs[1][6] = lax.optimization_barrier((place, outs[1][6]))
    arrived_first = exchange(outs[1][0], 2 * cap)
    outs[2][0], arrived_first = lax.optimization_barrier((outs[2][0], arrived_first))
    arrived_last = exchange(outs[2][0], cap)
    d_pooled = [o[1] for o in outs]
    grad_bw = ((outs[0][6] + outs[1][6]) + outs[2][6]).reshape(2, devices, per)
    columns = jnp.pad(
        jnp.transpose(grad_bw, (1, 0, 2)), ((0, 0), (per - 16, 30 - per), (0, 128 - per))
    )

    rows_pad = -(-per // 16) * 16
    per_freq = freq_rows // devices
    (dense,) = local_call(
        functools.partial(dense_grad_kernel, devices, per),
        [((8, devices // 8, rows_pad, 2 * rank), bf16)],
        [VMEM] * 13,
        [
            pltpu.VMEM((width + 16, 2 * rank), f32),
            pltpu.VMEM((devices // 8, 8, rows_pad, 2 * rank), bf16),
            pltpu.SemaphoreType.DMA((devices // 8,)),
        ],
        "dense_grads",
        62,
        12 * samples * width * rank,
        40 * MIB,
        [HBM],
    )(
        columns,
        *[o[2] for o in outs],
        *[o[5] for o in outs],
        *[o[3] for o in outs],
        *[o[4] for o in outs],
    )
    core, dense, arrived_first = lax.optimization_barrier((core, dense, arrived_first))
    dense = dense.reshape(devices, rows_pad, 2 * rank)
    near = [list(range(d, d + 8)) for d in range(0, devices, 8)]
    dense = lax.psum_scatter(dense, "dev", axis_index_groups=near, tiled=True)
    keep_f, send_f = local_call(
        functools.partial(freq_grad_kernel, features),
        [((devices // 2, per_freq, emb), bf16)] * 2,
        [SMEM, SMEM] + [HBM] * 3,
        [pltpu.VMEM((freq_rows, emb), f32)] * 6
        + [pltpu.VMEM((n_slots, emb), f32)] * 3
        + [pltpu.SemaphoreType.DMA((3,))],
        "freq_grads",
        62,
        0,
        120 * MIB,
    )(core, ids, *d_pooled)
    send_f, arrived_last = lax.optimization_barrier((send_f, arrived_last))
    got = lax.ppermute(send_f, "dev", other_core)
    both = (keep_f.astype(f32) + got.astype(f32)).astype(bf16)
    parts = lax.all_to_all(
        both, "dev", split_axis=0, concat_axis=0, axis_index_groups=same_core, tiled=True
    )
    (grad_inf,) = local_call(
        functools.partial(owner_kernel, devices, stride, cap),
        [((owned, emb), bf16)],
        [SMEM, VMEM, VMEM],
        [pltpu.VMEM((n_req, emb), f32)] + [pltpu.VMEM((owned + 8, emb), f32)] * 8,
        "owner_grads",
        62,
        0,
        60 * MIB,
    )(
        asked,
        arrived_first.reshape(devices, 2 * cap, emb),
        arrived_last.reshape(devices, cap, emb),
    )

    parts, grad_inf = lax.optimization_barrier((parts, grad_inf))
    (spread,) = local_call(
        spread_kernel,
        [((devices // 8, per_freq, emb), bf16)],
        [VMEM],
        [],
        "spread",
        62,
        0,
        4 * MIB,
    )(parts)
    sixteen = lax.all_to_all(
        spread,
        "dev",
        split_axis=0,
        concat_axis=0,
        axis_index_groups=[list(range(k, devices, 8)) for k in range(8)],
        tiled=True,
    ).reshape(freq_rows // 8, emb)
    sixteen, dense = lax.optimization_barrier((sixteen, dense))
    grad_freq = lax.all_gather(sixteen, "dev", axis_index_groups=near, tiled=True)
    dense = axis_sum(dense.reshape(4, 4, rows_pad, 2 * rank), 8).astype(bf16)
    dense = axis_sum(dense, 32)
    grad_u = dense[:per, :rank]
    grad_v = dense[:per, rank:].T
    grad_b = dense[per, :per]
    grad_w = dense[per + 1, :per]
    return (grad_u, grad_v, grad_b, grad_w, grad_freq, grad_inf)


def solution(mesh):
    in_specs = (
        P(None, "dev", None),
        P(None, "dev"),
        P(None, "dev", None, None),
        P(None, "dev", None, None),
        P(None, "dev", None, None),
        P(),
        P("dev", None),
        P(),
        P(),
        P(),
        P(),
        P(),
    )
    out_specs = (P("dev", None), P(None, "dev"), P("dev"), P("dev"), P(), P("dev", None))
    return jax.shard_map(
        on_device, mesh=mesh, in_specs=in_specs, out_specs=out_specs, check_vma=False
    )
```

```python
import functools
import math

import jax
import jax.numpy as jnp
from jax import lax
from jax.experimental import pallas as pl
from jax.experimental.pallas import tpu as pltpu
from jax.sharding import PartitionSpec as P

loss_scale = 1024.0
f32 = jnp.float32
bf16 = jnp.bfloat16
MIB = 1024 * 1024
SMEM = pl.BlockSpec(memory_space=pltpu.SMEM)
VMEM = pl.BlockSpec(memory_space=pltpu.VMEM)
HBM = pl.BlockSpec(memory_space=pltpu.HBM)
NT = (((1,), (1,)), ((), ()))
TN = (((0,), (0,)), ((), ()))


def tree_sum(terms):
    while len(terms) > 1:
        terms = [sum(terms[k : k + 2][1:], terms[k]) for k in range(0, len(terms), 2)]
    return terms[0]


def local_call(
    kernel, outs, in_specs, scratch, name, limit, flops, bytes_accessed, out_specs=None, aliases={}
):
    return pl.pallas_call(
        kernel,
        out_shape=[jax.ShapeDtypeStruct(s, d) for s, d in outs],
        in_specs=in_specs,
        out_specs=out_specs or [VMEM] * len(outs),
        scratch_shapes=scratch,
        compiler_params=pltpu.CompilerParams(vmem_limit_bytes=limit * MIB),
        cost_estimate=pl.CostEstimate(
            flops=flops, bytes_accessed=bytes_accessed, transcendentals=0
        ),
        input_output_aliases=aliases,
        name=name,
    )


def freq_kernel(blocks, samples, first_micro, ids, table_ref, *refs):
    *outs, table = refs
    table[...] = table_ref[...].astype(f32)
    unroll = 32
    for m, out in enumerate(outs):
        start = (first_micro + m) * blocks * 2 * samples

        def group(g, carry):
            def some(k, carry):
                for u in range(unroll):
                    s = k * unroll + u
                    first = ids[start + g * 2 * samples + s]
                    second = ids[start + g * 2 * samples + samples + s]
                    out[pl.ds(g * samples + s, 1), :] = (
                        table[pl.ds(first, 1), :] + table[pl.ds(second, 1), :]
                    )
                return carry

            return lax.fori_loop(0, samples // unroll, some, carry)

        lax.fori_loop(0, blocks, group, 0)


def lookup_kernel(peers, stride, start, cap, asked, table_ref, out, table, rows):
    table[...] = table_ref[...].astype(f32)

    def peer(d, carry):
        for c in range(cap):
            r = asked[d * stride + start + c]
            rows[pl.ds(d * cap + c, 1), :] = table[pl.ds(r, 1), :]
        return carry

    lax.fori_loop(0, peers, peer, 0)
    out[...] = rows[...].astype(bf16)


def micro_kernel(
    peers,
    cap,
    features,
    m,
    slot_start,
    fetch_start,
    ret_start,
    loss_mult,
    slots,
    out_b,
    fetched_hbm,
    freq_part_hbm,
    bottom,
    labels,
    cross_u_hbm,
    cross_v_hbm,
    bias,
    weight,
    *refs,
):
    (
        returned_hbm,
        d_pooled_hbm,
        x_zero_hbm,
        hidden_hbm,
        d_hidden_hbm,
        gate_low_hbm,
        grad_bw,
        arrived,
        *accs,
        gate,
        returned,
        x_zero,
        hidden_out,
        d_hidden_out,
        gate_low,
        cross_u,
        cross_v,
        sems,
    ) = refs[-25:]
    acc0 = accs[0]
    samples, width = x_zero.shape
    emb = bottom.shape[2]
    n_slots = features * samples
    ways = len(accs)
    loads = [
        pltpu.make_async_copy(
            fetched_hbm.at[:, pl.ds(fetch_start, cap), :], returned, sems.at[6]
        ),
        pltpu.make_async_copy(freq_part_hbm, acc0.at[pl.ds(0, n_slots), :], sems.at[7]),
        pltpu.make_async_copy(cross_u_hbm, cross_u, sems.at[8]),
        pltpu.make_async_copy(cross_v_hbm, cross_v, sems.at[9]),
    ]
    for load in loads:
        load.start()
    for a in accs[1:]:
        a[...] = jnp.zeros_like(a)
    acc0[n_slots:, :] = jnp.zeros((acc0.shape[0] - n_slots, emb), f32)
    loads[0].wait()
    arrived[...] = returned[...].astype(f32).reshape(peers * cap, emb)
    loads[1].wait()

    def add_peer(o, carry):
        for c in range(0, cap, ways):
            at = [slots[slot_start + (c + j) * peers + o] for j in range(ways)]
            new = [
                accs[j][pl.ds(at[j], 1), :] + arrived[pl.ds(o * cap + c + j, 1), :]
                for j in range(ways)
            ]
            for j in range(ways):
                accs[j][pl.ds(at[j], 1), :] = new[j]
        return carry

    lax.fori_loop(0, peers, add_peer, 0)

    x_zero[:, 0:emb] = bottom[m]
    for f in range(features):
        rows = pl.ds(f * samples, samples)
        total = tree_sum([a[rows, :] for a in accs])
        x_zero[:, (f + 1) * emb : (f + 2) * emb] = total.astype(bf16)

    loads[2].wait()
    loads[3].wait()
    hidden = jnp.dot(x_zero[...], cross_u[...], preferred_element_type=f32).astype(bf16)
    hidden_out[...] = hidden
    copies = [
        pltpu.make_async_copy(x_zero, x_zero_hbm, sems.at[0]),
        pltpu.make_async_copy(hidden_out, hidden_hbm, sems.at[1]),
    ]
    for copy in copies:
        copy.start()
    chunk = 3 * emb
    chunks = width // chunk
    partial = jnp.zeros((samples, emb), f32)
    for k in range(chunks):
        cols = slice(k * chunk, (k + 1) * chunk)
        value = jnp.dot(hidden, cross_v[:, cols], preferred_element_type=f32) + bias[:, cols]
        gate[:, cols] = value
        x_float = x_zero[:, cols].astype(f32)
        scored = (x_float * value + x_float) * weight[:, cols]
        for j in range(3):
            partial = partial + scored[:, j * emb : (j + 1) * emb]
    logits = jnp.sum(partial, axis=1, keepdims=True) + out_b[0]
    square = (samples, samples)
    diagonal = lax.broadcasted_iota(jnp.int32, square, 0) == lax.broadcasted_iota(
        jnp.int32, square, 1
    )
    label = jnp.sum(jnp.where(diagonal, labels[m : m + 1, :], 0.0), axis=1, keepdims=True)
    d_logit = (jax.nn.sigmoid(logits) - label) * loss_mult
    for k in range(chunks):
        cols = slice(k * chunk, (k + 1) * chunk)
        x_float = x_zero[:, cols].astype(f32)
        d_gate = (d_logit * weight[:, cols]) * x_float
        gate_low[:, cols] = d_gate.astype(bf16)
        crossed = x_float * gate[:, cols] + x_float
        grad_bw[0:1, cols] = jnp.sum(d_gate, axis=0, keepdims=True)
        grad_bw[1:2, cols] = jnp.sum(d_logit * crossed, axis=0, keepdims=True)
    d_hidden = lax.dot_general(
        gate_low[...], cross_v[...], NT, preferred_element_type=f32
    ).astype(bf16)
    d_hidden_out[...] = d_hidden
    later = [
        pltpu.make_async_copy(gate_low, gate_low_hbm, sems.at[2]),
        pltpu.make_async_copy(d_hidden_out, d_hidden_hbm, sems.at[3]),
    ]
    for copy in later:
        copy.start()
    for k in range(chunks):
        cols = slice(k * chunk, (k + 1) * chunk)
        back = lax.dot_general(d_hidden, cross_u[cols, :], NT, preferred_element_type=f32)
        d_input = (d_logit * weight[:, cols]) * (gate[:, cols] + 1.0) + back
        for j in range(3):
            f = 3 * k + j - 1
            if f >= 0:
                acc0[f * samples : (f + 1) * samples, :] = d_input[:, j * emb : (j + 1) * emb]
    acc0[n_slots:, :] = jnp.zeros((acc0.shape[0] - n_slots, emb), f32)
    pooled_copy = pltpu.make_async_copy(acc0.at[pl.ds(0, n_slots), :], d_pooled_hbm, sems.at[4])
    pooled_copy.start()

    def take_peer(o, carry):
        for c in range(cap):
            at = slots[slot_start + c * peers + o]
            arrived[pl.ds(o * cap + c, 1), :] = acc0[pl.ds(at, 1), :]
        return carry

    lax.fori_loop(0, peers, take_peer, 0)
    returned[...] = arrived[...].astype(bf16).reshape(peers, cap, emb)
    returned_copy = pltpu.make_async_copy(
        returned, returned_hbm.at[:, pl.ds(ret_start, cap), :], sems.at[5]
    )
    returned_copy.start()
    for copy in copies + later:
        copy.wait()
    pooled_copy.wait()
    returned_copy.wait()


def dense_grad_kernel(
    peers, per, columns, x0, x1, x2, g0, g1, g2, h0, h1, h2, e0, e1, e2, parts_hbm, total, parts, sem
):
    width = x0.shape[1]
    rank = h0.shape[1]
    chunk = 128
    h_all = jnp.concatenate([h0[...], h1[...], h2[...]], axis=0)
    e_all = jnp.concatenate([e0[...], e1[...], e2[...]], axis=0)
    for k in range(width // chunk):
        cols = slice(k * chunk, (k + 1) * chunk)
        x_all = jnp.concatenate([x0[:, cols], x1[:, cols], x2[:, cols]], axis=0)
        g_all = jnp.concatenate([g0[:, cols], g1[:, cols], g2[:, cols]], axis=0)
        total[cols, 0:rank] = lax.dot_general(x_all, e_all, TN, preferred_element_type=f32)
        total[cols, rank : 2 * rank] = lax.dot_general(
            g_all, h_all, TN, preferred_element_type=f32
        )
    total[width:, :] = jnp.zeros((total.shape[0] - width, 2 * rank), f32)
    rows = parts.shape[2]
    spare = lax.broadcasted_iota(jnp.int32, (16, 128), 0) >= per - 16

    def blocks(q, carry):
        base = q * 8 * per
        for i in range(8):
            skip = i * per % 8
            window = total[pl.ds(pl.multiple_of(base + (i * per - skip), 8), rows + 8), :]
            value = window[skip : skip + rows]
            parts[q, i, 0:16, :] = value[0:16].astype(bf16)
            parts[q, i, 16:32, 128:] = value[16:32, 128:].astype(bf16)
            parts[q, i, 16:32, 0:128] = jnp.where(
                spare, columns[q * 8 + i], value[16:32, 0:128]
            ).astype(bf16)
        pltpu.make_async_copy(
            parts.at[q], parts_hbm.at[:, q % 4 * 4 + q // 4], sem.at[q]
        ).start()
        return carry

    lax.fori_loop(0, peers // 8, blocks, 0)

    def ends(q, carry):
        pltpu.make_async_copy(
            parts.at[q], parts_hbm.at[:, q % 4 * 4 + q // 4], sem.at[q]
        ).wait()
        return carry

    lax.fori_loop(0, peers // 8, ends, 0)


def freq_grad_kernel(
    features, core, ids, d0, d1, d2, keep, send, *scratch
):
    *accs, buf0, buf1, buf2, sems = scratch
    pairs = len(accs) // 2
    samples = d0.shape[0] // features
    loads = [
        pltpu.make_async_copy(d, buf, sems.at[k])
        for k, (d, buf) in enumerate(((d0, buf0), (d1, buf1), (d2, buf2)))
    ]
    for load in loads:
        load.start()
    for a in accs:
        a[...] = jnp.zeros_like(a)
    for m, source in enumerate((buf0, buf1, buf2)):
        loads[m].wait()
        start = m * features * 2 * samples

        def feature(f, carry):
            base = f * samples
            first = start + f * 2 * samples
            for s in range(0, samples, pairs):
                count = min(pairs, samples - s)
                at = [
                    ids[first + h * samples + s + j] for j in range(count) for h in range(2)
                ]
                value = [source[pl.ds(base + s + j, 1), :] for j in range(count)]
                new = [accs[j][pl.ds(at[j], 1), :] + value[j // 2] for j in range(2 * count)]
                for j in range(2 * count):
                    accs[j][pl.ds(at[j], 1), :] = new[j]
            return carry

        lax.fori_loop(0, features, feature, 0)
    rows = 128
    mine = core[0]

    def block(q, carry):
        for ref, parity in ((keep, mine), (send, 1 - mine)):
            at = pl.ds(pl.multiple_of(((q % 4 * 2 + parity) * 16 + q // 4) * rows, rows), rows)
            ref[q] = tree_sum([a[at, :] for a in accs]).astype(bf16)
        return carry

    lax.fori_loop(0, keep.shape[0], block, 0)


def spread_kernel(parts, out):
    total = parts[0].astype(f32)
    for k in range(1, parts.shape[0]):
        total = total + parts[k].astype(f32)
    total = total.astype(bf16)
    for k in range(out.shape[0]):
        out[k] = total


def owner_kernel(peers, stride, cap, asked, arrived, out, rows, *accs):
    ways = len(accs)
    for a in accs:
        a[...] = jnp.zeros_like(a)
    emb = out.shape[1]
    for m in range(3):
        part = arrived[:, m * cap : (m + 1) * cap, :]
        rows[...] = part.astype(f32).reshape(peers * cap, emb)

        def peer(d, carry):
            for c in range(0, cap, ways):
                at = [asked[d * stride + m * cap + c + j] for j in range(ways)]
                new = [
                    accs[j][pl.ds(at[j], 1), :] + rows[pl.ds(d * cap + c + j, 1), :]
                    for j in range(ways)
                ]
                for j in range(ways):
                    accs[j][pl.ds(at[j], 1), :] = new[j]
            return carry

        lax.fori_loop(0, peers, peer, 0)
    at = slice(0, out.shape[0])
    out[...] = tree_sum([a[at, :] for a in accs]).astype(bf16)


def on_device(
    bottom,
    labels,
    freq_ids,
    req_rows,
    req_slot,
    freq_table,
    inf_table,
    cross_u,
    cross_v,
    cross_bias,
    out_w,
    out_b,
):
    devices = lax.axis_size("dev")
    micro, samples, emb = bottom.shape
    features = freq_ids.shape[2]
    hot = freq_ids.shape[3]
    owned = inf_table.shape[0]
    cap = req_rows.shape[3]
    width, rank = cross_u.shape
    freq_rows = freq_table.shape[0]
    n_slots = samples * features
    n_req = devices * cap
    per = width // devices
    loss_mult = loss_scale / math.sqrt(micro * samples * devices)
    me = lax.axis_index("dev")
    core = (me % 2).astype(jnp.int32).reshape(1)
    other_core = [(d, d ^ 1) for d in range(devices)]
    same_core = [list(range(c, devices, 2)) for c in range(2)]

    ids = jnp.transpose(freq_ids, (0, 2, 3, 1)).reshape(-1)
    rows_mc = jnp.transpose(req_rows[:, 0], (0, 2, 1))
    slot_mc = jnp.transpose(req_slot[:, 0], (0, 2, 1))
    is_live = (rows_mc < owned) & (slot_mc < n_slots)
    place = jnp.where(
        is_live, (slot_mc % features) * samples + slot_mc // features, n_slots
    ).reshape(-1)
    line = jnp.where(
        (req_rows < owned) & (req_slot < n_slots), req_rows, owned
    )[:, 0]
    line = jnp.transpose(line, (1, 0, 2)).reshape(devices, micro * cap)
    stride = -(-micro * cap // 128) * 128
    line = jnp.pad(line, ((0, 0), (0, stride - micro * cap)), constant_values=owned)
    asked = lax.all_to_all(line, "dev", split_axis=0, concat_axis=0, tiled=True).reshape(-1)

    def freq_rows_of(first_micro, count):
        return local_call(
            functools.partial(freq_kernel, features, samples, first_micro),
            [((n_slots, emb), f32)] * count,
            [SMEM, VMEM],
            [pltpu.VMEM((freq_rows, emb), f32)],
            f"freq_rows{first_micro}",
            62,
            0,
            (12 + 14 * count) * MIB,
        )(ids, freq_table)

    freq_part = list(freq_rows_of(0, 1))
    asked, freq_part[0] = lax.optimization_barrier((asked, freq_part[0]))
    asked_row = jnp.minimum(asked, owned - 1)
    weight = out_w.astype(f32).reshape(1, width)
    bias = cross_bias.reshape(1, width)
    label_rows = labels.astype(f32)
    bias_b = out_b.reshape(1)

    def axis_sum(blocks, step):
        at = me // step % 4
        total = lax.dynamic_index_in_dim(blocks, at, 0, keepdims=False).astype(f32)
        for k in range(1, 4):
            block = lax.dynamic_index_in_dim(blocks, (at + k) % 4, 0, keepdims=False)
            to = [(d, d + ((d // step % 4 + k) % 4 - d // step % 4) * step) for d in range(devices)]
            total = total + lax.ppermute(block, "dev", to).astype(f32)
        return total

    def exchange(rows, count):
        return lax.all_to_all(
            rows.reshape(devices, count, emb), "dev", split_axis=0, concat_axis=0, tiled=True
        ).reshape(n_req * count // cap, emb)

    outs = []

    def lookup(start, count):
        return local_call(
            functools.partial(lookup_kernel, devices, stride, start, count),
            [((devices * count, emb), bf16)],
            [SMEM, VMEM],
            [pltpu.VMEM((owned, emb), f32), pltpu.VMEM((devices * count, emb), f32)],
            f"lookup{start}",
            62,
            0,
            count * MIB * 5 // 8,
        )(asked_row, inf_table)[0]

    looked = lookup(0, cap)
    asked_row, looked = lax.optimization_barrier((asked_row, looked))
    looked_rest = lookup(cap, (micro - 1) * cap)
    fetched = exchange(looked, cap)
    ids, looked_rest = lax.optimization_barrier((ids, looked_rest))
    freq_part += freq_rows_of(1, 1)
    small = (place, weight, bias, label_rows, bias_b)
    looked_rest, fetched, freq_part[1], small = lax.optimization_barrier(
        (looked_rest, fetched, freq_part[1], small)
    )
    place, weight, bias, label_rows, bias_b = small
    fetched_rest = exchange(looked_rest, (micro - 1) * cap)
    ids, freq_part[1] = lax.optimization_barrier((ids, freq_part[1]))
    freq_part += freq_rows_of(2, 1)
    for m in range(micro):
        if m == 1:
            fetched_rest, outs[0][6], freq_part[2] = lax.optimization_barrier(
                (fetched_rest, outs[0][6], freq_part[2])
            )
        out = local_call(
            functools.partial(
                micro_kernel,
                devices,
                cap,
                features,
                m,
                m * n_req,
                max(m - 1, 0) * cap,
                m * cap,
                loss_mult,
            ),
            [
                ((devices, micro * cap, emb), bf16),
                ((n_slots, emb), f32),
                ((samples, width), bf16),
                ((samples, rank), bf16),
                ((samples, rank), bf16),
                ((samples, width), bf16),
                ((2, width), f32),
            ],
            [SMEM, SMEM, HBM, HBM, VMEM, VMEM, HBM, HBM, VMEM, VMEM] + ([HBM] if m else []),
            [pltpu.VMEM((n_req, emb), f32)]
            + [pltpu.VMEM((n_slots + 8, emb), f32)] * 8
            + [pltpu.VMEM((samples, width), f32)]
            + [pltpu.VMEM((devices, cap, emb), bf16), pltpu.VMEM((samples, width), bf16)]
            + [pltpu.VMEM((samples, rank), bf16)] * 2
            + [pltpu.VMEM((samples, width), bf16)]
            + [pltpu.VMEM((width, rank), bf16), pltpu.VMEM((rank, width), bf16)]
            + [pltpu.SemaphoreType.DMA((10,))],
            f"micro{m}",
            62,
            6 * samples * width * rank,
            60 * MIB,
            [HBM] * 6 + [VMEM],
            {10: 0} if m else {},
        )(
            place,
            bias_b,
            (fetched_rest if m else fetched).reshape(devices, -1, emb),
            freq_part[m],
            bottom,
            label_rows,
            cross_u,
            cross_v,
            bias,
            weight,
            *([outs[m - 1][0]] if m else []),
        )
        outs.append(list(out))
        if m == 1:
            place, outs[1][6] = lax.optimization_barrier((place, outs[1][6]))
    arrived = exchange(outs[2][0], micro * cap)
    d_pooled = [o[1] for o in outs]
    grad_bw = ((outs[0][6] + outs[1][6]) + outs[2][6]).reshape(2, devices, per)
    columns = jnp.pad(
        jnp.transpose(grad_bw, (1, 0, 2)), ((0, 0), (per - 16, 30 - per), (0, 128 - per))
    )

    rows_pad = -(-per // 16) * 16
    per_freq = freq_rows // devices
    (dense,) = local_call(
        functools.partial(dense_grad_kernel, devices, per),
        [((8, devices // 8, rows_pad, 2 * rank), bf16)],
        [VMEM] * 13,
        [
            pltpu.VMEM((width + 16, 2 * rank), f32),
            pltpu.VMEM((devices // 8, 8, rows_pad, 2 * rank), bf16),
            pltpu.SemaphoreType.DMA((devices // 8,)),
        ],
        "dense_grads",
        62,
        12 * samples * width * rank,
        40 * MIB,
        [HBM],
    )(
        columns,
        *[o[2] for o in outs],
        *[o[5] for o in outs],
        *[o[3] for o in outs],
        *[o[4] for o in outs],
    )
    core, dense = lax.optimization_barrier((core, dense))
    dense = dense.reshape(devices, rows_pad, 2 * rank)
    near = [list(range(d, d + 8)) for d in range(0, devices, 8)]
    dense = lax.psum_scatter(dense, "dev", axis_index_groups=near, tiled=True)
    keep_f, send_f = local_call(
        functools.partial(freq_grad_kernel, features),
        [((devices // 2, per_freq, emb), bf16)] * 2,
        [SMEM, SMEM] + [HBM] * 3,
        [pltpu.VMEM((freq_rows, emb), f32)] * 6
        + [pltpu.VMEM((n_slots, emb), f32)] * 3
        + [pltpu.SemaphoreType.DMA((3,))],
        "freq_grads",
        62,
        0,
        120 * MIB,
    )(core, ids, *d_pooled)
    got = lax.ppermute(send_f, "dev", other_core)
    both = (keep_f.astype(f32) + got.astype(f32)).astype(bf16)
    both, arrived = lax.optimization_barrier((both, arrived))
    parts = lax.all_to_all(
        both, "dev", split_axis=0, concat_axis=0, axis_index_groups=same_core, tiled=True
    )
    (grad_inf,) = local_call(
        functools.partial(owner_kernel, devices, stride, cap),
        [((owned, emb), bf16)],
        [SMEM, VMEM],
        [pltpu.VMEM((n_req, emb), f32)] + [pltpu.VMEM((owned + 8, emb), f32)] * 8,
        "owner_grads",
        62,
        0,
        60 * MIB,
    )(
        asked,
        arrived.reshape(devices, micro * cap, emb),
    )

    parts, grad_inf = lax.optimization_barrier((parts, grad_inf))
    (spread,) = local_call(
        spread_kernel,
        [((devices // 8, per_freq, emb), bf16)],
        [VMEM],
        [],
        "spread",
        62,
        0,
        4 * MIB,
    )(parts)
    sixteen = lax.all_to_all(
        spread,
        "dev",
        split_axis=0,
        concat_axis=0,
        axis_index_groups=[list(range(k, devices, 8)) for k in range(8)],
        tiled=True,
    ).reshape(freq_rows // 8, emb)
    sixteen, dense = lax.optimization_barrier((sixteen, dense))
    grad_freq = lax.all_gather(sixteen, "dev", axis_index_groups=near, tiled=True)
    dense = axis_sum(dense.reshape(4, 4, rows_pad, 2 * rank), 8).astype(bf16)
    dense = axis_sum(dense, 32)
    grad_u = dense[:per, :rank]
    grad_v = dense[:per, rank:].T
    grad_b = dense[per, :per]
    grad_w = dense[per + 1, :per]
    return (grad_u, grad_v, grad_b, grad_w, grad_freq, grad_inf)


def solution(mesh):
    in_specs = (
        P(None, "dev", None),
        P(None, "dev"),
        P(None, "dev", None, None),
        P(None, "dev", None, None),
        P(None, "dev", None, None),
        P(),
        P("dev", None),
        P(),
        P(),
        P(),
        P(),
        P(),
    )
    out_specs = (P("dev", None), P(None, "dev"), P("dev"), P("dev"), P(), P("dev", None))
    return jax.shard_map(
        on_device, mesh=mesh, in_specs=in_specs, out_specs=out_specs, check_vma=False
    )
```

```python
import functools
import math

import jax
import jax.numpy as jnp
from jax import lax
from jax.experimental import pallas as pl
from jax.experimental.pallas import tpu as pltpu
from jax.sharding import PartitionSpec as P

loss_scale = 1024.0
f32 = jnp.float32
bf16 = jnp.bfloat16
MIB = 1024 * 1024
SMEM = pl.BlockSpec(memory_space=pltpu.SMEM)
VMEM = pl.BlockSpec(memory_space=pltpu.VMEM)
HBM = pl.BlockSpec(memory_space=pltpu.HBM)
NT = (((1,), (1,)), ((), ()))
TN = (((0,), (0,)), ((), ()))


def tree_sum(terms):
    while len(terms) > 1:
        terms = [sum(terms[k : k + 2][1:], terms[k]) for k in range(0, len(terms), 2)]
    return terms[0]


def local_call(
    kernel, outs, in_specs, scratch, name, limit, flops, bytes_accessed, out_specs=None, aliases={}
):
    return pl.pallas_call(
        kernel,
        out_shape=[jax.ShapeDtypeStruct(s, d) for s, d in outs],
        in_specs=in_specs,
        out_specs=out_specs or [VMEM] * len(outs),
        scratch_shapes=scratch,
        compiler_params=pltpu.CompilerParams(vmem_limit_bytes=limit * MIB),
        cost_estimate=pl.CostEstimate(
            flops=flops, bytes_accessed=bytes_accessed, transcendentals=0
        ),
        input_output_aliases=aliases,
        name=name,
    )


def freq_kernel(blocks, samples, first_micro, ids, table_ref, *refs):
    *outs, table = refs
    table[...] = table_ref[...].astype(f32)
    unroll = 32
    for m, out in enumerate(outs):
        start = (first_micro + m) * blocks * 2 * samples

        def group(g, carry):
            def some(k, carry):
                for u in range(unroll):
                    s = k * unroll + u
                    first = ids[start + g * 2 * samples + s]
                    second = ids[start + g * 2 * samples + samples + s]
                    out[pl.ds(g * samples + s, 1), :] = (
                        table[pl.ds(first, 1), :] + table[pl.ds(second, 1), :]
                    )
                return carry

            return lax.fori_loop(0, samples // unroll, some, carry)

        lax.fori_loop(0, blocks, group, 0)


def lookup_kernel(peers, stride, start, cap, asked, table_ref, out, table, rows):
    table[...] = table_ref[...].astype(f32)

    def peer(d, carry):
        for c in range(cap):
            r = asked[d * stride + start + c]
            rows[pl.ds(d * cap + c, 1), :] = table[pl.ds(r, 1), :]
        return carry

    lax.fori_loop(0, peers, peer, 0)
    out[...] = rows[...].astype(bf16)


def micro_kernel(
    peers,
    cap,
    features,
    m,
    slot_start,
    fetch_start,
    ret_start,
    loss_mult,
    slots,
    out_b,
    fetched_hbm,
    freq_part_hbm,
    bottom,
    labels,
    cross_u_hbm,
    cross_v_hbm,
    bias,
    weight,
    *refs,
):
    (
        returned_hbm,
        d_pooled_hbm,
        x_zero_hbm,
        hidden_hbm,
        d_hidden_hbm,
        gate_low_hbm,
        grad_bw,
        arrived,
        *accs,
        gate,
        returned,
        x_zero,
        hidden_out,
        d_hidden_out,
        gate_low,
        cross_u,
        cross_v,
        sems,
    ) = refs[-25:]
    acc0 = accs[0]
    samples, width = x_zero.shape
    emb = bottom.shape[2]
    n_slots = features * samples
    ways = len(accs)
    loads = [
        pltpu.make_async_copy(
            fetched_hbm.at[:, pl.ds(fetch_start, cap), :], returned, sems.at[6]
        ),
        pltpu.make_async_copy(freq_part_hbm, acc0.at[pl.ds(0, n_slots), :], sems.at[7]),
        pltpu.make_async_copy(cross_u_hbm, cross_u, sems.at[8]),
        pltpu.make_async_copy(cross_v_hbm, cross_v, sems.at[9]),
    ]
    for load in loads:
        load.start()
    for a in accs[1:]:
        a[...] = jnp.zeros_like(a)
    acc0[n_slots:, :] = jnp.zeros((acc0.shape[0] - n_slots, emb), f32)
    loads[0].wait()
    arrived[...] = returned[...].astype(f32).reshape(peers * cap, emb)
    loads[1].wait()

    def add_peer(o, carry):
        for c in range(0, cap, ways):
            at = [slots[slot_start + (c + j) * peers + o] for j in range(ways)]
            new = [
                accs[j][pl.ds(at[j], 1), :] + arrived[pl.ds(o * cap + c + j, 1), :]
                for j in range(ways)
            ]
            for j in range(ways):
                accs[j][pl.ds(at[j], 1), :] = new[j]
        return carry

    lax.fori_loop(0, peers, add_peer, 0)

    x_zero[:, 0:emb] = bottom[m]
    for f in range(features):
        rows = pl.ds(f * samples, samples)
        total = tree_sum([a[rows, :] for a in accs])
        x_zero[:, (f + 1) * emb : (f + 2) * emb] = total.astype(bf16)

    loads[2].wait()
    loads[3].wait()
    hidden = jnp.dot(x_zero[...], cross_u[...], preferred_element_type=f32).astype(bf16)
    hidden_out[...] = hidden
    copies = [
        pltpu.make_async_copy(x_zero, x_zero_hbm, sems.at[0]),
        pltpu.make_async_copy(hidden_out, hidden_hbm, sems.at[1]),
    ]
    for copy in copies:
        copy.start()
    chunk = 3 * emb
    chunks = width // chunk
    partial = jnp.zeros((samples, emb), f32)
    for k in range(chunks):
        cols = slice(k * chunk, (k + 1) * chunk)
        value = jnp.dot(hidden, cross_v[:, cols], preferred_element_type=f32) + bias[:, cols]
        gate[:, cols] = value
        x_float = x_zero[:, cols].astype(f32)
        scored = (x_float * value + x_float) * weight[:, cols]
        for j in range(3):
            partial = partial + scored[:, j * emb : (j + 1) * emb]
    logits = jnp.sum(partial, axis=1, keepdims=True) + out_b[0]
    square = (samples, samples)
    diagonal = lax.broadcasted_iota(jnp.int32, square, 0) == lax.broadcasted_iota(
        jnp.int32, square, 1
    )
    label = jnp.sum(jnp.where(diagonal, labels[m : m + 1, :], 0.0), axis=1, keepdims=True)
    d_logit = (jax.nn.sigmoid(logits) - label) * loss_mult
    for k in range(chunks):
        cols = slice(k * chunk, (k + 1) * chunk)
        x_float = x_zero[:, cols].astype(f32)
        d_gate = (d_logit * weight[:, cols]) * x_float
        gate_low[:, cols] = d_gate.astype(bf16)
        crossed = x_float * gate[:, cols] + x_float
        grad_bw[0:1, cols] = jnp.sum(d_gate, axis=0, keepdims=True)
        grad_bw[1:2, cols] = jnp.sum(d_logit * crossed, axis=0, keepdims=True)
    d_hidden = lax.dot_general(
        gate_low[...], cross_v[...], NT, preferred_element_type=f32
    ).astype(bf16)
    d_hidden_out[...] = d_hidden
    later = [
        pltpu.make_async_copy(gate_low, gate_low_hbm, sems.at[2]),
        pltpu.make_async_copy(d_hidden_out, d_hidden_hbm, sems.at[3]),
    ]
    for copy in later:
        copy.start()
    for k in range(chunks):
        cols = slice(k * chunk, (k + 1) * chunk)
        back = lax.dot_general(d_hidden, cross_u[cols, :], NT, preferred_element_type=f32)
        d_input = (d_logit * weight[:, cols]) * (gate[:, cols] + 1.0) + back
        for j in range(3):
            f = 3 * k + j - 1
            if f >= 0:
                acc0[f * samples : (f + 1) * samples, :] = d_input[:, j * emb : (j + 1) * emb]
    acc0[n_slots:, :] = jnp.zeros((acc0.shape[0] - n_slots, emb), f32)
    pooled_copy = pltpu.make_async_copy(acc0.at[pl.ds(0, n_slots), :], d_pooled_hbm, sems.at[4])
    pooled_copy.start()

    def take_peer(o, carry):
        for c in range(cap):
            at = slots[slot_start + c * peers + o]
            arrived[pl.ds(o * cap + c, 1), :] = acc0[pl.ds(at, 1), :]
        return carry

    lax.fori_loop(0, peers, take_peer, 0)
    returned[...] = arrived[...].astype(bf16).reshape(peers, cap, emb)
    returned_copy = pltpu.make_async_copy(
        returned, returned_hbm.at[:, pl.ds(ret_start, cap), :], sems.at[5]
    )
    returned_copy.start()
    for copy in copies + later:
        copy.wait()
    pooled_copy.wait()
    returned_copy.wait()


def dense_grad_kernel(
    peers, per, columns, x0, x1, x2, g0, g1, g2, h0, h1, h2, e0, e1, e2, parts_hbm, total, parts, sem
):
    width = x0.shape[1]
    rank = h0.shape[1]
    chunk = 128
    h_all = jnp.concatenate([h0[...], h1[...], h2[...]], axis=0)
    e_all = jnp.concatenate([e0[...], e1[...], e2[...]], axis=0)
    for k in range(width // chunk):
        cols = slice(k * chunk, (k + 1) * chunk)
        x_all = jnp.concatenate([x0[:, cols], x1[:, cols], x2[:, cols]], axis=0)
        g_all = jnp.concatenate([g0[:, cols], g1[:, cols], g2[:, cols]], axis=0)
        total[cols, 0:rank] = lax.dot_general(x_all, e_all, TN, preferred_element_type=f32)
        total[cols, rank : 2 * rank] = lax.dot_general(
            g_all, h_all, TN, preferred_element_type=f32
        )
    total[width:, :] = jnp.zeros((total.shape[0] - width, 2 * rank), f32)
    rows = parts.shape[2]
    spare = lax.broadcasted_iota(jnp.int32, (16, 128), 0) >= per - 16

    def blocks(q, carry):
        base = q * 8 * per
        for i in range(8):
            skip = i * per % 8
            window = total[pl.ds(pl.multiple_of(base + (i * per - skip), 8), rows + 8), :]
            value = window[skip : skip + rows]
            parts[q, i, 0:16, :] = value[0:16].astype(bf16)
            parts[q, i, 16:32, 128:] = value[16:32, 128:].astype(bf16)
            parts[q, i, 16:32, 0:128] = jnp.where(
                spare, columns[q * 8 + i], value[16:32, 0:128]
            ).astype(bf16)
        pltpu.make_async_copy(
            parts.at[q], parts_hbm.at[:, q % 4 * 4 + q // 4], sem.at[q]
        ).start()
        return carry

    lax.fori_loop(0, peers // 8, blocks, 0)

    def ends(q, carry):
        pltpu.make_async_copy(
            parts.at[q], parts_hbm.at[:, q % 4 * 4 + q // 4], sem.at[q]
        ).wait()
        return carry

    lax.fori_loop(0, peers // 8, ends, 0)


def freq_grad_kernel(
    features, core, ids, d0, d1, d2, keep, send, *scratch
):
    *accs, buf0, buf1, buf2, sems = scratch
    pairs = len(accs) // 2
    samples = d0.shape[0] // features
    loads = [
        pltpu.make_async_copy(d, buf, sems.at[k])
        for k, (d, buf) in enumerate(((d0, buf0), (d1, buf1), (d2, buf2)))
    ]
    for load in loads:
        load.start()
    for a in accs:
        a[...] = jnp.zeros_like(a)
    for m, source in enumerate((buf0, buf1, buf2)):
        loads[m].wait()
        start = m * features * 2 * samples

        def feature(f, carry):
            base = f * samples
            first = start + f * 2 * samples
            for s in range(0, samples, pairs):
                count = min(pairs, samples - s)
                at = [
                    ids[first + h * samples + s + j] for j in range(count) for h in range(2)
                ]
                value = [source[pl.ds(base + s + j, 1), :] for j in range(count)]
                new = [accs[j][pl.ds(at[j], 1), :] + value[j // 2] for j in range(2 * count)]
                for j in range(2 * count):
                    accs[j][pl.ds(at[j], 1), :] = new[j]
            return carry

        lax.fori_loop(0, features, feature, 0)
    rows = 128
    mine = core[0]

    def block(q, carry):
        for ref, parity in ((keep, mine), (send, 1 - mine)):
            at = pl.ds(pl.multiple_of(((q % 4 * 2 + parity) * 16 + q // 4) * rows, rows), rows)
            ref[q] = tree_sum([a[at, :] for a in accs]).astype(bf16)
        return carry

    lax.fori_loop(0, keep.shape[0], block, 0)


def spread_kernel(parts, out):
    total = parts[0].astype(f32)
    for k in range(1, parts.shape[0]):
        total = total + parts[k].astype(f32)
    total = total.astype(bf16)
    for k in range(out.shape[0]):
        out[k] = total


def owner_kernel(peers, stride, cap, micros, asked, arrived, before, out, rows, *accs):
    ways = len(accs)
    for a in accs:
        a[...] = jnp.zeros_like(a)
    owned, emb = out.shape
    for k, m in enumerate(micros):
        part = arrived[:, k * cap : (k + 1) * cap, :]
        rows[...] = part.astype(f32).reshape(peers * cap, emb)

        def peer(d, carry):
            for c in range(0, cap, ways):
                at = [asked[d * stride + m * cap + c + j] for j in range(ways)]
                new = [
                    accs[j][pl.ds(at[j], 1), :] + rows[pl.ds(d * cap + c + j, 1), :]
                    for j in range(ways)
                ]
                for j in range(ways):
                    accs[j][pl.ds(at[j], 1), :] = new[j]
            return carry

        lax.fori_loop(0, peers, peer, 0)
    total = tree_sum([a[0:owned, :] for a in accs])
    if before is not None:
        total = total + before[...]
    out[...] = total.astype(out.dtype)


def first_owner_kernel(peers, stride, cap, micros, asked, arrived, out, rows, *accs):
    owner_kernel(peers, stride, cap, micros, asked, arrived, None, out, rows, *accs)


def on_device(
    bottom,
    labels,
    freq_ids,
    req_rows,
    req_slot,
    freq_table,
    inf_table,
    cross_u,
    cross_v,
    cross_bias,
    out_w,
    out_b,
):
    devices = lax.axis_size("dev")
    micro, samples, emb = bottom.shape
    features = freq_ids.shape[2]
    hot = freq_ids.shape[3]
    owned = inf_table.shape[0]
    cap = req_rows.shape[3]
    width, rank = cross_u.shape
    freq_rows = freq_table.shape[0]
    n_slots = samples * features
    n_req = devices * cap
    per = width // devices
    loss_mult = loss_scale / math.sqrt(micro * samples * devices)
    me = lax.axis_index("dev")
    core = (me % 2).astype(jnp.int32).reshape(1)
    other_core = [(d, d ^ 1) for d in range(devices)]
    same_core = [list(range(c, devices, 2)) for c in range(2)]

    ids = jnp.transpose(freq_ids, (0, 2, 3, 1)).reshape(-1)
    rows_mc = jnp.transpose(req_rows[:, 0], (0, 2, 1))
    slot_mc = jnp.transpose(req_slot[:, 0], (0, 2, 1))
    is_live = (rows_mc < owned) & (slot_mc < n_slots)
    place = jnp.where(
        is_live, (slot_mc % features) * samples + slot_mc // features, n_slots
    ).reshape(-1)
    line = jnp.where(
        (req_rows < owned) & (req_slot < n_slots), req_rows, owned
    )[:, 0]
    line = jnp.transpose(line, (1, 0, 2)).reshape(devices, micro * cap)
    stride = -(-micro * cap // 128) * 128
    line = jnp.pad(line, ((0, 0), (0, stride - micro * cap)), constant_values=owned)
    asked = lax.all_to_all(line, "dev", split_axis=0, concat_axis=0, tiled=True).reshape(-1)

    def freq_rows_of(first_micro, count):
        return local_call(
            functools.partial(freq_kernel, features, samples, first_micro),
            [((n_slots, emb), f32)] * count,
            [SMEM, VMEM],
            [pltpu.VMEM((freq_rows, emb), f32)],
            f"freq_rows{first_micro}",
            62,
            0,
            (12 + 14 * count) * MIB,
        )(ids, freq_table)

    freq_part = list(freq_rows_of(0, 1))
    asked, freq_part[0] = lax.optimization_barrier((asked, freq_part[0]))
    asked_row = jnp.minimum(asked, owned - 1)
    weight = out_w.astype(f32).reshape(1, width)
    bias = cross_bias.reshape(1, width)
    label_rows = labels.astype(f32)
    bias_b = out_b.reshape(1)

    def axis_sum(blocks, step):
        at = me // step % 4
        total = lax.dynamic_index_in_dim(blocks, at, 0, keepdims=False).astype(f32)
        for k in range(1, 4):
            block = lax.dynamic_index_in_dim(blocks, (at + k) % 4, 0, keepdims=False)
            to = [(d, d + ((d // step % 4 + k) % 4 - d // step % 4) * step) for d in range(devices)]
            total = total + lax.ppermute(block, "dev", to).astype(f32)
        return total

    def exchange(rows, count):
        return lax.all_to_all(
            rows.reshape(devices, count, emb), "dev", split_axis=0, concat_axis=0, tiled=True
        ).reshape(n_req * count // cap, emb)

    outs = []

    def lookup(start, count):
        return local_call(
            functools.partial(lookup_kernel, devices, stride, start, count),
            [((devices * count, emb), bf16)],
            [SMEM, VMEM],
            [pltpu.VMEM((owned, emb), f32), pltpu.VMEM((devices * count, emb), f32)],
            f"lookup{start}",
            62,
            0,
            count * MIB * 5 // 8,
        )(asked_row, inf_table)[0]

    looked = lookup(0, cap)
    asked_row, looked = lax.optimization_barrier((asked_row, looked))
    looked_rest = lookup(cap, (micro - 1) * cap)
    fetched = exchange(looked, cap)
    ids, looked_rest = lax.optimization_barrier((ids, looked_rest))
    freq_part += freq_rows_of(1, 1)
    small = (place, weight, bias, label_rows, bias_b)
    looked_rest, fetched, freq_part[1], small = lax.optimization_barrier(
        (looked_rest, fetched, freq_part[1], small)
    )
    place, weight, bias, label_rows, bias_b = small
    fetched_rest = exchange(looked_rest, (micro - 1) * cap)
    ids, freq_part[1] = lax.optimization_barrier((ids, freq_part[1]))
    freq_part += freq_rows_of(2, 1)
    for m in range(micro):
        if m == 1:
            fetched_rest, outs[0][6], freq_part[2] = lax.optimization_barrier(
                (fetched_rest, outs[0][6], freq_part[2])
            )
        out = local_call(
            functools.partial(
                micro_kernel,
                devices,
                cap,
                features,
                m,
                m * n_req,
                max(m - 1, 0) * cap,
                cap if m == 1 else 0,
                loss_mult,
            ),
            [
                ((devices, cap if m == 2 else 2 * cap, emb), bf16),
                ((n_slots, emb), f32),
                ((samples, width), bf16),
                ((samples, rank), bf16),
                ((samples, rank), bf16),
                ((samples, width), bf16),
                ((2, width), f32),
            ],
            [SMEM, SMEM, HBM, HBM, VMEM, VMEM, HBM, HBM, VMEM, VMEM] + ([HBM] if m == 1 else []),
            [pltpu.VMEM((n_req, emb), f32)]
            + [pltpu.VMEM((n_slots + 8, emb), f32)] * 8
            + [pltpu.VMEM((samples, width), f32)]
            + [pltpu.VMEM((devices, cap, emb), bf16), pltpu.VMEM((samples, width), bf16)]
            + [pltpu.VMEM((samples, rank), bf16)] * 2
            + [pltpu.VMEM((samples, width), bf16)]
            + [pltpu.VMEM((width, rank), bf16), pltpu.VMEM((rank, width), bf16)]
            + [pltpu.SemaphoreType.DMA((10,))],
            f"micro{m}",
            62,
            6 * samples * width * rank,
            60 * MIB,
            [HBM] * 6 + [VMEM],
            {10: 0} if m == 1 else {},
        )(
            place,
            bias_b,
            (fetched_rest if m else fetched).reshape(devices, -1, emb),
            freq_part[m],
            bottom,
            label_rows,
            cross_u,
            cross_v,
            bias,
            weight,
            *([outs[0][0]] if m == 1 else []),
        )
        outs.append(list(out))
        if m == 1:
            place, outs[1][6] = lax.optimization_barrier((place, outs[1][6]))
    arrived_first = exchange(outs[1][0], 2 * cap)
    d_pooled = [o[1] for o in outs]
    grad_bw = ((outs[0][6] + outs[1][6]) + outs[2][6]).reshape(2, devices, per)
    columns = jnp.pad(
        jnp.transpose(grad_bw, (1, 0, 2)), ((0, 0), (per - 16, 30 - per), (0, 128 - per))
    )

    rows_pad = -(-per // 16) * 16
    per_freq = freq_rows // devices
    (dense,) = local_call(
        functools.partial(dense_grad_kernel, devices, per),
        [((8, devices // 8, rows_pad, 2 * rank), bf16)],
        [VMEM] * 13,
        [
            pltpu.VMEM((width + 16, 2 * rank), f32),
            pltpu.VMEM((devices // 8, 8, rows_pad, 2 * rank), bf16),
            pltpu.SemaphoreType.DMA((devices // 8,)),
        ],
        "dense_grads",
        62,
        12 * samples * width * rank,
        40 * MIB,
        [HBM],
    )(
        columns,
        *[o[2] for o in outs],
        *[o[5] for o in outs],
        *[o[3] for o in outs],
        *[o[4] for o in outs],
    )
    core, dense, arrived_first = lax.optimization_barrier((core, dense, arrived_first))
    dense = dense.reshape(devices, rows_pad, 2 * rank)
    near = [list(range(d, d + 8)) for d in range(0, devices, 8)]
    dense = lax.psum_scatter(dense, "dev", axis_index_groups=near, tiled=True)
    keep_f, send_f = local_call(
        functools.partial(freq_grad_kernel, features),
        [((devices // 2, per_freq, emb), bf16)] * 2,
        [SMEM, SMEM] + [HBM] * 3,
        [pltpu.VMEM((freq_rows, emb), f32)] * 6
        + [pltpu.VMEM((n_slots, emb), f32)] * 3
        + [pltpu.SemaphoreType.DMA((3,))],
        "freq_grads",
        62,
        0,
        120 * MIB,
    )(core, ids, *d_pooled)
    got = lax.ppermute(send_f, "dev", other_core)
    both = (keep_f.astype(f32) + got.astype(f32)).astype(bf16)
    parts = lax.all_to_all(
        both, "dev", split_axis=0, concat_axis=0, axis_index_groups=same_core, tiled=True
    )
    owner_scratch = [pltpu.VMEM((n_req, emb), f32)] + [pltpu.VMEM((owned + 8, emb), f32)] * 8
    (partial_inf,) = local_call(
        functools.partial(first_owner_kernel, devices, stride, cap, (0, 1)),
        [((owned, emb), f32)],
        [SMEM, VMEM],
        owner_scratch,
        "owner_first",
        62,
        0,
        40 * MIB,
    )(asked, arrived_first.reshape(devices, 2 * cap, emb))
    parts, partial_inf, dense = lax.optimization_barrier((parts, partial_inf, dense))
    (spread,) = local_call(
        spread_kernel,
        [((devices // 8, per_freq, emb), bf16)],
        [VMEM],
        [],
        "spread",
        62,
        0,
        4 * MIB,
    )(parts)
    sixteen = lax.all_to_all(
        spread,
        "dev",
        split_axis=0,
        concat_axis=0,
        axis_index_groups=[list(range(k, devices, 8)) for k in range(8)],
        tiled=True,
    ).reshape(freq_rows // 8, emb)
    sixteen, last = lax.optimization_barrier((sixteen, outs[2][0]))
    arrived_last = exchange(last, cap)
    grad_freq = lax.all_gather(sixteen, "dev", axis_index_groups=near, tiled=True)
    dense = axis_sum(dense.reshape(4, 4, rows_pad, 2 * rank), 8).astype(bf16)
    dense = axis_sum(dense, 32)
    (grad_inf,) = local_call(
        functools.partial(owner_kernel, devices, stride, cap, (2,)),
        [((owned, emb), bf16)],
        [SMEM, VMEM, VMEM],
        owner_scratch,
        "owner_last",
        62,
        0,
        25 * MIB,
    )(asked, arrived_last.reshape(devices, cap, emb), partial_inf)
    grad_u = dense[:per, :rank]
    grad_v = dense[:per, rank:].T
    grad_b = dense[per, :per]
    grad_w = dense[per + 1, :per]
    return (grad_u, grad_v, grad_b, grad_w, grad_freq, grad_inf)


def solution(mesh):
    in_specs = (
        P(None, "dev", None),
        P(None, "dev"),
        P(None, "dev", None, None),
        P(None, "dev", None, None),
        P(None, "dev", None, None),
        P(),
        P("dev", None),
        P(),
        P(),
        P(),
        P(),
        P(),
    )
    out_specs = (P("dev", None), P(None, "dev"), P("dev"), P("dev"), P(), P("dev", None))
    return jax.shard_map(
        on_device, mesh=mesh, in_specs=in_specs, out_specs=out_specs, check_vma=False
    )
```

```python
import functools
import math

import jax
import jax.numpy as jnp
from jax import lax
from jax.experimental import pallas as pl
from jax.experimental.pallas import tpu as pltpu
from jax.sharding import PartitionSpec as P

loss_scale = 1024.0
f32 = jnp.float32
bf16 = jnp.bfloat16
MIB = 1024 * 1024
SMEM = pl.BlockSpec(memory_space=pltpu.SMEM)
VMEM = pl.BlockSpec(memory_space=pltpu.VMEM)
HBM = pl.BlockSpec(memory_space=pltpu.HBM)
NT = (((1,), (1,)), ((), ()))
TN = (((0,), (0,)), ((), ()))


def tree_sum(terms):
    while len(terms) > 1:
        terms = [sum(terms[k : k + 2][1:], terms[k]) for k in range(0, len(terms), 2)]
    return terms[0]


def local_call(
    kernel, outs, in_specs, scratch, name, limit, flops, bytes_accessed, out_specs=None, aliases={}
):
    return pl.pallas_call(
        kernel,
        out_shape=[jax.ShapeDtypeStruct(s, d) for s, d in outs],
        in_specs=in_specs,
        out_specs=out_specs or [VMEM] * len(outs),
        scratch_shapes=scratch,
        compiler_params=pltpu.CompilerParams(vmem_limit_bytes=limit * MIB),
        cost_estimate=pl.CostEstimate(
            flops=flops, bytes_accessed=bytes_accessed, transcendentals=0
        ),
        input_output_aliases=aliases,
        name=name,
    )


def freq_kernel(blocks, samples, first_micro, ids, table_ref, *refs):
    *outs, table = refs
    table[...] = table_ref[...].astype(f32)
    unroll = 128
    for m, out in enumerate(outs):
        start = (first_micro + m) * blocks * 2 * samples

        def group(g, carry):
            def some(k, carry):
                for u in range(unroll):
                    s = k * unroll + u
                    first = ids[start + g * 2 * samples + s]
                    second = ids[start + g * 2 * samples + samples + s]
                    out[pl.ds(g * samples + s, 1), :] = (
                        table[pl.ds(first, 1), :] + table[pl.ds(second, 1), :]
                    )
                return carry

            return lax.fori_loop(0, samples // unroll, some, carry)

        lax.fori_loop(0, blocks, group, 0)


def lookup_kernel(peers, stride, start, cap, asked, table_ref, out, table, rows):
    table[...] = table_ref[...].astype(f32)

    def peer(d, carry):
        for c in range(cap):
            r = asked[d * stride + start + c]
            rows[pl.ds(d * cap + c, 1), :] = table[pl.ds(r, 1), :]
        return carry

    lax.fori_loop(0, peers, peer, 0)
    out[...] = rows[...].astype(bf16)


def micro_kernel(
    peers,
    cap,
    features,
    m,
    slot_start,
    fetch_start,
    ret_start,
    loss_mult,
    slots,
    out_b,
    fetched_ref,
    freq_part_hbm,
    bottom,
    labels,
    cross_u_hbm,
    cross_v_hbm,
    bias,
    weight,
    *refs,
):
    (
        returned_hbm,
        d_pooled_hbm,
        x_zero_hbm,
        hidden_hbm,
        d_hidden_hbm,
        gate_low_hbm,
        grad_bw,
        arrived,
        *accs,
        gate,
        returned,
        x_zero,
        hidden_out,
        d_hidden_out,
        gate_low,
        cross_u,
        cross_v,
        sems,
    ) = refs[-25:]
    before = refs[0]
    acc0 = accs[0]
    samples, width = x_zero.shape
    emb = bottom.shape[2]
    n_slots = features * samples
    ways = len(accs)
    loads = [
        pltpu.make_async_copy(freq_part_hbm, acc0.at[pl.ds(0, n_slots), :], sems.at[7]),
        pltpu.make_async_copy(cross_u_hbm, cross_u, sems.at[8]),
        pltpu.make_async_copy(cross_v_hbm, cross_v, sems.at[9]),
    ]
    if m > 0:
        fetch = pltpu.make_async_copy(
            fetched_ref.at[:, pl.ds(fetch_start, cap), :], returned, sems.at[6]
        )
        fetch.start()
    for load in loads:
        load.start()
    for a in accs[1:]:
        a[...] = jnp.zeros_like(a)
    acc0[n_slots:, :] = jnp.zeros((acc0.shape[0] - n_slots, emb), f32)
    if m > 0:
        fetch.wait()
    source = returned if m > 0 else fetched_ref
    arrived[...] = source[...].astype(f32).reshape(peers * cap, emb)
    loads[0].wait()

    def add_peer(o, carry):
        for c in range(0, cap, ways):
            at = [slots[slot_start + (c + j) * peers + o] for j in range(ways)]
            new = [
                accs[j][pl.ds(at[j], 1), :] + arrived[pl.ds(o * cap + c + j, 1), :]
                for j in range(ways)
            ]
            for j in range(ways):
                accs[j][pl.ds(at[j], 1), :] = new[j]
        return carry

    lax.fori_loop(0, peers, add_peer, 0)

    x_zero[:, 0:emb] = bottom[m]
    for f in range(features):
        rows = pl.ds(f * samples, samples)
        total = tree_sum([a[rows, :] for a in accs])
        x_zero[:, (f + 1) * emb : (f + 2) * emb] = total.astype(bf16)

    loads[1].wait()
    loads[2].wait()
    hidden = jnp.dot(x_zero[...], cross_u[...], preferred_element_type=f32).astype(bf16)
    hidden_out[...] = hidden
    copies = [
        pltpu.make_async_copy(x_zero, x_zero_hbm, sems.at[0]),
        pltpu.make_async_copy(hidden_out, hidden_hbm, sems.at[1]),
    ]
    for copy in copies:
        copy.start()
    chunk = 3 * emb
    chunks = width // chunk
    partial = jnp.zeros((samples, emb), f32)
    for k in range(chunks):
        cols = slice(k * chunk, (k + 1) * chunk)
        value = jnp.dot(hidden, cross_v[:, cols], preferred_element_type=f32) + bias[:, cols]
        gate[:, cols] = value
        x_float = x_zero[:, cols].astype(f32)
        scored = (x_float * value + x_float) * weight[:, cols]
        for j in range(3):
            partial = partial + scored[:, j * emb : (j + 1) * emb]
    logits = jnp.sum(partial, axis=1, keepdims=True) + out_b[0]
    square = (samples, samples)
    diagonal = lax.broadcasted_iota(jnp.int32, square, 0) == lax.broadcasted_iota(
        jnp.int32, square, 1
    )
    label = jnp.sum(jnp.where(diagonal, labels[m : m + 1, :], 0.0), axis=1, keepdims=True)
    d_logit = (jax.nn.sigmoid(logits) - label) * loss_mult
    for k in range(chunks):
        cols = slice(k * chunk, (k + 1) * chunk)
        x_float = x_zero[:, cols].astype(f32)
        d_gate = (d_logit * weight[:, cols]) * x_float
        gate_low[:, cols] = d_gate.astype(bf16)
        crossed = x_float * gate[:, cols] + x_float
        sums = [
            jnp.sum(d_gate, axis=0, keepdims=True),
            jnp.sum(d_logit * crossed, axis=0, keepdims=True),
        ]
        for k_row in range(2):
            if m > 0:
                sums[k_row] = sums[k_row] + before[k_row : k_row + 1, cols]
            grad_bw[k_row : k_row + 1, cols] = sums[k_row]
    d_hidden = lax.dot_general(
        gate_low[...], cross_v[...], NT, preferred_element_type=f32
    ).astype(bf16)
    d_hidden_out[...] = d_hidden
    later = [
        pltpu.make_async_copy(gate_low, gate_low_hbm, sems.at[2]),
        pltpu.make_async_copy(d_hidden_out, d_hidden_hbm, sems.at[3]),
    ]
    for copy in later:
        copy.start()
    for k in range(chunks):
        cols = slice(k * chunk, (k + 1) * chunk)
        back = lax.dot_general(d_hidden, cross_u[cols, :], NT, preferred_element_type=f32)
        d_input = (d_logit * weight[:, cols]) * (gate[:, cols] + 1.0) + back
        for j in range(3):
            f = 3 * k + j - 1
            if f >= 0:
                acc0[f * samples : (f + 1) * samples, :] = d_input[:, j * emb : (j + 1) * emb]
    acc0[n_slots:, :] = jnp.zeros((acc0.shape[0] - n_slots, emb), f32)
    pooled_copy = pltpu.make_async_copy(acc0.at[pl.ds(0, n_slots), :], d_pooled_hbm, sems.at[4])
    pooled_copy.start()

    def take_peer(o, carry):
        for c in range(cap):
            at = slots[slot_start + c * peers + o]
            arrived[pl.ds(o * cap + c, 1), :] = acc0[pl.ds(at, 1), :]
        return carry

    lax.fori_loop(0, peers, take_peer, 0)
    returned[...] = arrived[...].astype(bf16).reshape(peers, cap, emb)
    returned_copy = pltpu.make_async_copy(
        returned, returned_hbm.at[:, pl.ds(ret_start, cap), :], sems.at[5]
    )
    returned_copy.start()
    for copy in copies + later:
        copy.wait()
    pooled_copy.wait()
    returned_copy.wait()


def dense_grad_kernel(
    peers, per, columns, x0, x1, x2, g0, g1, g2, h0, h1, h2, e0, e1, e2, parts_hbm, total, parts, sem
):
    width = x0.shape[1]
    rank = h0.shape[1]
    chunk = 128
    h_all = jnp.concatenate([h0[...], h1[...], h2[...]], axis=0)
    e_all = jnp.concatenate([e0[...], e1[...], e2[...]], axis=0)
    for k in range(width // chunk):
        cols = slice(k * chunk, (k + 1) * chunk)
        x_all = jnp.concatenate([x0[:, cols], x1[:, cols], x2[:, cols]], axis=0)
        g_all = jnp.concatenate([g0[:, cols], g1[:, cols], g2[:, cols]], axis=0)
        total[cols, 0:rank] = lax.dot_general(x_all, e_all, TN, preferred_element_type=f32)
        total[cols, rank : 2 * rank] = lax.dot_general(
            g_all, h_all, TN, preferred_element_type=f32
        )
    total[width:, :] = jnp.zeros((total.shape[0] - width, 2 * rank), f32)
    rows = parts.shape[2]
    spare = lax.broadcasted_iota(jnp.int32, (16, 128), 0) >= per - 16

    def blocks(q, carry):
        base = q * 8 * per
        for i in range(8):
            skip = i * per % 8
            window = total[pl.ds(pl.multiple_of(base + (i * per - skip), 8), rows + 8), :]
            value = window[skip : skip + rows]
            parts[q, i, 0:16, :] = value[0:16].astype(bf16)
            parts[q, i, 16:32, 128:] = value[16:32, 128:].astype(bf16)
            parts[q, i, 16:32, 0:128] = jnp.where(
                spare, columns[q * 8 + i], value[16:32, 0:128]
            ).astype(bf16)
        pltpu.make_async_copy(
            parts.at[q], parts_hbm.at[:, q % 4 * 4 + q // 4], sem.at[q]
        ).start()
        return carry

    lax.fori_loop(0, peers // 8, blocks, 0)

    def ends(q, carry):
        pltpu.make_async_copy(
            parts.at[q], parts_hbm.at[:, q % 4 * 4 + q // 4], sem.at[q]
        ).wait()
        return carry

    lax.fori_loop(0, peers // 8, ends, 0)


def freq_grad_kernel(
    features, core, ids, d0, d1, d2, keep, send, *scratch
):
    *accs, buf0, buf1, buf2, sems = scratch
    pairs = len(accs) // 2
    samples = d0.shape[0] // features
    loads = [
        pltpu.make_async_copy(d, buf, sems.at[k])
        for k, (d, buf) in enumerate(((d0, buf0), (d1, buf1), (d2, buf2)))
    ]
    for load in loads:
        load.start()
    for a in accs:
        a[...] = jnp.zeros_like(a)
    for m, source in enumerate((buf0, buf1, buf2)):
        loads[m].wait()
        start = m * features * 2 * samples

        def feature(f, carry):
            base = f * samples
            first = start + f * 2 * samples
            for s in range(0, samples, pairs):
                count = min(pairs, samples - s)
                at = [
                    ids[first + h * samples + s + j] for j in range(count) for h in range(2)
                ]
                value = [source[pl.ds(base + s + j, 1), :] for j in range(count)]
                new = [accs[j][pl.ds(at[j], 1), :] + value[j // 2] for j in range(2 * count)]
                for j in range(2 * count):
                    accs[j][pl.ds(at[j], 1), :] = new[j]
            return carry

        lax.fori_loop(0, features, feature, 0)
    rows = 128
    mine = core[0]

    def block(q, carry):
        for ref, parity in ((keep, mine), (send, 1 - mine)):
            at = pl.ds(pl.multiple_of(((q % 4 * 2 + parity) * 16 + q // 4) * rows, rows), rows)
            ref[q] = tree_sum([a[at, :] for a in accs]).astype(bf16)
        return carry

    lax.fori_loop(0, keep.shape[0], block, 0)


def spread_kernel(parts, out):
    total = parts[0].astype(f32)
    for k in range(1, parts.shape[0]):
        total = total + parts[k].astype(f32)
    total = total.astype(bf16)
    for k in range(out.shape[0]):
        out[k] = total


def owner_kernel(peers, stride, cap, asked, arrived, out, rows, *accs):
    ways = len(accs)
    for a in accs:
        a[...] = jnp.zeros_like(a)
    emb = out.shape[1]
    for m in range(3):
        part = arrived[:, m * cap : (m + 1) * cap, :]
        rows[...] = part.astype(f32).reshape(peers * cap, emb)

        def peer(d, carry):
            for c in range(0, cap, ways):
                at = [asked[d * stride + m * cap + c + j] for j in range(ways)]
                new = [
                    accs[j][pl.ds(at[j], 1), :] + rows[pl.ds(d * cap + c + j, 1), :]
                    for j in range(ways)
                ]
                for j in range(ways):
                    accs[j][pl.ds(at[j], 1), :] = new[j]
            return carry

        lax.fori_loop(0, peers, peer, 0)
    at = slice(0, out.shape[0])
    out[...] = tree_sum([a[at, :] for a in accs]).astype(bf16)


def on_device(
    bottom,
    labels,
    freq_ids,
    req_rows,
    req_slot,
    freq_table,
    inf_table,
    cross_u,
    cross_v,
    cross_bias,
    out_w,
    out_b,
):
    devices = lax.axis_size("dev")
    micro, samples, emb = bottom.shape
    features = freq_ids.shape[2]
    hot = freq_ids.shape[3]
    owned = inf_table.shape[0]
    cap = req_rows.shape[3]
    width, rank = cross_u.shape
    freq_rows = freq_table.shape[0]
    n_slots = samples * features
    n_req = devices * cap
    per = width // devices
    loss_mult = loss_scale / math.sqrt(micro * samples * devices)
    me = lax.axis_index("dev")
    core = (me % 2).astype(jnp.int32).reshape(1)
    other_core = [(d, d ^ 1) for d in range(devices)]
    same_core = [list(range(c, devices, 2)) for c in range(2)]

    ids = jnp.transpose(freq_ids, (0, 2, 3, 1)).reshape(-1)
    rows_mc = jnp.transpose(req_rows[:, 0], (0, 2, 1))
    slot_mc = jnp.transpose(req_slot[:, 0], (0, 2, 1))
    is_live = (rows_mc < owned) & (slot_mc < n_slots)
    place = jnp.where(
        is_live, (slot_mc % features) * samples + slot_mc // features, n_slots
    ).reshape(-1)
    line = jnp.where(
        (req_rows < owned) & (req_slot < n_slots), req_rows, owned
    )[:, 0]
    line = jnp.transpose(line, (1, 0, 2)).reshape(devices, micro * cap)
    stride = -(-micro * cap // 128) * 128
    line = jnp.pad(line, ((0, 0), (0, stride - micro * cap)), constant_values=owned)
    asked = lax.all_to_all(line, "dev", split_axis=0, concat_axis=0, tiled=True).reshape(-1)

    def freq_rows_of(first_micro, count):
        return local_call(
            functools.partial(freq_kernel, features, samples, first_micro),
            [((n_slots, emb), f32)] * count,
            [SMEM, VMEM],
            [pltpu.VMEM((freq_rows, emb), f32)],
            f"freq_rows{first_micro}",
            62,
            0,
            (12 + 14 * count) * MIB,
        )(ids, freq_table)

    freq_part = list(freq_rows_of(0, 1))
    asked, freq_part[0] = lax.optimization_barrier((asked, freq_part[0]))
    asked_row = jnp.minimum(asked, owned - 1)
    weight = out_w.astype(f32).reshape(1, width)
    bias = cross_bias.reshape(1, width)
    label_rows = labels.astype(f32)
    bias_b = out_b.reshape(1)

    def axis_sum(blocks, step):
        at = me // step % 4
        total = lax.dynamic_index_in_dim(blocks, at, 0, keepdims=False).astype(f32)
        for k in range(1, 4):
            block = lax.dynamic_index_in_dim(blocks, (at + k) % 4, 0, keepdims=False)
            to = [(d, d + ((d // step % 4 + k) % 4 - d // step % 4) * step) for d in range(devices)]
            total = total + lax.ppermute(block, "dev", to).astype(f32)
        return total

    def exchange(rows, count):
        return lax.all_to_all(
            rows.reshape(devices, count, emb), "dev", split_axis=0, concat_axis=0, tiled=True
        ).reshape(n_req * count // cap, emb)

    outs = []

    def lookup(start, count):
        return local_call(
            functools.partial(lookup_kernel, devices, stride, start, count),
            [((devices * count, emb), bf16)],
            [SMEM, VMEM],
            [pltpu.VMEM((owned, emb), f32), pltpu.VMEM((devices * count, emb), f32)],
            f"lookup{start}",
            62,
            0,
            count * MIB * 5 // 8,
        )(asked_row, inf_table)[0]

    looked = lookup(0, cap)
    asked_row, looked = lax.optimization_barrier((asked_row, looked))
    looked_rest = lookup(cap, (micro - 1) * cap)
    fetched = exchange(looked, cap)
    ids, looked_rest = lax.optimization_barrier((ids, looked_rest))
    freq_part += freq_rows_of(1, 1)
    small = (place, weight, bias, label_rows, bias_b)
    looked_rest, fetched, freq_part[1], small = lax.optimization_barrier(
        (looked_rest, fetched, freq_part[1], small)
    )
    place, weight, bias, label_rows, bias_b = small
    fetched_rest = exchange(looked_rest, (micro - 1) * cap)
    ids, freq_part[1] = lax.optimization_barrier((ids, freq_part[1]))
    freq_part += freq_rows_of(2, 1)
    for m in range(micro):
        if m == 1:
            fetched_rest, outs[0][6], freq_part[2] = lax.optimization_barrier(
                (fetched_rest, outs[0][6], freq_part[2])
            )
        out = local_call(
            functools.partial(
                micro_kernel,
                devices,
                cap,
                features,
                m,
                m * n_req,
                max(m - 1, 0) * cap,
                m * cap,
                loss_mult,
            ),
            [
                ((devices, micro * cap, emb), bf16),
                ((n_slots, emb), f32),
                ((samples, width), bf16),
                ((samples, rank), bf16),
                ((samples, rank), bf16),
                ((samples, width), bf16),
                ((2, width), f32),
            ],
            [SMEM, SMEM, HBM if m else VMEM, HBM, VMEM, VMEM, HBM, HBM, VMEM, VMEM] + ([VMEM, HBM] if m else []),
            [pltpu.VMEM((n_req, emb), f32)]
            + [pltpu.VMEM((n_slots + 8, emb), f32)] * 8
            + [pltpu.VMEM((samples, width), f32)]
            + [pltpu.VMEM((devices, cap, emb), bf16), pltpu.VMEM((samples, width), bf16)]
            + [pltpu.VMEM((samples, rank), bf16)] * 2
            + [pltpu.VMEM((samples, width), bf16)]
            + [pltpu.VMEM((width, rank), bf16), pltpu.VMEM((rank, width), bf16)]
            + [pltpu.SemaphoreType.DMA((10,))],
            f"micro{m}",
            62,
            6 * samples * width * rank,
            60 * MIB,
            [HBM] * 6 + [VMEM],
            {11: 0} if m else {},
        )(
            place,
            bias_b,
            (fetched_rest if m else fetched).reshape(devices, -1, emb),
            freq_part[m],
            bottom,
            label_rows,
            cross_u,
            cross_v,
            bias,
            weight,
            *([outs[m - 1][6], outs[m - 1][0]] if m else []),
        )
        outs.append(list(out))
        if m == 1:
            place, outs[1][6] = lax.optimization_barrier((place, outs[1][6]))
    arrived = exchange(outs[2][0], micro * cap)
    d_pooled = [o[1] for o in outs]
    grad_bw = outs[2][6].reshape(2, devices, per)
    columns = jnp.pad(
        jnp.transpose(grad_bw, (1, 0, 2)), ((0, 0), (per - 16, 30 - per), (0, 128 - per))
    )

    rows_pad = -(-per // 16) * 16
    per_freq = freq_rows // devices
    (dense,) = local_call(
        functools.partial(dense_grad_kernel, devices, per),
        [((8, devices // 8, rows_pad, 2 * rank), bf16)],
        [VMEM] * 13,
        [
            pltpu.VMEM((width + 16, 2 * rank), f32),
            pltpu.VMEM((devices // 8, 8, rows_pad, 2 * rank), bf16),
            pltpu.SemaphoreType.DMA((devices // 8,)),
        ],
        "dense_grads",
        62,
        12 * samples * width * rank,
        40 * MIB,
        [HBM],
    )(
        columns,
        *[o[2] for o in outs],
        *[o[5] for o in outs],
        *[o[3] for o in outs],
        *[o[4] for o in outs],
    )
    core, dense = lax.optimization_barrier((core, dense))
    dense = dense.reshape(devices, rows_pad, 2 * rank)
    near = [list(range(d, d + 8)) for d in range(0, devices, 8)]
    dense = lax.psum_scatter(dense, "dev", axis_index_groups=near, tiled=True)
    keep_f, send_f = local_call(
        functools.partial(freq_grad_kernel, features),
        [((devices // 2, per_freq, emb), bf16)] * 2,
        [SMEM, SMEM] + [HBM] * 3,
        [pltpu.VMEM((freq_rows, emb), f32)] * 6
        + [pltpu.VMEM((n_slots, emb), f32)] * 3
        + [pltpu.SemaphoreType.DMA((3,))],
        "freq_grads",
        62,
        0,
        120 * MIB,
    )(core, ids, *d_pooled)
    got = lax.ppermute(send_f, "dev", other_core)
    both = (keep_f.astype(f32) + got.astype(f32)).astype(bf16)
    both, arrived = lax.optimization_barrier((both, arrived))
    parts = lax.all_to_all(
        both, "dev", split_axis=0, concat_axis=0, axis_index_groups=same_core, tiled=True
    )
    (grad_inf,) = local_call(
        functools.partial(owner_kernel, devices, stride, cap),
        [((owned, emb), bf16)],
        [SMEM, VMEM],
        [pltpu.VMEM((n_req, emb), f32)] + [pltpu.VMEM((owned + 8, emb), f32)] * 8,
        "owner_grads",
        62,
        0,
        60 * MIB,
    )(
        asked,
        arrived.reshape(devices, micro * cap, emb),
    )

    parts, grad_inf = lax.optimization_barrier((parts, grad_inf))
    (spread,) = local_call(
        spread_kernel,
        [((devices // 8, per_freq, emb), bf16)],
        [VMEM],
        [],
        "spread",
        62,
        0,
        4 * MIB,
    )(parts)
    sixteen = lax.all_to_all(
        spread,
        "dev",
        split_axis=0,
        concat_axis=0,
        axis_index_groups=[list(range(k, devices, 8)) for k in range(8)],
        tiled=True,
    ).reshape(freq_rows // 8, emb)
    sixteen, dense = lax.optimization_barrier((sixteen, dense))
    grad_freq = lax.all_gather(sixteen, "dev", axis_index_groups=near, tiled=True)
    dense = axis_sum(dense.reshape(4, 4, rows_pad, 2 * rank), 8).astype(bf16)
    dense = axis_sum(dense, 32)
    grad_u = dense[:per, :rank]
    grad_v = dense[:per, rank:].T
    grad_b = dense[per, :per]
    grad_w = dense[per + 1, :per]
    return (grad_u, grad_v, grad_b, grad_w, grad_freq, grad_inf)


def solution(mesh):
    in_specs = (
        P(None, "dev", None),
        P(None, "dev"),
        P(None, "dev", None, None),
        P(None, "dev", None, None),
        P(None, "dev", None, None),
        P(),
        P("dev", None),
        P(),
        P(),
        P(),
        P(),
        P(),
    )
    out_specs = (P("dev", None), P(None, "dev"), P("dev"), P("dev"), P(), P("dev", None))
    return jax.shard_map(
        on_device, mesh=mesh, in_specs=in_specs, out_specs=out_specs, check_vma=False
    )
```
